32 devices in a mesh: copies: 2 (over x), expert: 4 (over y, core), tm: 4 (over z).
Axes of the slice: x: 2, y: 2, z: 4, core: 2. Of those that a mesh axis runs over, the one named last changes fastest.
Arguments:
- tokens: bfloat16 [4, 1024, 2048], P('tm', ('copies', 'expert')), parts along dimension 1, may hold values from -6 to 6
- route_ids: int32 [4, 1024, 6], P('tm', ('copies', 'expert')), parts along dimension 1, may hold values from 0 to 15, all different within a row; in each aligned block of 128 rows (0 to 127, 128 to 255, ..., all dimensions but the last counted through in order) at most 72 rows name the same one
- route_probs: float32 [4, 1024, 6], P('tm', ('copies', 'expert')), parts along dimension 1, may hold values from 0.05 to 1
- step_size: float32 [8], P(('copies', 'tm')), parts along dimension 0, may hold values from 0.2 to 0.6
- start_state: float32 [1024, 2048], P(('copies', 'expert')), parts along dimension 0, may hold values from -6 to 6
- w_gate: bfloat16 [16, 2048, 768], P('expert'), may hold values from -0.125 to 0.125
- w_up: bfloat16 [16, 2048, 768], P('expert'), may hold values from -0.125 to 0.125
- w_down: bfloat16 [16, 768, 2048], P('expert'), may hold values from -0.21875 to 0.21875
Outputs:
- new_iterate: float32 [4, 1024, 2048], P('tm', ('copies', 'expert')), parts along dimension 1
The draws below stay inside these ranges and needn't reach their ends.
There are 2 independent parts, one for each index of `copies`. The reference program is written for one: setup_inputs(seed, part) draws one part's arguments, and reference() takes and returns one part's arrays. A program takes and returns all parts, laid end to end along the dimension named above; an argument that names none is the same for every part. Nothing has to cross between parts.
Inputs may be any that keep to these rules, and one draw needn't show every extreme that they name: `route_ids`: each row names 6 different experts. In each aligned block of 128 rows (the tokens of one device), no expert is named by more than 72 rows, a bound that some block reaches.
All inputs are finite; a program needn't handle non-finite values.
Results may differ from the reference program's by a relative error of at most 0.0018.
Values may be sent and summed in bfloat16 or wider, within the bound.
No kernel may reach another device: no remote copies, remote signals or barrier semaphores. Data moves between devices by JAX's collectives and lax.ppermute only.
A program may use at most 128 MiB of HBM per device.

```python
import math
import jax
import jax.numpy as jnp
import numpy as np
from jax import lax

D = 2048
FF = 768
TOPK = 6
TOK_DEV = 128
EXPERTS = 16
C = 72
TIMESTEPS = 4
GROUP_TOK = 512
N_EXPERT = 4


def levels(rng, extent, pieces, smallest, largest):
    def one(dim, parts):
        draws = jax.random.uniform(jax.random.fold_in(jax.random.fold_in(rng, 6), dim), (parts,), jnp.float32, smallest / len(pieces), largest / len(pieces))
        return jnp.repeat(jnp.exp(draws), extent[dim] // parts).reshape((-1,) + (1,) * (len(extent) - dim - 1))

    factor_of = one(*pieces[0])
    for cut in pieces[1:]:
        factor_of = factor_of * one(*cut)
    return factor_of


def assign_block(rng, own, number, rows, count, top, reach, skew):
    order = jax.random.permutation(rng, count)
    packed, ordinary = load_shares(count, rows * top, reach, skew, True), load_shares(count, rows * top, reach, skew, False)
    places = jnp.arange(count)

    def named(lengths, rotation):
        used = int((lengths > 0).sum())
        fixed = max(1, used // 4)
        shifted = fixed + (places - fixed + rotation * (used - fixed)) % max(1, count - fixed)
        return jnp.zeros((count,), jnp.int32).at[order[jnp.where(places < fixed, places, shifted)]].set(jnp.asarray(lengths, jnp.int32))

    lengths = jnp.where(number % 4 == 0, named(packed, number // 4), named(ordinary, number - number // 4 - 1))
    mixed = jax.random.permutation(jax.random.fold_in(own, 3), count)
    donor, receiver = mixed[0:count // 2 * 2:2], mixed[1:count // 2 * 2:2]
    margin = jnp.minimum(lengths[donor] - 1, reach - lengths[receiver]) // 2
    margin = jnp.where((donor == order[0]) | (receiver == order[0]) | (lengths[receiver] == 0), 0, jnp.maximum(margin, 0))
    shifted = jax.random.randint(jax.random.fold_in(own, 4), (count // 2,), 0, 1 << 20) % (margin + 1)
    lengths = lengths.at[donor].add(-shifted).at[receiver].add(shifted)
    labels = jnp.searchsorted(jnp.cumsum(lengths), jnp.arange(rows * top), side="right").astype(jnp.int32)
    listing = labels.reshape(top, rows).T
    listing = listing[jax.random.permutation(jax.random.fold_in(own, 1), rows)]
    rotation = jax.random.randint(jax.random.fold_in(own, 2), (rows, 1), 0, top)
    return jnp.take_along_axis(listing, (jnp.arange(top)[None, :] + rotation) % top, axis=1)


def load_shares(amount, total, reach, slope, full):
    portions = [(1 << 20) // math.isqrt(rank ** slope) + 1 for rank in range(1, amount + 1)]
    largest = reach if full else min(reach, max(-(-total // amount), total * portions[0] // sum(portions)))
    least = 1 if total - largest >= amount - 1 else 0
    counts, spare = [largest] + [least] * (amount - 1), total - largest - least * (amount - 1)
    while spare > 0:
        movable = [i for i in range(1, amount) if counts[i] < largest] or [i for i in range(1, amount) if counts[i] < reach]
        whole, budget = sum([portions[i] for i in movable]), spare
        for i in movable:
            addition = min(reach - counts[i], max(1, budget * portions[i] // whole), spare)
            counts[i] = counts[i] + addition
            spare = spare - addition
    return np.array(counts)


def bell_draw(own_key, extent, spread, bound, split=(), kind=jnp.bfloat16):
    drawn = spread * jax.random.normal(own_key, extent, jnp.float32)
    if split:
        drawn = drawn * levels(own_key, extent, split, -0.22, 0.18)
    return jnp.clip(drawn, -bound, bound).astype(kind)


def setup_inputs(seed: int = 0, part: int = 0) -> dict:
    keys = jax.random.split(jax.random.key(seed), 9)
    part_keys = jax.random.split(jax.random.fold_in(keys[8], part), 9)
    tokens = bell_draw(part_keys[0], (TIMESTEPS, GROUP_TOK, D), 1.0, 6.0, ((0, 4), (1, 4)))
    route_ids_keys = jax.random.split(jax.random.fold_in(part_keys[1], 1), TIMESTEPS * GROUP_TOK // TOK_DEV)
    route_ids_turns = jax.random.permutation(jax.random.fold_in(part_keys[1], 3), TIMESTEPS * GROUP_TOK // TOK_DEV)
    route_ids = jax.vmap(lambda own, number: assign_block(jax.random.fold_in(part_keys[1], 2), own, number, TOK_DEV, EXPERTS, TOPK, C, 2))(route_ids_keys, route_ids_turns).reshape((TIMESTEPS, GROUP_TOK, TOPK))
    route_probs = jnp.clip(0.05 + 0.95 * jax.random.uniform(part_keys[2], (TIMESTEPS, GROUP_TOK, TOPK), jnp.float32) ** levels(part_keys[2], (TIMESTEPS, GROUP_TOK, TOPK), ((0, 4), (1, 4)), -0.2, 0.2), 0.05, 1.0)
    step_size = jnp.clip(jnp.exp(math.log(0.6) - 1.0986123 * jax.random.uniform(part_keys[3], (TIMESTEPS,), jnp.float32) ** levels(part_keys[3], (TIMESTEPS,), ((0, 4),), -0.2, 0.2)), 0.2, 0.6)
    start_state = bell_draw(part_keys[4], (GROUP_TOK, D), 1.0, 6.0, ((0, 4),), jnp.float32)
    w_gate = bell_draw(keys[5], (EXPERTS, D, FF), D ** -0.5, 0.125, ((0, 4),))
    w_up = bell_draw(keys[6], (EXPERTS, D, FF), D ** -0.5, 0.125, ((0, 4),))
    w_down = bell_draw(keys[7], (EXPERTS, FF, D), FF ** -0.5, 0.21875, ((0, 4),))
    return {"tokens": tokens, "route_ids": route_ids, "route_probs": route_probs, "step_size": step_size, "start_state": start_state, "w_gate": w_gate, "w_up": w_up, "w_down": w_down}


def reference(tokens, route_ids, route_probs, step_size, start_state, w_gate, w_up, w_down):
    blocks = TIMESTEPS * N_EXPERT
    values = tokens.astype(jnp.float32)
    normed = (values * lax.rsqrt(lax.optimization_barrier(jnp.mean(values * values, axis=-1, keepdims=True)) + 1e-06)).astype(jnp.bfloat16)
    normed = normed.reshape(blocks, TOK_DEV, D)
    padded = jnp.concatenate([normed, jnp.zeros((blocks, 1, D), jnp.bfloat16)], axis=1)
    flat_ids = route_ids.reshape(blocks, TOK_DEV * TOPK).astype(jnp.int32)
    one_hot = (flat_ids[:, :, None] == jnp.arange(EXPERTS, dtype=jnp.int32)[None, None, :]).astype(jnp.int32)
    earlier = jnp.cumsum(one_hot, axis=1) - one_hot
    position = lax.optimization_barrier(jnp.sum(earlier * one_hot, axis=2)).astype(jnp.int32)
    slot_index = (flat_ids * C + position).astype(jnp.int32)
    gate_probs = route_probs.astype(jnp.float32)
    weights = (gate_probs / lax.optimization_barrier(jnp.sum(gate_probs, axis=-1, keepdims=True))).reshape(blocks, TOK_DEV * TOPK)
    block_ids = jnp.arange(blocks, dtype=jnp.int32)[:, None]
    token_of = jnp.broadcast_to((jnp.arange(TOK_DEV * TOPK, dtype=jnp.int32) // TOPK)[None, :], slot_index.shape)
    slot_table = jnp.full((blocks, EXPERTS * C), TOK_DEV, jnp.int32).at[block_ids, slot_index].set(token_of)
    weight_table = jnp.zeros((blocks, EXPERTS * C), jnp.float32).at[block_ids, slot_index].set(weights)

    def expert_step(drift_rows, operands):
        gate_one, up_one, down_one, expert = operands
        slot_tokens = lax.dynamic_slice_in_dim(slot_table, expert * C, C, 1)
        scales = lax.dynamic_slice_in_dim(weight_table, expert * C, C, 1)
        slot_rows = jnp.take_along_axis(padded, slot_tokens[:, :, None], axis=1).reshape(blocks * C, D)
        gate_act = jnp.dot(slot_rows, gate_one, preferred_element_type=jnp.float32)
        up_act = jnp.dot(slot_rows, up_one, preferred_element_type=jnp.float32)
        hidden = (jax.nn.silu(gate_act) * up_act).astype(jnp.bfloat16)
        result = jnp.dot(hidden, down_one, preferred_element_type=jnp.float32).astype(jnp.bfloat16)
        result = lax.optimization_barrier(result).astype(jnp.float32).reshape(blocks, C, D)
        drift_rows = drift_rows.at[block_ids, slot_tokens].add(scales[:, :, None] * result)
        return (drift_rows, None)
    initial = jnp.zeros((blocks, TOK_DEV + 1, D), jnp.float32)
    drift_rows, unused_out = lax.scan(expert_step, initial, (w_gate, w_up, w_down, jnp.arange(EXPERTS, dtype=jnp.int32)))
    drift_rows = drift_rows[:, :TOK_DEV, :].reshape(TIMESTEPS, GROUP_TOK, D)
    increment = step_size.astype(jnp.float32)[:, None, None] * drift_rows
    return start_state[None, :, :] + jnp.cumsum(increment, axis=0)
```

```python
import functools

import jax
import jax.numpy as jnp
from jax import lax
from jax.experimental import pallas as pl
from jax.experimental.pallas import tpu as pltpu
from jax.sharding import PartitionSpec as P

ANY = pl.BlockSpec(memory_space=pl.ANY)
VMEM = pl.BlockSpec(memory_space=pltpu.VMEM)


def split_of(size):
    for width in (256, 128):
        if size % width == 0:
            return width
    return size


def hidden_kernel(blocks, capacity, *refs):
    tables = refs[:blocks]
    tokens = refs[blocks : 2 * blocks]
    gate_hbm, up_hbm, out_ref = refs[2 * blocks : 2 * blocks + 3]
    toks, gates, ups, rows, spread, coef, tok_sem, gate_sem, up_sem = refs[2 * blocks + 3 :]
    local, features, units = gates.shape
    count = tokens[0].shape[0]
    pairs = blocks // 2
    experts = local * lax.axis_size("expert")
    first = lax.axis_index("expert") * local

    token_copies = [
        pltpu.make_async_copy(tokens[b], toks.at[pl.ds(b * count, count)], tok_sem.at[b]) for b in range(blocks)
    ]
    gate_copies = [pltpu.make_async_copy(gate_hbm.at[j], gates.at[j], gate_sem.at[j]) for j in range(local)]
    up_copies = [pltpu.make_async_copy(up_hbm.at[j], ups.at[j], up_sem.at[j]) for j in range(local)]
    for copy in token_copies:
        copy.start()
    for j in range(local):
        gate_copies[j].start()
        up_copies[j].start()

    before = lax.broadcasted_iota(jnp.int32, (count, count), 0)
    after = lax.broadcasted_iota(jnp.int32, (count, count), 1)
    upto = jnp.where(before <= after, 1.0, 0.0).astype(jnp.bfloat16)
    slot_ids = lax.broadcasted_iota(jnp.int32, (2 * capacity, 2 * count), 0).astype(jnp.float32)
    lane_ids = lax.broadcasted_iota(jnp.int32, (1, 2 * count), 1)
    offset = jnp.where(lane_ids >= count, float(capacity), 0.0)

    for p in range(pairs):
        for b in (2 * p, 2 * p + 1):
            token_copies[b].wait()
        table = [tables[2 * p], tables[2 * p + 1]]
        weight = jnp.concatenate([t[pl.ds(first, local), :] for t in table], axis=1)
        scale = jnp.concatenate([t[pl.ds(experts, 1), :] for t in table], axis=1)
        chosen = weight > 0.0
        ones = jnp.where(chosen, 1.0, 0.0)
        ranks = []
        for part in range(2):
            piece = ones[:, part * count : (part + 1) * count]
            piece = jnp.concatenate([piece, jnp.zeros((-local % 16, count), jnp.float32)], axis=0)
            ranks.append(jnp.dot(piece.astype(jnp.bfloat16), upto, preferred_element_type=jnp.float32)[:local])
        slot = jnp.where(chosen, jnp.concatenate(ranks, axis=1) - 1.0 + offset, -1.0)
        pair_tokens = toks[pl.ds(2 * p * count, 2 * count), :]
        for j in range(local):
            hit = slot_ids == slot[j : j + 1, :]
            hot = jnp.where(hit, 1.0, 0.0)
            coef[j, p, :, 0:1] = jnp.sum(jnp.where(hit, scale, 0.0), axis=1, keepdims=True)
            coef[j, p, :, 1:2] = jnp.sum(jnp.where(hit, weight[j : j + 1, :], 0.0), axis=1, keepdims=True)
            spread[j, p] = hot.T.astype(jnp.bfloat16)
            packed = jnp.dot(hot.astype(jnp.bfloat16), pair_tokens, preferred_element_type=jnp.float32)
            rows[j, pl.ds(p * 2 * capacity, 2 * capacity), :] = packed.astype(jnp.bfloat16)

    width = split_of(units)
    for j in range(local):
        gate_copies[j].wait()
        up_copies[j].wait()
        own = rows[j]
        for f in range(units // width):
            columns = pl.ds(f * width, width)
            gate = jnp.dot(own, gates[j, :, columns], preferred_element_type=jnp.float32)
            up = jnp.dot(own, ups[j, :, columns], preferred_element_type=jnp.float32)
            for p in range(pairs):
                part = slice(p * 2 * capacity, (p + 1) * 2 * capacity)
                scale = coef[j, p, :, 0:1]
                weight = coef[j, p, :, 1:2]
                g = gate[part] * scale
                h = (g / (1.0 + jnp.exp(-g))) * (up[part] * (scale * weight))
                placed = jnp.dot(spread[j, p], h.astype(jnp.bfloat16), preferred_element_type=jnp.float32)
                out_ref[pl.ds(p * 2 * count, 2 * count), pl.ds(j * units + f * width, width)] = placed.astype(
                    jnp.bfloat16
                )


def hidden_rows(tables, tokens, w_gate, w_up, capacity):
    blocks = len(tokens)
    count, features = tokens[0].shape
    local, _, units = w_gate.shape
    pairs = blocks // 2
    return pl.pallas_call(
        functools.partial(hidden_kernel, blocks, capacity),
        out_shape=jax.ShapeDtypeStruct((blocks * count, local * units), jnp.bfloat16),
        in_specs=[VMEM] * blocks + [ANY] * (blocks + 2),
        out_specs=VMEM,
        scratch_shapes=[
            pltpu.VMEM((blocks * count, features), jnp.bfloat16),
            pltpu.VMEM(w_gate.shape, jnp.bfloat16),
            pltpu.VMEM(w_up.shape, jnp.bfloat16),
            pltpu.VMEM((local, blocks * capacity, features), jnp.bfloat16),
            pltpu.VMEM((local, pairs, 2 * count, 2 * capacity), jnp.bfloat16),
            pltpu.VMEM((local, pairs, 2 * capacity, 128), jnp.float32),
            pltpu.SemaphoreType.DMA((blocks,)),
            pltpu.SemaphoreType.DMA((local,)),
            pltpu.SemaphoreType.DMA((local,)),
        ],
        compiler_params=pltpu.CompilerParams(vmem_limit_bytes=56 * 1024 * 1024),
        cost_estimate=pl.CostEstimate(
            flops=4 * local * blocks * capacity * features * units,
            bytes_accessed=4 * local * features * units,
            transcendentals=local * blocks * capacity * units,
        ),
        name="hidden_rows",
    )(*tables, *tokens, w_gate, w_up)


def down_kernel(start, hidden_ref, down_hbm, keep_ref, send_ref, weights, sems):
    local, units, width = weights.shape
    copies = [
        pltpu.make_async_copy(down_hbm.at[j, :, pl.ds(start, width)], weights.at[j], sems.at[j]) for j in range(local)
    ]
    for copy in copies:
        copy.start()
    total = None
    for j in range(local):
        copies[j].wait()
        term = jnp.dot(hidden_ref[:, pl.ds(j * units, units)], weights[j], preferred_element_type=jnp.float32)
        total = term if total is None else total + term
    half = keep_ref.shape[0]
    keep_ref[...] = total[:half]
    send_ref[...] = total[half:].astype(jnp.bfloat16)


def down_rows(hidden, w_down, start, width):
    total_rows = hidden.shape[0]
    local, units, _ = w_down.shape
    half = total_rows // 2
    return pl.pallas_call(
        functools.partial(down_kernel, start),
        out_shape=(
            jax.ShapeDtypeStruct((half, width), jnp.float32),
            jax.ShapeDtypeStruct((half, width), jnp.bfloat16),
        ),
        in_specs=[VMEM, ANY],
        out_specs=(VMEM, VMEM),
        scratch_shapes=[
            pltpu.VMEM((local, units, width), jnp.bfloat16),
            pltpu.SemaphoreType.DMA((local,)),
        ],
        compiler_params=pltpu.CompilerParams(vmem_limit_bytes=32 * 1024 * 1024),
        cost_estimate=pl.CostEstimate(
            flops=2 * total_rows * local * units * width,
            bytes_accessed=2 * local * units * width,
            transcendentals=0,
        ),
        name="down_rows",
    )(hidden, w_down)


def shards(tokens, route_ids, route_probs, step_size, start_state, w_gate, w_up, w_down):
    members = lax.axis_size("expert")
    steps = lax.axis_size("tm")
    tok_count, feature_count = tokens.shape[1:]
    topk_count = route_ids.shape[2]
    expert_total = w_gate.shape[0] * members
    capacity = 3 * tok_count * topk_count // (2 * expert_total)
    chips = members // 2

    def swapped(value):
        return lax.ppermute(value, "expert", [(i, i ^ 1) for i in range(members)])

    def shifted(value, by):
        return lax.ppermute(value, "expert", [(i, (i + 2 * by) % members) for i in range(members)])

    own = tokens[0]
    values = own.astype(jnp.float32)
    scale = lax.rsqrt(jnp.mean(values * values, axis=-1) + 1e-06)
    probs = route_probs[0]
    shares = step_size[0] * probs / jnp.sum(probs, axis=-1, keepdims=True)
    names = jnp.arange(expert_total, dtype=jnp.int32)[:, None, None]
    weights = jnp.sum(jnp.where(route_ids[0][None] == names, shares[None], 0.0), axis=2)
    table = jnp.concatenate(
        [weights, scale[None], jnp.zeros((-(expert_total + 1) % 8, tok_count), jnp.float32)], axis=0
    )

    def gathered(value):
        same = [value] + [shifted(value, by) for by in range(1, chips)]
        return same + [swapped(piece) for piece in same]

    token_blocks = gathered(own)
    table_blocks = gathered(table)
    hidden = hidden_rows(table_blocks, token_blocks, w_gate, w_up, capacity)

    parts = 4
    width = feature_count // parts
    out = []
    for c in range(parts):
        keep, send = down_rows(hidden, w_down, c * width, width)
        sums = keep + swapped(send).astype(jnp.float32)
        total = sums[:tok_count]
        for by in range(1, chips):
            piece = sums[by * tok_count : (by + 1) * tok_count].astype(jnp.bfloat16)
            total = total + shifted(piece, -by).astype(jnp.float32)
        for step in range(1, steps):
            passed = lax.ppermute(total.astype(jnp.bfloat16), "tm", [(step - 1, step)])
            total = total + passed.astype(jnp.float32)
        out.append(start_state[:, c * width : (c + 1) * width] + total)
    return jnp.concatenate(out, axis=1)[None]


def solution(mesh):
    return jax.shard_map(
        shards,
        mesh=mesh,
        in_specs=(
            P("tm", ("copies", "expert"), None),
            P("tm", ("copies", "expert"), None),
            P("tm", ("copies", "expert"), None),
            P(("copies", "tm")),
            P(("copies", "expert"), None),
            P("expert", None, None),
            P("expert", None, None),
            P("expert", None, None),
        ),
        out_specs=P("tm", ("copies", "expert"), None),
        check_vma=False,
    )
```

```python
import functools

import jax
import jax.numpy as jnp
from jax import lax
from jax.experimental import pallas as pl
from jax.experimental.pallas import tpu as pltpu
from jax.sharding import PartitionSpec as P

ANY = pl.BlockSpec(memory_space=pl.ANY)
HBM = pl.BlockSpec(memory_space=pltpu.HBM)
SMEM = pl.BlockSpec(memory_space=pltpu.SMEM)
VMEM = pl.BlockSpec(memory_space=pltpu.VMEM)
VMEM_GRANT = 12 * 1024 * 1024


def in_hbm(value):
    return pltpu.with_memory_space_constraint(value, pltpu.HBM)


def table_kernel(experts, step_ref, ids_ref, probs_ref, tokens_ref, out_ref):
    count, choices = ids_ref.shape
    lanes = -(-(experts + 1) // 128) * 128
    probs = probs_ref[...]
    shares = step_ref[0] * probs / jnp.sum(probs, axis=1, keepdims=True)
    names = lax.broadcasted_iota(jnp.int32, (count, lanes), 1)
    table = jnp.zeros((count, lanes), jnp.float32)
    for k in range(choices):
        table = table + jnp.where(ids_ref[:, k : k + 1] == names, shares[:, k : k + 1], 0.0)
    values = tokens_ref[...].astype(jnp.float32)
    scale = lax.rsqrt(jnp.mean(values * values, axis=1, keepdims=True) + 1e-06)
    table = jnp.where(names == experts, scale, table)
    out_ref[...] = table.T[: out_ref.shape[0]]


def make_table(step_size, ids, probs, tokens, experts):
    height = -(-(experts + 1) // 8) * 8
    return pl.pallas_call(
        functools.partial(table_kernel, experts),
        out_shape=jax.ShapeDtypeStruct((height, tokens.shape[0]), jnp.float32),
        in_specs=[SMEM, VMEM, VMEM, VMEM],
        out_specs=VMEM,
        compiler_params=pltpu.CompilerParams(vmem_limit_bytes=VMEM_GRANT),
        name="make_table",
    )(step_size, ids, probs, tokens)


def plan_pair(tables, capacity, local, hots, coefs):
    count = tables[0].shape[1]
    experts = local * lax.axis_size("expert")
    first = lax.axis_index("expert") * local
    before = lax.broadcasted_iota(jnp.int32, (count, count), 0)
    after = lax.broadcasted_iota(jnp.int32, (count, count), 1)
    upto = jnp.where(before <= after, 1.0, 0.0).astype(jnp.bfloat16)
    slot_ids = lax.broadcasted_iota(jnp.int32, (2 * capacity, 2 * count), 0).astype(jnp.float32)
    lane_ids = lax.broadcasted_iota(jnp.int32, (1, 2 * count), 1)
    offset = jnp.where(lane_ids >= count, float(capacity), 0.0)
    weight = jnp.concatenate([t[pl.ds(first, local), :] for t in tables], axis=1)
    scale = jnp.concatenate([t[pl.ds(experts, 1), :] for t in tables], axis=1)
    chosen = weight > 0.0
    ones = jnp.where(chosen, 1.0, 0.0)
    ranks = []
    for part in range(2):
        piece = ones[:, part * count : (part + 1) * count]
        piece = jnp.concatenate([piece, jnp.zeros((-local % 16, count), jnp.float32)], axis=0)
        ranks.append(jnp.dot(piece.astype(jnp.bfloat16), upto, preferred_element_type=jnp.float32)[:local])
    slot = jnp.where(chosen, jnp.concatenate(ranks, axis=1) - 1.0 + offset, -1.0)
    for j in range(local):
        hit = slot_ids == slot[j : j + 1, :]
        hots[j] = jnp.where(hit, 1.0, 0.0).astype(jnp.bfloat16)
        coefs[j, :, 0:1] = jnp.sum(jnp.where(hit, scale, 0.0), axis=1, keepdims=True)
        coefs[j, :, 1:2] = jnp.sum(jnp.where(hit, weight[j : j + 1, :], 0.0), axis=1, keepdims=True)


def pack_pair(hots, tokens, rows):
    both = jnp.concatenate([t[...] for t in tokens], axis=0)
    for j in range(hots.shape[0]):
        rows[j] = jnp.dot(hots[j], both, preferred_element_type=jnp.float32).astype(jnp.bfloat16)


def expert_hidden(j, rows, hots, coefs, gates, ups, out_ref, base):
    units = gates.shape[2]
    size = hots.shape[2]
    gate = jnp.dot(rows[j], gates[j], preferred_element_type=jnp.float32)
    up = jnp.dot(rows[j], ups[j], preferred_element_type=jnp.float32)
    scale = coefs[j, :, 0:1]
    weight = coefs[j, :, 1:2]
    g = gate * scale
    h = (g / (1.0 + jnp.exp(-g))) * (up * (scale * weight))
    placed = lax.dot_general(
        hots[j], h.astype(jnp.bfloat16), (((0,), (0,)), ((), ())), preferred_element_type=jnp.float32
    )
    out_ref[pl.ds(base, size), pl.ds(j * units, units)] = placed.astype(jnp.bfloat16)


def near_kernel(far_count, capacity, *refs):
    tables = refs[: 2 + far_count]
    tokens = refs[2 + far_count : 4 + far_count]
    gate_hbm, up_hbm, hidden, gates, ups, far_hots, far_coefs = refs[4 + far_count : 11 + far_count]
    hots, coefs, rows, gate_sem, up_sem = refs[11 + far_count :]
    local = gates.shape[0]
    copies = [
        (
            pltpu.make_async_copy(gate_hbm.at[j], gates.at[j], gate_sem.at[j]),
            pltpu.make_async_copy(up_hbm.at[j], ups.at[j], up_sem.at[j]),
        )
        for j in range(local)
    ]
    for pair in copies:
        for copy in pair:
            copy.start()
    plan_pair(tables[:2], capacity, local, hots, coefs)
    pack_pair(hots, tokens, rows)
    for p in range(far_count // 2):
        plan_pair(tables[2 + 2 * p : 4 + 2 * p], capacity, local, far_hots.at[p], far_coefs.at[p])
    for j in range(local):
        for copy in copies[j]:
            copy.wait()
        expert_hidden(j, rows, hots, coefs, gates, ups, hidden, 0)


def near_hidden(tables, tokens, w_gate, w_up, capacity):
    count, features = tokens[0].shape
    local, _, units = w_gate.shape
    far_count = len(tables) - 2
    pairs = far_count // 2
    plan = (local, 2 * capacity, 2 * count)
    scales = (local, 2 * capacity, 128)
    return pl.pallas_call(
        functools.partial(near_kernel, far_count, capacity),
        out_shape=(
            pltpu.VMEM(((pairs + 1) * 2 * count, local * units), jnp.bfloat16),
            pltpu.VMEM(w_gate.shape, w_gate.dtype),
            pltpu.VMEM(w_up.shape, w_up.dtype),
            jax.ShapeDtypeStruct((pairs,) + plan, jnp.bfloat16),
            jax.ShapeDtypeStruct((pairs,) + scales, jnp.float32),
        ),
        in_specs=[VMEM] * (4 + far_count) + [HBM] * 2,
        out_specs=(VMEM,) * 5,
        scratch_shapes=[
            pltpu.VMEM(plan, jnp.bfloat16),
            pltpu.VMEM(scales, jnp.float32),
            pltpu.VMEM((local, 2 * capacity, features), jnp.bfloat16),
            pltpu.SemaphoreType.DMA((local,)),
            pltpu.SemaphoreType.DMA((local,)),
        ],
        compiler_params=pltpu.CompilerParams(vmem_limit_bytes=VMEM_GRANT),
        cost_estimate=pl.CostEstimate(
            flops=8 * local * capacity * features * units,
            bytes_accessed=4 * local * features * units,
            transcendentals=2 * local * capacity * units,
        ),
        name="near_hidden",
    )(*tables, *tokens, in_hbm(w_gate), in_hbm(w_up))


def far_kernel(far_count, *refs):
    tokens = refs[:far_count]
    hots, coefs, gates, ups, down_hbm, _, hidden, downs, rows, sem = refs[far_count:]
    copy = pltpu.make_async_copy(down_hbm, downs, sem)
    copy.start()
    for p in range(far_count // 2):
        pack_pair(hots.at[p], tokens[2 * p : 2 * p + 2], rows)
        for j in range(gates.shape[0]):
            expert_hidden(j, rows, hots.at[p], coefs.at[p], gates, ups, hidden, (p + 1) * hots.shape[3])
    copy.wait()


def far_hidden(tokens, hots, coefs, gates, ups, w_down, hidden):
    pairs, local, slots, size = hots.shape
    features, units = gates.shape[1:]
    return pl.pallas_call(
        functools.partial(far_kernel, len(tokens)),
        out_shape=(
            pltpu.VMEM(hidden.shape, hidden.dtype),
            pltpu.VMEM(w_down.shape, w_down.dtype),
        ),
        in_specs=[VMEM] * (len(tokens) + 4) + [HBM, VMEM],
        out_specs=(VMEM,) * 2,
        scratch_shapes=[
            pltpu.VMEM((local, slots, features), jnp.bfloat16),
            pltpu.SemaphoreType.DMA,
        ],
        compiler_params=pltpu.CompilerParams(vmem_limit_bytes=VMEM_GRANT),
        cost_estimate=pl.CostEstimate(
            flops=4 * pairs * local * slots * features * units,
            bytes_accessed=2 * local * features * units,
            transcendentals=pairs * local * slots * units,
        ),
        input_output_aliases={len(tokens) + 5: 0},
        name="far_hidden",
    )(*tokens, hots, coefs, gates, ups, in_hbm(w_down), hidden)


def down_kernel(start, width, hidden_ref, down_ref, *refs):
    keep_ref, send_ref = refs[-2:]
    local, units, _ = down_ref.shape
    total = None
    for j in range(local):
        term = jnp.dot(
            hidden_ref[:, pl.ds(j * units, units)],
            down_ref[j, :, pl.ds(start, width)],
            preferred_element_type=jnp.float32,
        )
        total = term if total is None else total + term
    count = keep_ref.shape[1]
    for p in range(keep_ref.shape[0]):
        keep_ref[p] = total[2 * p * count : (2 * p + 1) * count]
        send_ref[p] = total[(2 * p + 1) * count : (2 * p + 2) * count].astype(jnp.bfloat16)


def down_rows(hidden, downs, orders, count, start, width):
    total_rows = hidden.shape[0]
    local, units, _ = downs.shape
    pairs = total_rows // (2 * count)
    return pl.pallas_call(
        functools.partial(down_kernel, start, width),
        out_shape=(
            jax.ShapeDtypeStruct((pairs, count, width), jnp.float32),
            jax.ShapeDtypeStruct((pairs, count, width), jnp.bfloat16),
        ),
        in_specs=[VMEM, VMEM] + [ANY] * len(orders),
        out_specs=(VMEM, VMEM),
        compiler_params=pltpu.CompilerParams(vmem_limit_bytes=VMEM_GRANT),
        cost_estimate=pl.CostEstimate(
            flops=2 * total_rows * local * units * width,
            bytes_accessed=2 * local * units * width,
            transcendentals=0,
        ),
        name="down_rows",
    )(hidden, downs, *orders)


def tie_kernel(value_ref, order_ref, out_ref):
    pass


def tie(value, order):
    return pl.pallas_call(
        tie_kernel,
        out_shape=jax.ShapeDtypeStruct(value.shape, value.dtype),
        in_specs=[ANY, ANY],
        out_specs=ANY,
        input_output_aliases={0: 0},
        compiler_params=pltpu.CompilerParams(vmem_limit_bytes=1024 * 1024),
        name="tie",
    )(value, order)


def shards(tokens, route_ids, route_probs, step_size, start_state, w_gate, w_up, w_down):
    members = lax.axis_size("expert")
    steps = lax.axis_size("tm")
    tok_count, feature_count = tokens.shape[1:]
    topk_count = route_ids.shape[2]
    expert_total = w_gate.shape[0] * members
    capacity = 3 * tok_count * topk_count // (2 * expert_total)
    chips = members // 2

    def swapped(value, by=0):
        return lax.ppermute(value, "expert", [(i, (i + 2 * by) % members ^ 1) for i in range(members)])

    def shifted(value, by):
        return lax.ppermute(value, "expert", [(i, (i + 2 * by) % members) for i in range(members)])

    own = tokens[0]
    far_same = [shifted(own, by) for by in range(1, chips)]
    token_near = [own, swapped(own)]
    table = make_table(step_size, route_ids[0], route_probs[0], own, expert_total)
    tables = [table, swapped(table)]
    for by in range(1, chips):
        tables += [shifted(table, by), swapped(table, by)]
    hidden, gates, ups, hots, coefs = near_hidden(tables, token_near, w_gate, w_up, capacity)
    token_far = []
    for piece in far_same:
        piece = tie(piece, hots)
        token_far += [piece, swapped(piece)]
    hidden, downs = far_hidden(token_far, hots, coefs, gates, ups, w_down, hidden)

    parts = 4
    width = feature_count // parts
    increments = []
    keeps, sums, backs = [], [], []
    for c in range(parts):
        orders = keeps[-1:] + (sums[c - 2 : c - 1] if c > 1 else []) + (backs[c - 3] if c > 2 else [])
        keep, send = down_rows(hidden, downs, orders, tok_count, c * width, width)
        total = keep + swapped(send).astype(jnp.float32)
        far = total[1:].astype(jnp.bfloat16)
        back = [shifted(far[by - 1], -by) for by in range(1, chips)]
        keeps.append(keep)
        sums.append(far)
        backs.append(back)
        total = total[0]
        for piece in back:
            total = total + piece.astype(jnp.float32)
        increments.append(total)

    place = lax.axis_index("tm")
    prefixes = []
    passed = None
    for wave in range(parts + steps - 1):
        total = jnp.zeros((tok_count, width), jnp.float32)
        for c in range(max(0, wave - steps + 1), min(wave, parts - 1) + 1):
            total = jnp.where(place == wave - c, increments[c], total)
        if passed is not None:
            total = total + passed.astype(jnp.float32)
        prefixes.append(total)
        if wave < parts + steps - 2:
            passed = lax.ppermute(total.astype(jnp.bfloat16), "tm", [(s, s + 1) for s in range(steps - 1)])
    out = []
    for c in range(parts):
        total = prefixes[c]
        for s in range(1, steps):
            total = jnp.where(place == s, prefixes[c + s], total)
        out.append(start_state[:, c * width : (c + 1) * width] + total)
    return jnp.concatenate(out, axis=1)[None]


def solution(mesh):
    return jax.shard_map(
        shards,
        mesh=mesh,
        in_specs=(
            P("tm", ("copies", "expert"), None),
            P("tm", ("copies", "expert"), None),
            P("tm", ("copies", "expert"), None),
            P(("copies", "tm")),
            P(("copies", "expert"), None),
            P("expert", None, None),
            P("expert", None, None),
            P("expert", None, None),
        ),
        out_specs=P("tm", ("copies", "expert"), None),
        check_vma=False,
    )
```

```python
import functools

import jax
import jax.numpy as jnp
from jax import lax
from jax.experimental import pallas as pl
from jax.experimental.pallas import tpu as pltpu
from jax.sharding import PartitionSpec as P

ANY = pl.BlockSpec(memory_space=pl.ANY)
HBM = pl.BlockSpec(memory_space=pltpu.HBM)
VMEM = pl.BlockSpec(memory_space=pltpu.VMEM)
GRANT = pltpu.CompilerParams(vmem_limit_bytes=7 * 1024 * 1024)
BRIEF = pl.CostEstimate(flops=0, bytes_accessed=0, transcendentals=0)
SMALL = pltpu.CompilerParams(vmem_limit_bytes=2 * 1024 * 1024)


def in_hbm(value):
    return pltpu.with_memory_space_constraint(value, pltpu.HBM)


def slots_of(capacity, blocks):
    return -(-capacity * blocks // 16) * 16


def fill_table(experts, step_ref, ids_ref, probs_ref, tokens_ref, out_ref):
    count, choices = ids_ref.shape
    lanes = -(-(experts + 1) // 128) * 128
    probs = probs_ref[...]
    shares = step_ref[0] * probs / jnp.sum(probs, axis=1, keepdims=True)
    names = lax.broadcasted_iota(jnp.int32, (count, lanes), 1)
    table = jnp.zeros((count, lanes), jnp.float32)
    for k in range(choices):
        table = table + jnp.where(ids_ref[:, k : k + 1] == names, shares[:, k : k + 1], 0.0)
    values = tokens_ref[...].astype(jnp.float32)
    scale = lax.rsqrt(jnp.mean(values * values, axis=1, keepdims=True) + 1e-06)
    table = jnp.where(names == experts, scale, table)
    out_ref[...] = table.T[: out_ref.shape[0]]


def plan(tables, capacity, hots, coefs):
    local, slots, width = hots.shape
    blocks = len(tables)
    count = width // blocks
    experts = local * lax.axis_size("expert")
    first = lax.axis_index("expert") * local
    before = lax.broadcasted_iota(jnp.int32, (count, count), 0)
    after = lax.broadcasted_iota(jnp.int32, (count, count), 1)
    upto = jnp.where(before <= after, 1.0, 0.0).astype(jnp.bfloat16)
    slot_ids = lax.broadcasted_iota(jnp.int32, (slots, width), 0).astype(jnp.float32)
    weights, scales, places = [], [], []
    for b in range(blocks):
        weight = tables[b][pl.ds(first, local), :]
        ones = jnp.where(weight > 0.0, 1.0, 0.0)
        padded = jnp.concatenate([ones, jnp.zeros((-local % 16, count), jnp.float32)], axis=0)
        rank = jnp.dot(padded.astype(jnp.bfloat16), upto, preferred_element_type=jnp.float32)[:local]
        places.append(jnp.where(weight > 0.0, rank + float(b * capacity - 1), -1.0))
        weights.append(weight)
        scales.append(tables[b][pl.ds(experts, 1), :])
    weight = jnp.concatenate(weights, axis=1) if blocks > 1 else weights[0]
    scale = jnp.concatenate(scales, axis=1) if blocks > 1 else scales[0]
    place = jnp.concatenate(places, axis=1) if blocks > 1 else places[0]
    for j in range(local):
        hit = slot_ids == place[j : j + 1, :]
        hots[j] = jnp.where(hit, 1.0, 0.0).astype(jnp.bfloat16)
        coefs[j, :, 0:1] = jnp.sum(jnp.where(hit, scale, 0.0), axis=1, keepdims=True)
        coefs[j, :, 1:2] = jnp.sum(jnp.where(hit, weight[j : j + 1, :], 0.0), axis=1, keepdims=True)


def pack(hots, tokens, rows):
    for j in range(hots.shape[0]):
        rows[j] = jnp.dot(hots[j], tokens, preferred_element_type=jnp.float32).astype(jnp.bfloat16)


def expert_hidden(j, rows, hots, coefs, gates, ups, out_ref, base):
    units = gates.shape[2]
    size = hots.shape[2]
    gate = jnp.dot(rows[j], gates[j], preferred_element_type=jnp.float32)
    up = jnp.dot(rows[j], ups[j], preferred_element_type=jnp.float32)
    scale = coefs[j, :, 0:1]
    weight = coefs[j, :, 1:2]
    g = gate * scale
    h = (g / (1.0 + jnp.exp(-g))) * (up * (scale * weight))
    placed = lax.dot_general(
        hots[j], h.astype(jnp.bfloat16), (((0,), (0,)), ((), ())), preferred_element_type=jnp.float32
    )
    out_ref[pl.ds(base, size), pl.ds(j * units, units)] = placed.astype(jnp.bfloat16)


def plan_scratch(local, slots, width, features):
    return [
        pltpu.VMEM((local, slots, width), jnp.bfloat16),
        pltpu.VMEM((local, slots, 128), jnp.float32),
        pltpu.VMEM((local, slots, features), jnp.bfloat16),
    ]


def own_kernel(capacity, *refs):
    step, ids_hbm, probs_hbm, tokens_hbm, gate_hbm, up_hbm = refs[:6]
    table, hidden, gates, ups = refs[6:10]
    ids, probs, tokens, hots, coefs, rows, sems, gate_sem, up_sem = refs[10:]
    local = gates.shape[0]
    smalls = [
        pltpu.make_async_copy(source, target, sems.at[i])
        for i, (source, target) in enumerate(
            ((ids_hbm.at[0], ids), (probs_hbm.at[0], probs), (tokens_hbm.at[0], tokens))
        )
    ]
    larges = []
    for j in range(local):
        larges.append(pltpu.make_async_copy(gate_hbm.at[j], gates.at[j], gate_sem.at[j]))
        larges.append(pltpu.make_async_copy(up_hbm.at[j], ups.at[j], up_sem.at[j]))
    for copy in smalls + larges:
        copy.start()
    for copy in smalls:
        copy.wait()
    fill_table(local * lax.axis_size("expert"), step, ids, probs, tokens, table)
    plan([table], capacity, hots, coefs)
    pack(hots, tokens[...], rows)
    for j in range(local):
        larges[2 * j].wait()
        larges[2 * j + 1].wait()
        expert_hidden(j, rows, hots, coefs, gates, ups, hidden, 0)


def own_hidden(step_size, ids, probs, tokens, w_gate, w_up, capacity, experts, blocks):
    count, features = tokens.shape[1:]
    local, _, units = w_gate.shape
    height = -(-(experts + 1) // 8) * 8
    inputs = (ids, probs, tokens, w_gate, w_up)
    return pl.pallas_call(
        functools.partial(own_kernel, capacity),
        out_shape=(
            jax.ShapeDtypeStruct((height, count), jnp.float32),
            pltpu.VMEM((blocks * count, local * units), jnp.bfloat16),
            pltpu.VMEM(w_gate.shape, w_gate.dtype),
            pltpu.VMEM(w_up.shape, w_up.dtype),
        ),
        in_specs=[pl.BlockSpec(memory_space=pltpu.SMEM)] + [HBM] * 5,
        out_specs=(VMEM,) * 4,
        scratch_shapes=[
            pltpu.VMEM(ids.shape[1:], jnp.int32),
            pltpu.VMEM(probs.shape[1:], jnp.float32),
            pltpu.VMEM((count, features), jnp.bfloat16),
        ]
        + plan_scratch(local, slots_of(capacity, 1), count, features)
        + [
            pltpu.SemaphoreType.DMA((3,)),
            pltpu.SemaphoreType.DMA((local,)),
            pltpu.SemaphoreType.DMA((local,)),
        ],
        compiler_params=GRANT,
        cost_estimate=pl.CostEstimate(
            flops=4 * local * capacity * features * units,
            bytes_accessed=4 * local * features * units,
            transcendentals=local * capacity * units,
        ),
        name="own_hidden",
    )(step_size, *[in_hbm(value) for value in inputs])


def partner_kernel(capacity, table, tokens, gates, ups, down_hbm, start_hbm, _, hidden, downs, start, *scratch):
    hots, coefs, rows, sems = scratch
    copies = [
        pltpu.make_async_copy(down_hbm, downs, sems.at[0]),
        pltpu.make_async_copy(start_hbm, start, sems.at[1]),
    ]
    for copy in copies:
        copy.start()
    plan([table], capacity, hots, coefs)
    pack(hots, tokens[...], rows)
    for j in range(gates.shape[0]):
        expert_hidden(j, rows, hots, coefs, gates, ups, hidden, hots.shape[2])
    for copy in copies:
        copy.wait()


def partner_hidden(table, tokens, gates, ups, w_down, start_state, hidden, capacity):
    count, features = tokens.shape
    local, _, units = gates.shape
    return pl.pallas_call(
        functools.partial(partner_kernel, capacity),
        out_shape=(
            pltpu.VMEM(hidden.shape, hidden.dtype),
            pltpu.VMEM(w_down.shape, w_down.dtype),
            pltpu.VMEM(start_state.shape, start_state.dtype),
        ),
        in_specs=[VMEM] * 4 + [HBM] * 2 + [VMEM],
        out_specs=(VMEM,) * 3,
        scratch_shapes=plan_scratch(local, slots_of(capacity, 1), count, features)
        + [pltpu.SemaphoreType.DMA((2,))],
        input_output_aliases={6: 0},
        compiler_params=GRANT,
        cost_estimate=pl.CostEstimate(
            flops=4 * local * capacity * features * units,
            bytes_accessed=2 * local * features * units,
            transcendentals=local * capacity * units,
        ),
        name="partner_hidden",
    )(table, tokens, gates, ups, in_hbm(w_down), in_hbm(start_state), hidden)


def far_plan_kernel(capacity, far_count, *refs):
    tables = refs[:far_count]
    hots, coefs = refs[-2:]
    for p in range(far_count // 2):
        plan(tables[2 * p : 2 * p + 2], capacity, hots.at[p], coefs.at[p])


def far_plan(tables, order, capacity, local):
    pairs = len(tables) // 2
    count = tables[0].shape[1]
    slots = slots_of(capacity, 2)
    return pl.pallas_call(
        functools.partial(far_plan_kernel, capacity, len(tables)),
        out_shape=(
            pltpu.VMEM((pairs, local, slots, 2 * count), jnp.bfloat16),
            pltpu.VMEM((pairs, local, slots, 128), jnp.float32),
        ),
        in_specs=[VMEM] * len(tables) + [ANY],
        out_specs=(VMEM,) * 2,
        compiler_params=SMALL,
        cost_estimate=BRIEF,
        name="far_plan",
    )(*tables, order)


def far_kernel(far_count, *refs):
    tokens = refs[:far_count]
    hots, coefs, gates, ups, _, hidden, rows = refs[far_count:]
    for p in range(far_count // 2):
        both = jnp.concatenate([tokens[2 * p][...], tokens[2 * p + 1][...]], axis=0)
        pack(hots.at[p], both, rows)
        for j in range(gates.shape[0]):
            expert_hidden(j, rows, hots.at[p], coefs.at[p], gates, ups, hidden, (p + 1) * hots.shape[3])


def far_hidden(tokens, hots, coefs, gates, ups, hidden):
    pairs, local, slots, size = hots.shape
    features, units = gates.shape[1:]
    return pl.pallas_call(
        functools.partial(far_kernel, len(tokens)),
        out_shape=pltpu.VMEM(hidden.shape, hidden.dtype),
        in_specs=[VMEM] * (len(tokens) + 5),
        out_specs=VMEM,
        scratch_shapes=[pltpu.VMEM((local, slots, features), jnp.bfloat16)],
        input_output_aliases={len(tokens) + 4: 0},
        compiler_params=GRANT,
        cost_estimate=pl.CostEstimate(
            flops=4 * pairs * local * slots * features * units,
            bytes_accessed=4 * local * features * units,
            transcendentals=pairs * local * slots * units,
        ),
        name="far_hidden",
    )(*tokens, hots, coefs, gates, ups, hidden)


def down_kernel(start, width, hidden_ref, down_ref, _, keep_ref, send_ref):
    local, units, _ = down_ref.shape
    total = None
    for j in range(local):
        term = jnp.dot(
            hidden_ref[:, pl.ds(j * units, units)],
            down_ref[j, :, pl.ds(start, width)],
            preferred_element_type=jnp.float32,
        )
        total = term if total is None else total + term
    count = keep_ref.shape[1]
    for p in range(keep_ref.shape[0]):
        keep_ref[p] = total[2 * p * count : (2 * p + 1) * count]
        send_ref[p] = total[(2 * p + 1) * count : (2 * p + 2) * count].astype(jnp.bfloat16)


def down_rows(hidden, downs, order, count, start, width):
    total_rows = hidden.shape[0]
    local, units, _ = downs.shape
    pairs = total_rows // (2 * count)
    return pl.pallas_call(
        functools.partial(down_kernel, start, width),
        out_shape=(
            pltpu.VMEM((pairs, count, width), jnp.float32),
            pltpu.VMEM((pairs, count, width), jnp.bfloat16),
        ),
        in_specs=[VMEM, VMEM, ANY],
        out_specs=(VMEM, VMEM),
        compiler_params=GRANT,
        cost_estimate=BRIEF,
        name="down_rows",
    )(hidden, downs, order)


def core_sum_kernel(keep, got, _, own, far):
    own[...] = keep[0] + got[0].astype(jnp.float32)
    for p in range(1, keep.shape[0]):
        far[p - 1] = (keep[p] + got[p].astype(jnp.float32)).astype(jnp.bfloat16)


def core_sum(keep, got, order):
    pairs, count, width = keep.shape
    return pl.pallas_call(
        core_sum_kernel,
        out_shape=(
            pltpu.VMEM((count, width), jnp.float32),
            pltpu.VMEM((pairs - 1, count, width), jnp.bfloat16),
        ),
        in_specs=[VMEM, VMEM, ANY],
        out_specs=(VMEM, VMEM),
        compiler_params=SMALL,
        cost_estimate=BRIEF,
        name="core_sum",
    )(keep, got, order)


def chip_sum_kernel(backs, own, *refs):
    total = own[...]
    for p in range(backs):
        total = total + refs[p][...].astype(jnp.float32)
    refs[-2][...] = total
    refs[-1][...] = total.astype(jnp.bfloat16)


def chip_sum(own, backs, order):
    return pl.pallas_call(
        functools.partial(chip_sum_kernel, len(backs)),
        out_shape=(pltpu.VMEM(own.shape, jnp.float32), pltpu.VMEM(own.shape, jnp.bfloat16)),
        in_specs=[VMEM] * (1 + len(backs)) + [ANY],
        out_specs=(VMEM, VMEM),
        compiler_params=SMALL,
        cost_estimate=BRIEF,
        name="chip_sum",
    )(own, *backs, order)


def chain_kernel(base, got, _, out):
    out[...] = (base[...] + got[...].astype(jnp.float32)).astype(jnp.bfloat16)


def chain_step(base, got, order):
    return pl.pallas_call(
        chain_kernel,
        out_shape=pltpu.VMEM(base.shape, jnp.bfloat16),
        in_specs=[VMEM, VMEM, ANY],
        out_specs=VMEM,
        compiler_params=SMALL,
        cost_estimate=BRIEF,
        name="chain_step",
    )(base, got, order)


def finish_kernel(first, gots, *refs):
    start, base = refs[:2]
    out, mark, block, sem = refs[-4:]
    mark[...] = jnp.zeros_like(mark)
    columns = pl.ds(first, base.shape[1])
    total = start[:, columns] + base[...]
    for got in refs[2 : 2 + gots]:
        total = total + got[...].astype(jnp.float32)
    block[...] = total
    copy = pltpu.make_async_copy(block, out.at[:, columns], sem)
    copy.start()
    copy.wait()


def finish(start, base, gots, order, out, first):
    inputs = [start, base, *gots, order] + ([] if out is None else [out])
    shape = (pltpu.HBM(start.shape, jnp.float32), pltpu.VMEM((8, 128), jnp.float32))
    return pl.pallas_call(
        functools.partial(finish_kernel, first, len(gots)),
        out_shape=shape,
        in_specs=[VMEM] * (2 + len(gots)) + [ANY] + ([] if out is None else [HBM]),
        out_specs=(HBM, VMEM),
        scratch_shapes=[pltpu.VMEM(base.shape, jnp.float32), pltpu.SemaphoreType.DMA],
        input_output_aliases={} if out is None else {len(inputs) - 1: 0},
        compiler_params=SMALL,
        cost_estimate=BRIEF,
        name="finish",
    )(*inputs)


def tie_kernel(value_ref, order_ref, out_ref):
    pass


def tie(value, order):
    return pl.pallas_call(
        tie_kernel,
        out_shape=jax.ShapeDtypeStruct(value.shape, value.dtype),
        in_specs=[ANY, ANY],
        out_specs=ANY,
        input_output_aliases={0: 0},
        compiler_params=SMALL,
        cost_estimate=BRIEF,
        name="tie",
    )(value, order)


def shards(tokens, route_ids, route_probs, step_size, start_state, w_gate, w_up, w_down):
    members = lax.axis_size("expert")
    steps = lax.axis_size("tm")
    tok_count, feature_count = tokens.shape[1:]
    topk_count = route_ids.shape[2]
    expert_total = w_gate.shape[0] * members
    capacity = 3 * tok_count * topk_count // (2 * expert_total)
    chips = members // 2

    def swapped(value, by=0):
        return lax.ppermute(value, "expert", [(i, (i + 2 * by) % members ^ 1) for i in range(members)])

    def shifted(value, by):
        return lax.ppermute(value, "expert", [(i, (i + 2 * by) % members) for i in range(members)])

    own = tokens[0]
    far_same = [shifted(own, by) for by in range(1, chips)]
    partner = swapped(own)
    table, hidden, gates, ups = own_hidden(
        step_size, route_ids, route_probs, tokens, w_gate, w_up, capacity, expert_total, members
    )
    partner_table = swapped(table)
    far_tables = []
    for by in range(1, chips):
        far_tables += [shifted(table, by), swapped(table, by)]
    hidden, downs, start = partner_hidden(
        partner_table, partner, gates, ups, w_down, start_state, hidden, capacity
    )
    far_tokens = []
    for piece in far_same:
        piece = tie(piece, downs)
        far_tokens += [piece, swapped(piece)]
    hots, coefs = far_plan(far_tables, downs, capacity, w_gate.shape[0])
    hidden = far_hidden(far_tokens, hots, coefs, gates, ups, hidden)

    sixteenths = (4, 4, 6, 2)
    parts = len(sixteenths)
    widths = [feature_count // 16 * share for share in sixteenths]
    firsts = [sum(widths[:c]) for c in range(parts)]
    events = []
    for c in range(parts):
        events.append((2.0 * c, "down", c, 0))
        events.append((2.0 * c + 3.9, "core", c, 0))
        for hop in range(steps):
            events.append((5.95 + 3.2 * c + 5.5 * hop, "chip" if hop == 0 else "chain", c, hop))
    order, out = hidden, None
    keeps, gots, owns, backs, bases, arrived = {}, {}, {}, {}, {}, {c: [] for c in range(parts)}
    for _, kind, c, hop in sorted(events):
        if kind == "down":
            keeps[c], send = down_rows(hidden, downs, order, tok_count, firsts[c], widths[c])
            gots[c] = swapped(send)
            order = keeps[c]
        elif kind == "core":
            owns[c], far = core_sum(keeps[c], gots[c], order)
            backs[c] = [shifted(far[by - 1], -by) for by in range(1, chips)]
            order = owns[c]
        else:
            if kind == "chip":
                bases[c], send = chip_sum(owns[c], backs[c], order)
                order = send
            elif hop < steps - 1:
                send = chain_step(bases[c], arrived[c][-1], order)
                order = send
            if hop < steps - 1:
                arrived[c].append(lax.ppermute(send, "tm", [(hop, hop + 1)]))
            else:
                out, order = finish(start, bases[c], arrived[c], order, out, firsts[c])
    return out[None]


def solution(mesh):
    return jax.shard_map(
        shards,
        mesh=mesh,
        in_specs=(
            P("tm", ("copies", "expert"), None),
            P("tm", ("copies", "expert"), None),
            P("tm", ("copies", "expert"), None),
            P(("copies", "tm")),
            P(("copies", "expert"), None),
            P("expert", None, None),
            P("expert", None, None),
            P("expert", None, None),
        ),
        out_specs=P("tm", ("copies", "expert"), None),
        check_vma=False,
    )
```

```python
import functools

import jax
import jax.numpy as jnp
from jax import lax
from jax.experimental import pallas as pl
from jax.experimental.pallas import tpu as pltpu
from jax.sharding import PartitionSpec as P

ANY = pl.BlockSpec(memory_space=pl.ANY)
HBM = pl.BlockSpec(memory_space=pltpu.HBM)
VMEM = pl.BlockSpec(memory_space=pltpu.VMEM)
GRANT = pltpu.CompilerParams(vmem_limit_bytes=7 * 1024 * 1024)
BRIEF = pl.CostEstimate(flops=0, bytes_accessed=0, transcendentals=0)
SMALL = pltpu.CompilerParams(vmem_limit_bytes=2 * 1024 * 1024)


def in_hbm(value):
    return pltpu.with_memory_space_constraint(value, pltpu.HBM)


def slots_of(capacity, blocks):
    return -(-capacity * blocks // 16) * 16


def table_kernel(experts, step, ids, probs, tokens_hbm, table, tokens, sem):
    copy = pltpu.make_async_copy(tokens_hbm.at[0], tokens, sem)
    copy.start()
    choices, _, count = ids.shape
    total = probs[0]
    for k in range(1, choices):
        total = total + probs[k]
    names = lax.broadcasted_iota(jnp.int32, table.shape, 0)
    value = jnp.zeros(table.shape, jnp.float32)
    for k in range(choices):
        value = value + jnp.where(ids[k] == names, step[0] * probs[k] / total, 0.0)
    copy.wait()
    rows = tokens[...].astype(jnp.float32)
    scale = lax.rsqrt(jnp.mean(rows * rows, axis=1, keepdims=True) + 1e-06)
    scale = jnp.broadcast_to(scale, (count, 128)).T[:1]
    table[...] = jnp.where(names == experts, scale, value)


def make_table(step_size, ids, probs, tokens, experts):
    count, features = tokens.shape[1:]
    height = -(-(experts + 1) // 8) * 8
    return pl.pallas_call(
        functools.partial(table_kernel, experts),
        out_shape=(
            pltpu.VMEM((height, count), jnp.float32),
            pltpu.VMEM((count, features), tokens.dtype),
        ),
        in_specs=[pl.BlockSpec(memory_space=pltpu.SMEM), VMEM, VMEM, HBM],
        out_specs=(VMEM, VMEM),
        scratch_shapes=[pltpu.SemaphoreType.DMA],
        compiler_params=SMALL,
        name="make_table",
    )(step_size, jnp.transpose(ids, (2, 0, 1)), jnp.transpose(probs, (2, 0, 1)), in_hbm(tokens))


def plan(tables, capacity, hots, coefs):
    local, slots, width = hots.shape
    blocks = len(tables)
    count = width // blocks
    experts = local * lax.axis_size("expert")
    first = lax.axis_index("expert") * local
    before = lax.broadcasted_iota(jnp.int32, (count, count), 0)
    after = lax.broadcasted_iota(jnp.int32, (count, count), 1)
    upto = jnp.where(before <= after, 1.0, 0.0).astype(jnp.bfloat16)
    slot_ids = lax.broadcasted_iota(jnp.int32, (slots, width), 0).astype(jnp.float32)
    weights, scales, places = [], [], []
    for b in range(blocks):
        weight = tables[b][pl.ds(first, local), :]
        ones = jnp.where(weight > 0.0, 1.0, 0.0)
        padded = jnp.concatenate([ones, jnp.zeros((-local % 16, count), jnp.float32)], axis=0)
        rank = jnp.dot(padded.astype(jnp.bfloat16), upto, preferred_element_type=jnp.float32)[:local]
        places.append(jnp.where(weight > 0.0, rank + float(b * capacity - 1), -1.0))
        weights.append(weight)
        scales.append(tables[b][pl.ds(experts, 1), :])
    weight = jnp.concatenate(weights, axis=1) if blocks > 1 else weights[0]
    scale = jnp.concatenate(scales, axis=1) if blocks > 1 else scales[0]
    place = jnp.concatenate(places, axis=1) if blocks > 1 else places[0]
    for j in range(local):
        hit = slot_ids == place[j : j + 1, :]
        hots[j] = jnp.where(hit, 1.0, 0.0).astype(jnp.bfloat16)
        coefs[j, :, 0:1] = jnp.sum(jnp.where(hit, scale, 0.0), axis=1, keepdims=True)
        coefs[j, :, 1:2] = jnp.sum(jnp.where(hit, weight[j : j + 1, :], 0.0), axis=1, keepdims=True)


def pack(hots, tokens, rows):
    for j in range(hots.shape[0]):
        rows[j] = jnp.dot(hots[j], tokens, preferred_element_type=jnp.float32).astype(jnp.bfloat16)


def expert_hidden(j, rows, hots, coefs, gates, ups, out_ref, base):
    units = gates.shape[2]
    size = hots.shape[2]
    gate = jnp.dot(rows[j], gates[j], preferred_element_type=jnp.float32)
    up = jnp.dot(rows[j], ups[j], preferred_element_type=jnp.float32)
    scale = coefs[j, :, 0:1]
    weight = coefs[j, :, 1:2]
    g = gate * scale
    h = (g / (1.0 + jnp.exp(-g))) * (up * (scale * weight))
    placed = lax.dot_general(
        hots[j], h.astype(jnp.bfloat16), (((0,), (0,)), ((), ())), preferred_element_type=jnp.float32
    )
    out_ref[pl.ds(base, size), pl.ds(j * units, units)] = placed.astype(jnp.bfloat16)


def near_kernel(capacity, *refs):
    tables, tokens = refs[:2], refs[2:4]
    gate_hbm, up_hbm, down_hbm, start_hbm, hidden, gates, ups, downs, start = refs[4:13]
    hots, coefs, rows, gate_sem, up_sem, rest_sem = refs[13:]
    local = gates.shape[0]
    copies = []
    for j in range(local):
        copies.append(pltpu.make_async_copy(gate_hbm.at[j], gates.at[j], gate_sem.at[j]))
        copies.append(pltpu.make_async_copy(up_hbm.at[j], ups.at[j], up_sem.at[j]))
    copies.append(pltpu.make_async_copy(down_hbm, downs, rest_sem.at[0]))
    copies.append(pltpu.make_async_copy(start_hbm, start, rest_sem.at[1]))
    for copy in copies:
        copy.start()
    plan(tables, capacity, hots, coefs)
    pack(hots, jnp.concatenate([t[...] for t in tokens], axis=0), rows)
    for j in range(local):
        copies[2 * j].wait()
        copies[2 * j + 1].wait()
        expert_hidden(j, rows, hots, coefs, gates, ups, hidden, 0)
    for copy in copies[2 * local :]:
        copy.wait()


def near_hidden(tables, tokens, w_gate, w_up, w_down, start_state, capacity, blocks):
    count, features = tokens[0].shape
    local, _, units = w_gate.shape
    slots = slots_of(capacity, 2)
    return pl.pallas_call(
        functools.partial(near_kernel, capacity),
        out_shape=(
            pltpu.VMEM((blocks * count, local * units), jnp.bfloat16),
            pltpu.VMEM(w_gate.shape, w_gate.dtype),
            pltpu.VMEM(w_up.shape, w_up.dtype),
            pltpu.VMEM(w_down.shape, w_down.dtype),
            pltpu.VMEM(start_state.shape, start_state.dtype),
        ),
        in_specs=[VMEM] * 4 + [HBM] * 4,
        out_specs=(VMEM,) * 5,
        scratch_shapes=[
            pltpu.VMEM((local, slots, 2 * count), jnp.bfloat16),
            pltpu.VMEM((local, slots, 128), jnp.float32),
            pltpu.VMEM((local, slots, features), jnp.bfloat16),
            pltpu.SemaphoreType.DMA((local,)),
            pltpu.SemaphoreType.DMA((local,)),
            pltpu.SemaphoreType.DMA((2,)),
        ],
        compiler_params=GRANT,
        cost_estimate=pl.CostEstimate(
            flops=4 * local * slots * features * units,
            bytes_accessed=6 * local * features * units,
            transcendentals=local * slots * units,
        ),
        name="near_hidden",
    )(*tables, *tokens, *[in_hbm(value) for value in (w_gate, w_up, w_down, start_state)])


def far_plan_kernel(capacity, far_count, *refs):
    tables = refs[:far_count]
    hots, coefs = refs[-2:]
    for p in range(far_count // 2):
        plan(tables[2 * p : 2 * p + 2], capacity, hots.at[p], coefs.at[p])


def far_plan(tables, order, capacity, local):
    pairs = len(tables) // 2
    count = tables[0].shape[1]
    slots = slots_of(capacity, 2)
    return pl.pallas_call(
        functools.partial(far_plan_kernel, capacity, len(tables)),
        out_shape=(
            pltpu.VMEM((pairs, local, slots, 2 * count), jnp.bfloat16),
            pltpu.VMEM((pairs, local, slots, 128), jnp.float32),
        ),
        in_specs=[VMEM] * len(tables) + [ANY],
        out_specs=(VMEM,) * 2,
        compiler_params=SMALL,
        cost_estimate=BRIEF,
        name="far_plan",
    )(*tables, order)


def far_kernel(far_count, *refs):
    tokens = refs[:far_count]
    hots, coefs, gates, ups, _, hidden, rows = refs[far_count:]
    for p in range(far_count // 2):
        both = jnp.concatenate([tokens[2 * p][...], tokens[2 * p + 1][...]], axis=0)
        pack(hots.at[p], both, rows)
        for j in range(gates.shape[0]):
            expert_hidden(j, rows, hots.at[p], coefs.at[p], gates, ups, hidden, (p + 1) * hots.shape[3])


def far_hidden(tokens, hots, coefs, gates, ups, hidden):
    pairs, local, slots, size = hots.shape
    features, units = gates.shape[1:]
    return pl.pallas_call(
        functools.partial(far_kernel, len(tokens)),
        out_shape=pltpu.VMEM(hidden.shape, hidden.dtype),
        in_specs=[VMEM] * (len(tokens) + 5),
        out_specs=VMEM,
        scratch_shapes=[pltpu.VMEM((local, slots, features), jnp.bfloat16)],
        input_output_aliases={len(tokens) + 4: 0},
        compiler_params=GRANT,
        cost_estimate=pl.CostEstimate(
            flops=4 * pairs * local * slots * features * units,
            bytes_accessed=4 * local * features * units,
            transcendentals=pairs * local * slots * units,
        ),
        name="far_hidden",
    )(*tokens, hots, coefs, gates, ups, hidden)


def down_kernel(start, width, hidden_ref, down_ref, _, keep_ref, send_ref):
    local, units, _ = down_ref.shape
    total = None
    for j in range(local):
        term = jnp.dot(
            hidden_ref[:, pl.ds(j * units, units)],
            down_ref[j, :, pl.ds(start, width)],
            preferred_element_type=jnp.float32,
        )
        total = term if total is None else total + term
    count = keep_ref.shape[1]
    for p in range(keep_ref.shape[0]):
        keep_ref[p] = total[2 * p * count : (2 * p + 1) * count]
        send_ref[p] = total[(2 * p + 1) * count : (2 * p + 2) * count].astype(jnp.bfloat16)


def down_rows(hidden, downs, order, count, start, width):
    total_rows = hidden.shape[0]
    local, units, _ = downs.shape
    pairs = total_rows // (2 * count)
    return pl.pallas_call(
        functools.partial(down_kernel, start, width),
        out_shape=(
            pltpu.VMEM((pairs, count, width), jnp.float32),
            pltpu.VMEM((pairs, count, width), jnp.bfloat16),
        ),
        in_specs=[VMEM, VMEM, ANY],
        out_specs=(VMEM, VMEM),
        compiler_params=GRANT,
        cost_estimate=BRIEF,
        name="down_rows",
    )(hidden, downs, order)


def core_sum_kernel(keep, got, _, own, far):
    own[...] = keep[0] + got[0].astype(jnp.float32)
    for p in range(1, keep.shape[0]):
        far[p - 1] = (keep[p] + got[p].astype(jnp.float32)).astype(jnp.bfloat16)


def core_sum(keep, got, order):
    pairs, count, width = keep.shape
    return pl.pallas_call(
        core_sum_kernel,
        out_shape=(
            pltpu.VMEM((count, width), jnp.float32),
            pltpu.VMEM((pairs - 1, count, width), jnp.bfloat16),
        ),
        in_specs=[VMEM, VMEM, ANY],
        out_specs=(VMEM, VMEM),
        compiler_params=SMALL,
        cost_estimate=BRIEF,
        name="core_sum",
    )(keep, got, order)


def wave_kernel(wave, window, backs, got_count, *refs):
    place = lax.axis_index("tm")
    send, prefix = refs[-2:]
    for n, i in enumerate(window):
        own = refs[n * (1 + backs)]
        more = refs[n * (1 + backs) + 1 : (n + 1) * (1 + backs)]

        @pl.when(place == wave - i)
        def _(own=own, more=more, first=wave == i):
            total = own[...]
            for ref in more:
                total = total + ref[...].astype(jnp.float32)
            if not first:
                total = total + refs[len(window) * (1 + backs)][...].astype(jnp.float32)
            prefix[...] = total
            send[...] = total.astype(jnp.bfloat16)


def wave_step(wave, window, owns, backs, got, order):
    inputs = []
    for i in window:
        inputs += [owns[i], *backs[i]]
    inputs += [] if got is None else [got]
    shape = owns[window[0]].shape
    return pl.pallas_call(
        functools.partial(wave_kernel, wave, window, len(backs[window[0]]), 0 if got is None else 1),
        out_shape=(pltpu.VMEM(shape, jnp.bfloat16), pltpu.VMEM(shape, jnp.float32)),
        in_specs=[VMEM] * len(inputs) + [ANY],
        out_specs=(VMEM, VMEM),
        compiler_params=SMALL,
        cost_estimate=BRIEF,
        name="wave_step",
    )(*inputs, order)


def finish_kernel(wave, chunks, stride, lane, start, prefix, *refs):
    out, mark, block, sem = refs[-4:]
    mark[...] = jnp.zeros_like(mark)
    place = lax.axis_index("tm")
    width = prefix.shape[1]
    for i in range(chunks):

        @pl.when(place == wave - i)
        def _(i=i):
            columns = pl.ds((i * stride + lane) * width, width)
            block[...] = start[:, columns] + prefix[...]
            copy = pltpu.make_async_copy(block, out.at[:, columns], sem)
            copy.start()
            copy.wait()


def finish(wave, chunks, stride, lane, start, prefix, out):
    inputs = [start, prefix] + ([] if out is None else [out])
    return pl.pallas_call(
        functools.partial(finish_kernel, wave, chunks, stride, lane),
        out_shape=(pltpu.HBM(start.shape, jnp.float32), pltpu.VMEM((8, 128), jnp.float32)),
        in_specs=[VMEM] * 2 + ([] if out is None else [HBM]),
        out_specs=(HBM, VMEM),
        scratch_shapes=[pltpu.VMEM(prefix.shape, jnp.float32), pltpu.SemaphoreType.DMA],
        input_output_aliases={} if out is None else {2: 0},
        compiler_params=SMALL,
        cost_estimate=BRIEF,
        name="finish",
    )(*inputs)


def tie_kernel(value_ref, order_ref, out_ref):
    pass


def tie(value, order):
    return pl.pallas_call(
        tie_kernel,
        out_shape=jax.ShapeDtypeStruct(value.shape, value.dtype),
        in_specs=[ANY, ANY],
        out_specs=ANY,
        input_output_aliases={0: 0},
        compiler_params=SMALL,
        cost_estimate=BRIEF,
        name="tie",
    )(value, order)


def shards(tokens, route_ids, route_probs, step_size, start_state, w_gate, w_up, w_down):
    members = lax.axis_size("expert")
    steps = lax.axis_size("tm")
    tok_count, feature_count = tokens.shape[1:]
    topk_count = route_ids.shape[2]
    expert_total = w_gate.shape[0] * members
    capacity = 3 * tok_count * topk_count // (2 * expert_total)
    chips = members // 2

    def swapped(value, by=0):
        return lax.ppermute(value, "expert", [(i, (i + 2 * by) % members ^ 1) for i in range(members)])

    def shifted(value, by):
        return lax.ppermute(value, "expert", [(i, (i + 2 * by) % members) for i in range(members)])

    own = tokens[0]
    far_same = [shifted(own, by) for by in range(1, chips)]
    partner = swapped(own)
    table, own = make_table(step_size, route_ids, route_probs, tokens, expert_total)
    tables = [table, swapped(table)]
    far_tables = []
    for by in range(1, chips):
        far_tables += [shifted(table, by), swapped(table, by)]
    hidden, gates, ups, downs, start = near_hidden(
        tables, [own, partner], w_gate, w_up, w_down, start_state, capacity, members
    )
    hots, coefs = far_plan(far_tables, hidden, capacity, w_gate.shape[0])
    far_tokens = []
    for piece in far_same:
        piece = tie(piece, coefs)
        far_tokens += [piece, swapped(piece)]
    hidden = far_hidden(far_tokens, hots, coefs, gates, ups, hidden)

    lanes, chunks = 2, 2
    parts = lanes * chunks
    width = feature_count // parts
    events = []
    for c in range(parts):
        events.append((1.8 * c + (0.9 if c > 1 else 0.0), "down", c, 0))
        events.append((3.9 + 2.45 * c, "core", c, 0))
    for lane in range(lanes):
        ready = 9.9 + 3.0 * lane
        for wave in range(chunks + steps - 1):
            events.append((ready, "wave", lane, wave))
            ready += 6.7
    order, out = hidden, None
    keeps, gots, owns, backs = {}, {}, {}, {}
    arrived = {}
    for _, kind, c, wave in sorted(events):
        if kind == "down":
            keeps[c], send = down_rows(hidden, downs, order, tok_count, c * width, width)
            gots[c] = swapped(send)
            order = keeps[c]
        elif kind == "core":
            owns[c], far = core_sum(keeps[c], gots[c], order)
            backs[c] = [shifted(far[by - 1], -by) for by in range(1, chips)]
            order = owns[c]
        else:
            window = [i for i in range(chunks) if 0 <= wave - i < steps]
            lane_owns = {i: owns[i * lanes + c] for i in window}
            lane_backs = {i: backs[i * lanes + c] for i in window}
            send, prefix = wave_step(wave, window, lane_owns, lane_backs, arrived.get(c), order)
            if wave < chunks + steps - 2:
                arrived[c] = lax.ppermute(send, "tm", [(z, z + 1) for z in range(steps - 1)])
            out, order = finish(wave, chunks, lanes, c, start, prefix, out)
    return out[None]


def solution(mesh):
    return jax.shard_map(
        shards,
        mesh=mesh,
        in_specs=(
            P("tm", ("copies", "expert"), None),
            P("tm", ("copies", "expert"), None),
            P("tm", ("copies", "expert"), None),
            P(("copies", "tm")),
            P(("copies", "expert"), None),
            P("expert", None, None),
            P("expert", None, None),
            P("expert", None, None),
        ),
        out_specs=P("tm", ("copies", "expert"), None),
        check_vma=False,
    )
```

```python
import functools

import jax
import jax.numpy as jnp
from jax import lax
from jax.experimental import pallas as pl
from jax.experimental.pallas import tpu as pltpu
from jax.sharding import PartitionSpec as P

ANY = pl.BlockSpec(memory_space=pl.ANY)
HBM = pl.BlockSpec(memory_space=pltpu.HBM)
VMEM = pl.BlockSpec(memory_space=pltpu.VMEM)
GRANT = pltpu.CompilerParams(vmem_limit_bytes=7 * 1024 * 1024)
BRIEF = pl.CostEstimate(flops=0, bytes_accessed=0, transcendentals=0)
SMALL = pltpu.CompilerParams(vmem_limit_bytes=2 * 1024 * 1024)


def in_hbm(value):
    return pltpu.with_memory_space_constraint(value, pltpu.HBM)


def slots_of(capacity, blocks):
    return -(-capacity * blocks // 16) * 16


def table_kernel(experts, step, ids_hbm, probs_hbm, tokens_hbm, table, tokens, ids, probs, sems):
    copy = pltpu.make_async_copy(tokens_hbm.at[0], tokens, sems.at[0])
    smalls = [
        pltpu.make_async_copy(ids_hbm, ids, sems.at[1]),
        pltpu.make_async_copy(probs_hbm, probs, sems.at[2]),
    ]
    copy.start()
    for small in smalls:
        small.start()
    for small in smalls:
        small.wait()
    choices, _, count = ids.shape
    total = probs[0]
    for k in range(1, choices):
        total = total + probs[k]
    names = lax.broadcasted_iota(jnp.int32, table.shape, 0)
    value = jnp.zeros(table.shape, jnp.float32)
    for k in range(choices):
        value = value + jnp.where(ids[k] == names, step[0] * probs[k] / total, 0.0)
    copy.wait()
    rows = tokens[...].astype(jnp.float32)
    scale = lax.rsqrt(jnp.mean(rows * rows, axis=1, keepdims=True) + 1e-06)
    scale = jnp.broadcast_to(scale, (count, 128)).T[:1]
    table[...] = jnp.where(names == experts, scale, value)


def make_table(step_size, ids, probs, tokens, experts):
    count, features = tokens.shape[1:]
    height = -(-(experts + 1) // 8) * 8
    ids, probs = jnp.transpose(ids, (2, 0, 1)), jnp.transpose(probs, (2, 0, 1))
    return pl.pallas_call(
        functools.partial(table_kernel, experts),
        out_shape=(
            pltpu.VMEM((height, count), jnp.float32),
            pltpu.VMEM((count, features), tokens.dtype),
        ),
        in_specs=[pl.BlockSpec(memory_space=pltpu.SMEM), HBM, HBM, HBM],
        out_specs=(VMEM, VMEM),
        scratch_shapes=[
            pltpu.VMEM(ids.shape, ids.dtype),
            pltpu.VMEM(probs.shape, probs.dtype),
            pltpu.SemaphoreType.DMA((3,)),
        ],
        compiler_params=SMALL,
        name="make_table",
    )(step_size, in_hbm(ids), in_hbm(probs), in_hbm(tokens))


def plan(tables, capacity, hots, coefs):
    local, slots, width = hots.shape
    blocks = len(tables)
    count = width // blocks
    experts = local * lax.axis_size("expert")
    first = lax.axis_index("expert") * local
    before = lax.broadcasted_iota(jnp.int32, (count, count), 0)
    after = lax.broadcasted_iota(jnp.int32, (count, count), 1)
    upto = jnp.where(before <= after, 1.0, 0.0).astype(jnp.bfloat16)
    slot_ids = lax.broadcasted_iota(jnp.int32, (slots, width), 0).astype(jnp.float32)
    weights, scales, places = [], [], []
    for b in range(blocks):
        weight = tables[b][pl.ds(first, local), :]
        ones = jnp.where(weight > 0.0, 1.0, 0.0)
        padded = jnp.concatenate([ones, jnp.zeros((-local % 16, count), jnp.float32)], axis=0)
        rank = jnp.dot(padded.astype(jnp.bfloat16), upto, preferred_element_type=jnp.float32)[:local]
        places.append(jnp.where(weight > 0.0, rank + float(b * capacity - 1), -1.0))
        weights.append(weight)
        scales.append(tables[b][pl.ds(experts, 1), :])
    weight = jnp.concatenate(weights, axis=1) if blocks > 1 else weights[0]
    scale = jnp.concatenate(scales, axis=1) if blocks > 1 else scales[0]
    place = jnp.concatenate(places, axis=1) if blocks > 1 else places[0]
    for j in range(local):
        hit = slot_ids == place[j : j + 1, :]
        hots[j] = jnp.where(hit, 1.0, 0.0).astype(jnp.bfloat16)
        coefs[j, :, 0:1] = jnp.sum(jnp.where(hit, scale, 0.0), axis=1, keepdims=True)
        coefs[j, :, 1:2] = jnp.sum(jnp.where(hit, weight[j : j + 1, :], 0.0), axis=1, keepdims=True)


def pack(hots, tokens, rows):
    for j in range(hots.shape[0]):
        rows[j] = jnp.dot(hots[j], tokens, preferred_element_type=jnp.float32).astype(jnp.bfloat16)


def expert_hidden(j, rows, hots, coefs, gates, ups, out_ref, base):
    units = gates.shape[2]
    size = hots.shape[2]
    gate = jnp.dot(rows[j], gates[j], preferred_element_type=jnp.float32)
    up = jnp.dot(rows[j], ups[j], preferred_element_type=jnp.float32)
    scale = coefs[j, :, 0:1]
    weight = coefs[j, :, 1:2]
    g = gate * scale
    h = (g / (1.0 + jnp.exp(-g))) * (up * (scale * weight))
    placed = lax.dot_general(
        hots[j], h.astype(jnp.bfloat16), (((0,), (0,)), ((), ())), preferred_element_type=jnp.float32
    )
    out_ref[pl.ds(base, size), pl.ds(j * units, units)] = placed.astype(jnp.bfloat16)


def near_kernel(capacity, *refs):
    tables, tokens = refs[:2], refs[2:4]
    gate_hbm, up_hbm, hidden, gates, ups = refs[4:9]
    hots, coefs, rows, gate_sem, up_sem = refs[9:]
    local = gates.shape[0]
    copies = []
    for j in range(local):
        copies.append(pltpu.make_async_copy(gate_hbm.at[j], gates.at[j], gate_sem.at[j]))
        copies.append(pltpu.make_async_copy(up_hbm.at[j], ups.at[j], up_sem.at[j]))
    for copy in copies:
        copy.start()
    plan(tables, capacity, hots, coefs)
    pack(hots, jnp.concatenate([t[...] for t in tokens], axis=0), rows)
    for j in range(local):
        copies[2 * j].wait()
        copies[2 * j + 1].wait()
        expert_hidden(j, rows, hots, coefs, gates, ups, hidden, 0)


def near_hidden(tables, tokens, w_gate, w_up, capacity, blocks):
    count, features = tokens[0].shape
    local, _, units = w_gate.shape
    slots = slots_of(capacity, 2)
    return pl.pallas_call(
        functools.partial(near_kernel, capacity),
        out_shape=(
            pltpu.VMEM((blocks * count, local * units), jnp.bfloat16),
            pltpu.VMEM(w_gate.shape, w_gate.dtype),
            pltpu.VMEM(w_up.shape, w_up.dtype),
        ),
        in_specs=[VMEM] * 4 + [HBM] * 2,
        out_specs=(VMEM,) * 3,
        scratch_shapes=[
            pltpu.VMEM((local, slots, 2 * count), jnp.bfloat16),
            pltpu.VMEM((local, slots, 128), jnp.float32),
            pltpu.VMEM((local, slots, features), jnp.bfloat16),
            pltpu.SemaphoreType.DMA((local,)),
            pltpu.SemaphoreType.DMA((local,)),
        ],
        compiler_params=GRANT,
        cost_estimate=pl.CostEstimate(
            flops=4 * local * slots * features * units,
            bytes_accessed=4 * local * features * units,
            transcendentals=local * slots * units,
        ),
        name="near_hidden",
    )(*tables, *tokens, in_hbm(w_gate), in_hbm(w_up))


def far_plan_kernel(capacity, far_count, *refs):
    tables = refs[:far_count]
    hots, coefs = refs[-2:]
    for p in range(far_count // 2):
        plan(tables[2 * p : 2 * p + 2], capacity, hots.at[p], coefs.at[p])


def far_plan(tables, order, capacity, local):
    pairs = len(tables) // 2
    count = tables[0].shape[1]
    slots = slots_of(capacity, 2)
    return pl.pallas_call(
        functools.partial(far_plan_kernel, capacity, len(tables)),
        out_shape=(
            pltpu.VMEM((pairs, local, slots, 2 * count), jnp.bfloat16),
            pltpu.VMEM((pairs, local, slots, 128), jnp.float32),
        ),
        in_specs=[VMEM] * len(tables) + [ANY],
        out_specs=(VMEM,) * 2,
        compiler_params=SMALL,
        cost_estimate=BRIEF,
        name="far_plan",
    )(*tables, order)


def far_kernel(far_count, *refs):
    tokens = refs[:far_count]
    hots, coefs, gates, ups, down_hbm, start_hbm, _, hidden, downs, start, rows, sems = refs[far_count:]
    copies = [
        pltpu.make_async_copy(down_hbm, downs, sems.at[0]),
        pltpu.make_async_copy(start_hbm, start, sems.at[1]),
    ]
    for copy in copies:
        copy.start()
    for p in range(far_count // 2):
        both = jnp.concatenate([tokens[2 * p][...], tokens[2 * p + 1][...]], axis=0)
        pack(hots.at[p], both, rows)
        for j in range(gates.shape[0]):
            expert_hidden(j, rows, hots.at[p], coefs.at[p], gates, ups, hidden, (p + 1) * hots.shape[3])
    for copy in copies:
        copy.wait()


def far_hidden(tokens, hots, coefs, gates, ups, w_down, start_state, hidden):
    pairs, local, slots, size = hots.shape
    features, units = gates.shape[1:]
    return pl.pallas_call(
        functools.partial(far_kernel, len(tokens)),
        out_shape=(
            pltpu.VMEM(hidden.shape, hidden.dtype),
            pltpu.VMEM(w_down.shape, w_down.dtype),
            pltpu.VMEM(start_state.shape, start_state.dtype),
        ),
        in_specs=[VMEM] * (len(tokens) + 4) + [HBM] * 2 + [VMEM],
        out_specs=(VMEM,) * 3,
        scratch_shapes=[
            pltpu.VMEM((local, slots, features), jnp.bfloat16),
            pltpu.SemaphoreType.DMA((2,)),
        ],
        input_output_aliases={len(tokens) + 6: 0},
        compiler_params=GRANT,
        cost_estimate=pl.CostEstimate(
            flops=4 * pairs * local * slots * features * units,
            bytes_accessed=6 * local * features * units,
            transcendentals=pairs * local * slots * units,
        ),
        name="far_hidden",
    )(*tokens, hots, coefs, gates, ups, in_hbm(w_down), in_hbm(start_state), hidden)


def down_kernel(core, start, hidden_ref, down_ref, _, out_ref):
    pairs, count, width = out_ref.shape
    local, units, _ = down_ref.shape
    columns = pl.ds(start, width)
    total = None
    for j in range(local):
        inner = pl.ds(j * units, units)
        parts = [hidden_ref[pl.ds((2 * p + core) * count, count), inner] for p in range(pairs)]
        term = jnp.dot(
            jnp.concatenate(parts, axis=0), down_ref[j, :, columns], preferred_element_type=jnp.float32
        )
        total = term if total is None else total + term
    for p in range(pairs):
        out_ref[p] = total[p * count : (p + 1) * count].astype(out_ref.dtype)


def down_rows(hidden, downs, order, core, count, start, width, dtype):
    pairs = hidden.shape[0] // (2 * count)
    return pl.pallas_call(
        functools.partial(down_kernel, core, start),
        out_shape=pltpu.VMEM((pairs, count, width), dtype),
        in_specs=[VMEM, VMEM, ANY],
        out_specs=VMEM,
        compiler_params=GRANT,
        cost_estimate=BRIEF,
        name="down_rows",
    )(hidden, downs, order)


def core_sum_kernel(chunks, keep, got, _, *outs):
    pairs, _, width = keep.shape
    width = width // chunks
    for i in range(chunks):
        columns = pl.ds(i * width, width)
        outs[2 * i][...] = keep[0, :, columns] + got[0, :, columns].astype(jnp.float32)
        for p in range(1, pairs):
            total = keep[p, :, columns] + got[p, :, columns].astype(jnp.float32)
            outs[2 * i + 1][p - 1] = total.astype(jnp.bfloat16)


def core_sum(keep, got, order, chunks):
    pairs, count, width = keep.shape
    shapes = []
    for _ in range(chunks):
        shapes.append(pltpu.VMEM((count, width // chunks), jnp.float32))
        shapes.append(pltpu.VMEM((pairs - 1, count, width // chunks), jnp.bfloat16))
    return pl.pallas_call(
        functools.partial(core_sum_kernel, chunks),
        out_shape=tuple(shapes),
        in_specs=[VMEM, VMEM, ANY],
        out_specs=(VMEM,) * len(shapes),
        compiler_params=SMALL,
        cost_estimate=BRIEF,
        name="core_sum",
    )(keep, got, order)


def wave_kernel(wave, window, backs, got_count, *refs):
    place = lax.axis_index("tm")
    send, prefix = refs[-2:]
    for n, i in enumerate(window):
        own = refs[n * (1 + backs)]
        more = refs[n * (1 + backs) + 1 : (n + 1) * (1 + backs)]

        @pl.when(place == wave - i)
        def _(own=own, more=more, first=wave == i):
            total = own[...]
            for ref in more:
                total = total + ref[...].astype(jnp.float32)
            if not first:
                total = total + refs[len(window) * (1 + backs)][...].astype(jnp.float32)
            prefix[...] = total
            send[...] = total.astype(jnp.bfloat16)


def wave_step(wave, window, owns, backs, got, order):
    inputs = []
    for i in window:
        inputs += [owns[i], *backs[i]]
    inputs += [] if got is None else [got]
    shape = owns[window[0]].shape
    return pl.pallas_call(
        functools.partial(wave_kernel, wave, window, len(backs[window[0]]), 0 if got is None else 1),
        out_shape=(pltpu.VMEM(shape, jnp.bfloat16), pltpu.VMEM(shape, jnp.float32)),
        in_specs=[VMEM] * len(inputs) + [ANY],
        out_specs=(VMEM, VMEM),
        compiler_params=SMALL,
        cost_estimate=BRIEF,
        name="wave_step",
    )(*inputs, order)


def finish_kernel(wave, chunks, stride, lane, start, prefix, *refs):
    out, mark, block, sem = refs[-4:]
    mark[...] = jnp.zeros_like(mark)
    place = lax.axis_index("tm")
    width = prefix.shape[1]
    for i in range(chunks):

        @pl.when(place == wave - i)
        def _(i=i):
            columns = pl.ds((i * stride + lane) * width, width)
            block[...] = start[:, columns] + prefix[...]
            copy = pltpu.make_async_copy(block, out.at[:, columns], sem)
            copy.start()
            copy.wait()


def finish(wave, chunks, stride, lane, start, prefix, out):
    inputs = [start, prefix] + ([] if out is None else [out])
    return pl.pallas_call(
        functools.partial(finish_kernel, wave, chunks, stride, lane),
        out_shape=(pltpu.HBM(start.shape, jnp.float32), pltpu.VMEM((8, 128), jnp.float32)),
        in_specs=[VMEM] * 2 + ([] if out is None else [HBM]),
        out_specs=(HBM, VMEM),
        scratch_shapes=[pltpu.VMEM(prefix.shape, jnp.float32), pltpu.SemaphoreType.DMA],
        input_output_aliases={} if out is None else {2: 0},
        compiler_params=SMALL,
        cost_estimate=BRIEF,
        name="finish",
    )(*inputs)


def tie_kernel(value_ref, order_ref, out_ref):
    pass


def tie(value, order):
    return pl.pallas_call(
        tie_kernel,
        out_shape=jax.ShapeDtypeStruct(value.shape, value.dtype),
        in_specs=[ANY, ANY],
        out_specs=ANY,
        input_output_aliases={0: 0},
        compiler_params=SMALL,
        cost_estimate=BRIEF,
        name="tie",
    )(value, order)


def shards(tokens, route_ids, route_probs, step_size, start_state, w_gate, w_up, w_down):
    members = lax.axis_size("expert")
    steps = lax.axis_size("tm")
    tok_count, feature_count = tokens.shape[1:]
    topk_count = route_ids.shape[2]
    expert_total = w_gate.shape[0] * members
    capacity = 3 * tok_count * topk_count // (2 * expert_total)
    chips = members // 2

    def swapped(value, by=0):
        return lax.ppermute(value, "expert", [(i, (i + 2 * by) % members ^ 1) for i in range(members)])

    def shifted(value, by):
        return lax.ppermute(value, "expert", [(i, (i + 2 * by) % members) for i in range(members)])

    own = tokens[0]
    far_same = [shifted(own, by) for by in range(1, chips)]
    partner = swapped(own)
    table, own = make_table(step_size, route_ids, route_probs, tokens, expert_total)
    tables = [table, swapped(table)]
    far_tables = []
    for by in range(1, chips):
        far_tables += [shifted(table, by), swapped(table, by)]
    hidden, gates, ups = near_hidden(tables, [own, partner], w_gate, w_up, capacity, members)
    hots, coefs = far_plan(far_tables, hidden, capacity, w_gate.shape[0])
    far_tokens = []
    for piece in far_same:
        piece = tie(piece, coefs)
        far_tokens += [piece, swapped(piece)]
    hidden, downs, start = far_hidden(far_tokens, hots, coefs, gates, ups, w_down, start_state, hidden)

    lanes, chunks, halves = 2, 2, 2
    parts = lanes * chunks
    each = parts // halves
    width = feature_count // parts
    events = []
    for h in range(halves):
        events.append((4.2 * h, "send", h, 0))
        events.append((4.2 * h + 1.9, "keep", h, 0))
        events.append((4.2 if h == 0 else 10.0 + 1.9 * (h - 1), "core", h, 0))
    for lane in range(lanes):
        ready = 9.9 + 3.0 * lane
        for wave in range(chunks + steps - 1):
            events.append((ready, "wave", lane, wave))
            ready += 6.0
    order, out = hidden, None
    gots, keeps, owns, backs, arrived = {}, {}, {}, {}, {}
    for _, kind, c, wave in sorted(events):
        if kind == "send":
            send = down_rows(hidden, downs, order, 1, tok_count, c * each * width, each * width, jnp.bfloat16)
            gots[c] = swapped(send)
            order = send
        elif kind == "keep":
            keeps[c] = down_rows(hidden, downs, order, 0, tok_count, c * each * width, each * width, jnp.float32)
            order = keeps[c]
        elif kind == "core":
            sums = core_sum(keeps[c], gots[c], order, each)
            for i in range(each):
                owns[c * each + i] = sums[2 * i]
                backs[c * each + i] = [shifted(sums[2 * i + 1][by - 1], -by) for by in range(1, chips)]
            order = sums[0]
        else:
            window = [i for i in range(chunks) if 0 <= wave - i < steps]
            lane_owns = {i: owns[i * lanes + c] for i in window}
            lane_backs = {i: backs[i * lanes + c] for i in window}
            send, prefix = wave_step(wave, window, lane_owns, lane_backs, arrived.get(c), order)
            if wave < chunks + steps - 2:
                arrived[c] = lax.ppermute(send, "tm", [(z, (z + 1) % steps) for z in range(steps)])
            out, order = finish(wave, chunks, lanes, c, start, prefix, out)
    return out[None]


def solution(mesh):
    return jax.shard_map(
        shards,
        mesh=mesh,
        in_specs=(
            P("tm", ("copies", "expert"), None),
            P("tm", ("copies", "expert"), None),
            P("tm", ("copies", "expert"), None),
            P(("copies", "tm")),
            P(("copies", "expert"), None),
            P("expert", None, None),
            P("expert", None, None),
            P("expert", None, None),
        ),
        out_specs=P("tm", ("copies", "expert"), None),
        check_vma=False,
    )
```

```python
import functools

import jax
import jax.numpy as jnp
from jax import lax
from jax.experimental import pallas as pl
from jax.experimental.pallas import tpu as pltpu
from jax.sharding import PartitionSpec as P

ANY = pl.BlockSpec(memory_space=pl.ANY)
HBM = pl.BlockSpec(memory_space=pltpu.HBM)
VMEM = pl.BlockSpec(memory_space=pltpu.VMEM)
GRANT = pltpu.CompilerParams(vmem_limit_bytes=7 * 1024 * 1024)
BRIEF = pl.CostEstimate(flops=0, bytes_accessed=0, transcendentals=0)
SMALL = pltpu.CompilerParams(vmem_limit_bytes=2 * 1024 * 1024)


def in_hbm(value):
    return pltpu.with_memory_space_constraint(value, pltpu.HBM)


def slots_of(capacity, blocks):
    return -(-capacity * blocks // 16) * 16


def table_kernel(experts, ids_hbm, probs_hbm, tokens_hbm, table, tokens, ids, probs, sems):
    copy = pltpu.make_async_copy(tokens_hbm.at[0], tokens, sems.at[0])
    smalls = [
        pltpu.make_async_copy(ids_hbm, ids, sems.at[1]),
        pltpu.make_async_copy(probs_hbm, probs, sems.at[2]),
    ]
    copy.start()
    for small in smalls:
        small.start()
    for small in smalls:
        small.wait()
    choices, _, count = ids.shape
    total = probs[0]
    for k in range(1, choices):
        total = total + probs[k]
    names = lax.broadcasted_iota(jnp.int32, table.shape, 0)
    value = jnp.zeros(table.shape, jnp.float32)
    for k in range(choices):
        value = value + jnp.where(ids[k] == names, probs[k] / total, 0.0)
    copy.wait()
    rows = tokens[...].astype(jnp.float32)
    scale = lax.rsqrt(jnp.mean(rows * rows, axis=1, keepdims=True) + 1e-06)
    scale = jnp.broadcast_to(scale, (count, 128)).T[:1]
    table[...] = jnp.where(names == experts, scale, value)


def make_table(ids, probs, tokens, experts):
    count, features = tokens.shape[1:]
    height = -(-(experts + 1) // 8) * 8
    ids, probs = jnp.transpose(ids, (2, 0, 1)), jnp.transpose(probs, (2, 0, 1))
    return pl.pallas_call(
        functools.partial(table_kernel, experts),
        out_shape=(
            pltpu.VMEM((height, count), jnp.float32),
            pltpu.VMEM((count, features), tokens.dtype),
        ),
        in_specs=[HBM] * 3,
        out_specs=(VMEM, VMEM),
        scratch_shapes=[
            pltpu.VMEM(ids.shape, ids.dtype),
            pltpu.VMEM(probs.shape, probs.dtype),
            pltpu.SemaphoreType.DMA((3,)),
        ],
        compiler_params=SMALL,
        name="make_table",
    )(in_hbm(ids), in_hbm(probs), in_hbm(tokens))


def plan(tables, capacity, hots, coefs):
    local, slots, width = hots.shape
    blocks = len(tables)
    count = width // blocks
    experts = local * lax.axis_size("expert")
    first = lax.axis_index("expert") * local
    before = lax.broadcasted_iota(jnp.int32, (count, count), 0)
    after = lax.broadcasted_iota(jnp.int32, (count, count), 1)
    upto = jnp.where(before <= after, 1.0, 0.0).astype(jnp.bfloat16)
    slot_ids = lax.broadcasted_iota(jnp.int32, (slots, width), 0).astype(jnp.float32)
    weights, scales, places = [], [], []
    for b in range(blocks):
        weight = tables[b][pl.ds(first, local), :]
        ones = jnp.where(weight > 0.0, 1.0, 0.0)
        padded = jnp.concatenate([ones, jnp.zeros((-local % 16, count), jnp.float32)], axis=0)
        rank = jnp.dot(padded.astype(jnp.bfloat16), upto, preferred_element_type=jnp.float32)[:local]
        places.append(jnp.where(weight > 0.0, rank + float(b * capacity - 1), -1.0))
        weights.append(weight)
        scales.append(tables[b][pl.ds(experts, 1), :])
    weight = jnp.concatenate(weights, axis=1) if blocks > 1 else weights[0]
    scale = jnp.concatenate(scales, axis=1) if blocks > 1 else scales[0]
    place = jnp.concatenate(places, axis=1) if blocks > 1 else places[0]
    for j in range(local):
        hit = slot_ids == place[j : j + 1, :]
        hots[j] = jnp.where(hit, 1.0, 0.0).astype(jnp.bfloat16)
        coefs[j, :, 0:1] = jnp.sum(jnp.where(hit, scale, 0.0), axis=1, keepdims=True)
        coefs[j, :, 1:2] = jnp.sum(jnp.where(hit, weight[j : j + 1, :], 0.0), axis=1, keepdims=True)


def pack(hots, tokens, rows):
    for j in range(hots.shape[0]):
        rows[j] = jnp.dot(hots[j], tokens, preferred_element_type=jnp.float32).astype(jnp.bfloat16)


def expert_hidden(j, rows, hots, coefs, gates, ups, out_ref, base):
    units = gates.shape[2]
    size = hots.shape[2]
    gate = jnp.dot(rows[j], gates[j], preferred_element_type=jnp.float32)
    up = jnp.dot(rows[j], ups[j], preferred_element_type=jnp.float32)
    scale = coefs[j, :, 0:1]
    weight = coefs[j, :, 1:2]
    g = gate * scale
    h = (g / (1.0 + jnp.exp(-g))) * (up * (scale * weight))
    placed = lax.dot_general(
        hots[j], h.astype(jnp.bfloat16), (((0,), (0,)), ((), ())), preferred_element_type=jnp.float32
    )
    out_ref[pl.ds(base, size), pl.ds(j * units, units)] = placed.astype(jnp.bfloat16)


def near_kernel(capacity, *refs):
    tables, tokens = refs[:2], refs[2:4]
    gate_hbm, up_hbm, hidden, gates, ups = refs[4:9]
    hots, coefs, rows, gate_sem, up_sem = refs[9:]
    local = gates.shape[0]
    copies = []
    for j in range(local):
        copies.append(pltpu.make_async_copy(gate_hbm.at[j], gates.at[j], gate_sem.at[j]))
        copies.append(pltpu.make_async_copy(up_hbm.at[j], ups.at[j], up_sem.at[j]))
    for copy in copies:
        copy.start()
    plan(tables, capacity, hots, coefs)
    pack(hots, jnp.concatenate([t[...] for t in tokens], axis=0), rows)
    for j in range(local):
        copies[2 * j].wait()
        copies[2 * j + 1].wait()
        expert_hidden(j, rows, hots, coefs, gates, ups, hidden, 0)


def near_hidden(tables, tokens, w_gate, w_up, capacity, blocks):
    count, features = tokens[0].shape
    local, _, units = w_gate.shape
    slots = slots_of(capacity, 2)
    return pl.pallas_call(
        functools.partial(near_kernel, capacity),
        out_shape=(
            pltpu.VMEM((blocks * count, local * units), jnp.bfloat16),
            pltpu.VMEM(w_gate.shape, w_gate.dtype),
            pltpu.VMEM(w_up.shape, w_up.dtype),
        ),
        in_specs=[VMEM] * 4 + [HBM] * 2,
        out_specs=(VMEM,) * 3,
        scratch_shapes=[
            pltpu.VMEM((local, slots, 2 * count), jnp.bfloat16),
            pltpu.VMEM((local, slots, 128), jnp.float32),
            pltpu.VMEM((local, slots, features), jnp.bfloat16),
            pltpu.SemaphoreType.DMA((local,)),
            pltpu.SemaphoreType.DMA((local,)),
        ],
        compiler_params=GRANT,
        cost_estimate=pl.CostEstimate(
            flops=4 * local * slots * features * units,
            bytes_accessed=4 * local * features * units,
            transcendentals=local * slots * units,
        ),
        name="near_hidden",
    )(*tables, *tokens, in_hbm(w_gate), in_hbm(w_up))


def far_plan_kernel(capacity, far_count, *refs):
    tables = refs[:far_count]
    step, _, hots, coefs, factor = refs[far_count:]
    factor[...] = jnp.full(factor.shape, step[0])
    for p in range(far_count // 2):
        plan(tables[2 * p : 2 * p + 2], capacity, hots.at[p], coefs.at[p])


def far_plan(tables, step_size, order, capacity, local):
    pairs = len(tables) // 2
    count = tables[0].shape[1]
    slots = slots_of(capacity, 2)
    return pl.pallas_call(
        functools.partial(far_plan_kernel, capacity, len(tables)),
        out_shape=(
            pltpu.VMEM((pairs, local, slots, 2 * count), jnp.bfloat16),
            pltpu.VMEM((pairs, local, slots, 128), jnp.float32),
            pltpu.VMEM((8, 128), jnp.float32),
        ),
        in_specs=[VMEM] * len(tables) + [pl.BlockSpec(memory_space=pltpu.SMEM), ANY],
        out_specs=(VMEM,) * 3,
        compiler_params=SMALL,
        cost_estimate=BRIEF,
        name="far_plan",
    )(*tables, step_size, order)


def far_kernel(far_count, *refs):
    tokens = refs[:far_count]
    hots, coefs, gates, ups, down_hbm, start_hbm, _, hidden, downs, start, rows, sems = refs[far_count:]
    copies = [
        pltpu.make_async_copy(down_hbm, downs, sems.at[0]),
        pltpu.make_async_copy(start_hbm, start, sems.at[1]),
    ]
    for copy in copies:
        copy.start()
    for p in range(far_count // 2):
        both = jnp.concatenate([tokens[2 * p][...], tokens[2 * p + 1][...]], axis=0)
        pack(hots.at[p], both, rows)
        for j in range(gates.shape[0]):
            expert_hidden(j, rows, hots.at[p], coefs.at[p], gates, ups, hidden, (p + 1) * hots.shape[3])
    for copy in copies:
        copy.wait()


def far_hidden(tokens, hots, coefs, gates, ups, w_down, start_state, hidden):
    pairs, local, slots, size = hots.shape
    features, units = gates.shape[1:]
    return pl.pallas_call(
        functools.partial(far_kernel, len(tokens)),
        out_shape=(
            pltpu.VMEM(hidden.shape, hidden.dtype),
            pltpu.VMEM(w_down.shape, w_down.dtype),
            pltpu.VMEM(start_state.shape, start_state.dtype),
        ),
        in_specs=[VMEM] * (len(tokens) + 4) + [HBM] * 2 + [VMEM],
        out_specs=(VMEM,) * 3,
        scratch_shapes=[
            pltpu.VMEM((local, slots, features), jnp.bfloat16),
            pltpu.SemaphoreType.DMA((2,)),
        ],
        input_output_aliases={len(tokens) + 6: 0},
        compiler_params=GRANT,
        cost_estimate=pl.CostEstimate(
            flops=4 * pairs * local * slots * features * units,
            bytes_accessed=6 * local * features * units,
            transcendentals=pairs * local * slots * units,
        ),
        name="far_hidden",
    )(*tokens, hots, coefs, gates, ups, in_hbm(w_down), in_hbm(start_state), hidden)


def down_kernel(core, start, hidden_ref, down_ref, _, out_ref):
    pairs, count, width = out_ref.shape
    local, units, _ = down_ref.shape
    columns = pl.ds(start, width)
    total = None
    for j in range(local):
        inner = pl.ds(j * units, units)
        parts = [hidden_ref[pl.ds((2 * p + core) * count, count), inner] for p in range(pairs)]
        term = jnp.dot(
            jnp.concatenate(parts, axis=0), down_ref[j, :, columns], preferred_element_type=jnp.float32
        )
        total = term if total is None else total + term
    for p in range(pairs):
        out_ref[p] = total[p * count : (p + 1) * count].astype(out_ref.dtype)


def down_rows(hidden, downs, order, core, count, start, width, dtype):
    pairs = hidden.shape[0] // (2 * count)
    return pl.pallas_call(
        functools.partial(down_kernel, core, start),
        out_shape=pltpu.VMEM((pairs, count, width), dtype),
        in_specs=[VMEM, VMEM, ANY],
        out_specs=VMEM,
        compiler_params=GRANT,
        cost_estimate=BRIEF,
        name="down_rows",
    )(hidden, downs, order)


def core_sum_kernel(chunks, keep, got, factor, _, *outs):
    pairs, _, width = keep.shape
    width = width // chunks
    step = factor[0:1, 0:1]
    for i in range(chunks):
        columns = pl.ds(i * width, width)
        for p in range(pairs):
            total = step * (keep[p, :, columns] + got[p, :, columns].astype(jnp.float32))
            if p == 0:
                outs[2 * i][...] = total
            else:
                outs[2 * i + 1][p - 1] = total.astype(jnp.bfloat16)


def core_sum(keep, got, factor, order, chunks):
    pairs, count, width = keep.shape
    shapes = []
    for _ in range(chunks):
        shapes.append(pltpu.VMEM((count, width // chunks), jnp.float32))
        shapes.append(pltpu.VMEM((pairs - 1, count, width // chunks), jnp.bfloat16))
    return pl.pallas_call(
        functools.partial(core_sum_kernel, chunks),
        out_shape=tuple(shapes),
        in_specs=[VMEM, VMEM, VMEM, ANY],
        out_specs=(VMEM,) * len(shapes),
        compiler_params=SMALL,
        cost_estimate=BRIEF,
        name="core_sum",
    )(keep, got, factor, order)


def lane_total(wave, i, backs, refs, got):
    own, *more = refs[: 1 + backs]
    total = own[...]
    for ref in more:
        total = total + ref[...].astype(jnp.float32)
    return total if got is None or wave == i else total + got[...].astype(jnp.float32)


def wave_kernel(wave, window, backs, has_got, *refs):
    place = lax.axis_index("tm")
    send, prefix = refs[-2:]
    got = refs[len(window) * (1 + backs)] if has_got else None
    for n, i in enumerate(window):

        @pl.when(place == wave - i)
        def _(n=n, i=i):
            total = lane_total(wave, i, backs, refs[n * (1 + backs) :], got)
            prefix[...] = total
            send[...] = total.astype(jnp.bfloat16)


def lane_inputs(window, owns, backs, got):
    inputs = []
    for i in window:
        inputs += [owns[i], *backs[i]]
    return inputs + ([] if got is None else [got])


def wave_step(wave, window, owns, backs, got, order):
    inputs = lane_inputs(window, owns, backs, got)
    shape = owns[window[0]].shape
    return pl.pallas_call(
        functools.partial(wave_kernel, wave, window, len(backs[window[0]]), got is not None),
        out_shape=(pltpu.VMEM(shape, jnp.bfloat16), pltpu.VMEM(shape, jnp.float32)),
        in_specs=[VMEM] * len(inputs) + [ANY],
        out_specs=(VMEM, VMEM),
        compiler_params=SMALL,
        cost_estimate=BRIEF,
        name="wave_step",
    )(*inputs, order)


def put_columns(out, block, sem, first):
    copy = pltpu.make_async_copy(block, out.at[:, pl.ds(first, block.shape[1])], sem)
    copy.start()
    copy.wait()


def finish_kernel(wave, window, stride, lane, start, _, prefix, *refs):
    out, mark, block, sem = refs[-4:]
    mark[...] = jnp.zeros_like(mark)
    width = prefix.shape[1]
    for i in window:

        @pl.when(lax.axis_index("tm") == wave - i)
        def _(first=(i * stride + lane) * width):
            block[...] = start[:, pl.ds(first, width)] + prefix[...]
            put_columns(out, block, sem, first)


def last_kernel(wave, i, backs, first, start, order, *refs):
    out, mark, block, sem = refs[-4:]
    mark[...] = jnp.zeros_like(mark)

    @pl.when(lax.axis_index("tm") == wave - i)
    def _():
        total = lane_total(wave, i, backs, refs, refs[1 + backs])
        block[...] = start[:, pl.ds(first, block.shape[1])] + total
        put_columns(out, block, sem, first)


def write_chunk(kernel, inputs, out, width, name):
    specs = [VMEM, ANY] + [VMEM] * (len(inputs) - 2)
    if out is not None:
        inputs, specs = inputs + [out], specs + [HBM]
    start = inputs[0]
    return pl.pallas_call(
        kernel,
        out_shape=(pltpu.HBM(start.shape, jnp.float32), pltpu.VMEM((8, 128), jnp.float32)),
        in_specs=specs,
        out_specs=(HBM, VMEM),
        scratch_shapes=[pltpu.VMEM((start.shape[0], width), jnp.float32), pltpu.SemaphoreType.DMA],
        input_output_aliases={} if out is None else {len(inputs) - 1: 0},
        compiler_params=SMALL,
        cost_estimate=BRIEF,
        name=name,
    )(*inputs)


def tie_kernel(value_ref, order_ref, out_ref):
    pass


def tie(value, order):
    return pl.pallas_call(
        tie_kernel,
        out_shape=jax.ShapeDtypeStruct(value.shape, value.dtype),
        in_specs=[ANY, ANY],
        out_specs=ANY,
        input_output_aliases={0: 0},
        compiler_params=SMALL,
        cost_estimate=BRIEF,
        name="tie",
    )(value, order)


def shards(tokens, route_ids, route_probs, step_size, start_state, w_gate, w_up, w_down):
    members = lax.axis_size("expert")
    steps = lax.axis_size("tm")
    tok_count, feature_count = tokens.shape[1:]
    topk_count = route_ids.shape[2]
    expert_total = w_gate.shape[0] * members
    capacity = 3 * tok_count * topk_count // (2 * expert_total)
    chips = members // 2

    def swapped(value):
        return lax.ppermute(value, "expert", [(i, i ^ 1) for i in range(members)])

    def shifted(value, by):
        return lax.ppermute(value, "expert", [(i, (i + 2 * by) % members) for i in range(members)])

    own = tokens[0]
    far_same = [shifted(own, by) for by in range(1, chips)]
    partner = swapped(own)
    table, own = make_table(route_ids, route_probs, tokens, expert_total)
    far_table = [shifted(table, by) for by in range(1, chips)]
    hidden, gates, ups = near_hidden([table, swapped(table)], [own, partner], w_gate, w_up, capacity, members)
    far_tables, far_tokens = [], []
    for value, piece in zip(far_table, far_same):
        value = tie(value, hidden)
        piece = tie(piece, value)
        far_tables += [value, swapped(value)]
        far_tokens += [piece, swapped(piece)]
    hots, coefs, factor = far_plan(far_tables, step_size, hidden, capacity, w_gate.shape[0])
    hidden, downs, start = far_hidden(far_tokens, hots, coefs, gates, ups, w_down, start_state, hidden)

    lanes, chunks, halves = 2, 2, 2
    parts = lanes * chunks
    each = parts // halves
    width = feature_count // parts
    events = []
    for h in range(halves):
        events.append((4.2 * h, "send", h, 0))
        events.append((4.2 * h + 1.9, "keep", h, 0))
        events.append((4.2 if h == 0 else 10.0 + 1.9 * (h - 1), "core", h, 0))
    for lane in range(lanes):
        ready = 9.9 + 3.0 * lane
        for wave in range(chunks + steps - 1):
            events.append((ready, "wave", lane, wave))
            ready += 6.0
    order, out = hidden, None
    gots, keeps, owns, backs, arrived = {}, {}, {}, {}, {}
    for _, kind, c, wave in sorted(events):
        if kind == "send":
            send = down_rows(hidden, downs, order, 1, tok_count, c * each * width, each * width, jnp.bfloat16)
            gots[c] = swapped(send)
            order = send
        elif kind == "keep":
            keeps[c] = down_rows(hidden, downs, order, 0, tok_count, c * each * width, each * width, jnp.float32)
            order = keeps[c]
        elif kind == "core":
            sums = core_sum(keeps[c], gots[c], factor, order, each)
            for i in range(each):
                owns[c * each + i] = sums[2 * i]
                backs[c * each + i] = [shifted(sums[2 * i + 1][by - 1], -by) for by in range(1, chips)]
            order = sums[0]
        else:
            window = [i for i in range(chunks) if 0 <= wave - i < steps]
            lane_owns = {i: owns[i * lanes + c] for i in window}
            lane_backs = {i: backs[i * lanes + c] for i in window}
            got = arrived.get(c)
            if wave < chunks + steps - 2:
                send, prefix = wave_step(wave, window, lane_owns, lane_backs, got, order)
                senders = [z for z in range(steps - 1) if wave - z in window]
                ring = dict.fromkeys(range(steps))
                ring.update({z: z + 1 for z in senders})
                ring[senders[-1] + 1] = senders[0]
                pairs = [(z, z if to is None else to) for z, to in ring.items()]
                arrived[c] = lax.ppermute(send, "tm", pairs)
                kernel = functools.partial(finish_kernel, wave, window, lanes, c)
                out, order = write_chunk(kernel, [start, order, prefix], out, width, "finish")
            else:
                i = window[0]
                kernel = functools.partial(
                    last_kernel, wave, i, len(lane_backs[i]), (i * lanes + c) * width
                )
                inputs = [start, order] + lane_inputs(window, lane_owns, lane_backs, got)
                out, order = write_chunk(kernel, inputs, out, width, "last")
    return out[None]


def solution(mesh):
    return jax.shard_map(
        shards,
        mesh=mesh,
        in_specs=(
            P("tm", ("copies", "expert"), None),
            P("tm", ("copies", "expert"), None),
            P("tm", ("copies", "expert"), None),
            P(("copies", "tm")),
            P(("copies", "expert"), None),
            P("expert", None, None),
            P("expert", None, None),
            P("expert", None, None),
        ),
        out_specs=P("tm", ("copies", "expert"), None),
        check_vma=False,
    )
```

```python
import functools

import jax
import jax.numpy as jnp
from jax import lax
from jax.experimental import pallas as pl
from jax.experimental.pallas import tpu as pltpu
from jax.sharding import PartitionSpec as P

ANY = pl.BlockSpec(memory_space=pl.ANY)
HBM = pl.BlockSpec(memory_space=pltpu.HBM)
VMEM = pl.BlockSpec(memory_space=pltpu.VMEM)
GRANT = pltpu.CompilerParams(vmem_limit_bytes=7 * 1024 * 1024)
BRIEF = pl.CostEstimate(flops=0, bytes_accessed=0, transcendentals=0)
SMALL = pltpu.CompilerParams(vmem_limit_bytes=2 * 1024 * 1024)


def in_hbm(value):
    return pltpu.with_memory_space_constraint(value, pltpu.HBM)


def slots_of(capacity, blocks):
    return -(-capacity * blocks // 16) * 16


def table_kernel(experts, ids_hbm, probs_hbm, tokens_hbm, table, tokens, ids, probs, sems):
    copy = pltpu.make_async_copy(tokens_hbm.at[0], tokens, sems.at[0])
    smalls = [
        pltpu.make_async_copy(ids_hbm, ids, sems.at[1]),
        pltpu.make_async_copy(probs_hbm, probs, sems.at[2]),
    ]
    copy.start()
    for small in smalls:
        small.start()
    for small in smalls:
        small.wait()
    choices, _, count = ids.shape
    total = probs[0]
    for k in range(1, choices):
        total = total + probs[k]
    names = lax.broadcasted_iota(jnp.int32, table.shape, 0)
    value = jnp.zeros(table.shape, jnp.float32)
    for k in range(choices):
        value = value + jnp.where(ids[k] == names, probs[k] / total, 0.0)
    copy.wait()
    rows = tokens[...].astype(jnp.float32)
    scale = lax.rsqrt(jnp.mean(rows * rows, axis=1, keepdims=True) + 1e-06)
    scale = jnp.broadcast_to(scale, (count, 128)).T[:1]
    table[...] = jnp.where(names == experts, scale, value)


def make_table(ids, probs, tokens, experts):
    count, features = tokens.shape[1:]
    height = -(-(experts + 1) // 8) * 8
    ids, probs = jnp.transpose(ids, (2, 0, 1)), jnp.transpose(probs, (2, 0, 1))
    return pl.pallas_call(
        functools.partial(table_kernel, experts),
        out_shape=(
            pltpu.VMEM((height, count), jnp.float32),
            pltpu.VMEM((count, features), tokens.dtype),
        ),
        in_specs=[HBM] * 3,
        out_specs=(VMEM, VMEM),
        scratch_shapes=[
            pltpu.VMEM(ids.shape, ids.dtype),
            pltpu.VMEM(probs.shape, probs.dtype),
            pltpu.SemaphoreType.DMA((3,)),
        ],
        compiler_params=SMALL,
        name="make_table",
    )(in_hbm(ids), in_hbm(probs), in_hbm(tokens))


def plan(tables, capacity, hots, coefs):
    local, slots, width = hots.shape
    blocks = len(tables)
    count = width // blocks
    experts = local * lax.axis_size("expert")
    first = lax.axis_index("expert") * local
    before = lax.broadcasted_iota(jnp.int32, (count, count), 0)
    after = lax.broadcasted_iota(jnp.int32, (count, count), 1)
    upto = jnp.where(before <= after, 1.0, 0.0).astype(jnp.bfloat16)
    slot_ids = lax.broadcasted_iota(jnp.int32, (slots, width), 0).astype(jnp.float32)
    weights, scales, places = [], [], []
    for b in range(blocks):
        weight = tables[b][pl.ds(first, local), :]
        ones = jnp.where(weight > 0.0, 1.0, 0.0)
        padded = jnp.concatenate([ones, jnp.zeros((-local % 16, count), jnp.float32)], axis=0)
        rank = jnp.dot(padded.astype(jnp.bfloat16), upto, preferred_element_type=jnp.float32)[:local]
        places.append(jnp.where(weight > 0.0, rank + float(b * capacity - 1), -1.0))
        weights.append(weight)
        scales.append(tables[b][pl.ds(experts, 1), :])
    weight = jnp.concatenate(weights, axis=1) if blocks > 1 else weights[0]
    scale = jnp.concatenate(scales, axis=1) if blocks > 1 else scales[0]
    place = jnp.concatenate(places, axis=1) if blocks > 1 else places[0]
    for j in range(local):
        hit = slot_ids == place[j : j + 1, :]
        hots[j] = jnp.where(hit, 1.0, 0.0).astype(jnp.bfloat16)
        coefs[j, :, 0:1] = jnp.sum(jnp.where(hit, scale, 0.0), axis=1, keepdims=True)
        coefs[j, :, 1:2] = jnp.sum(jnp.where(hit, weight[j : j + 1, :], 0.0), axis=1, keepdims=True)


def pack(hots, tokens, rows):
    for j in range(hots.shape[0]):
        rows[j] = jnp.dot(hots[j], tokens, preferred_element_type=jnp.float32).astype(jnp.bfloat16)


def expert_hidden(j, rows, hots, coefs, gates, ups, out_ref, base):
    units = gates.shape[2]
    size = hots.shape[2]
    gate = jnp.dot(rows[j], gates[j], preferred_element_type=jnp.float32)
    up = jnp.dot(rows[j], ups[j], preferred_element_type=jnp.float32)
    scale = coefs[j, :, 0:1]
    weight = coefs[j, :, 1:2]
    g = gate * scale
    h = (g / (1.0 + jnp.exp(-g))) * (up * (scale * weight))
    placed = lax.dot_general(
        hots[j], h.astype(jnp.bfloat16), (((0,), (0,)), ((), ())), preferred_element_type=jnp.float32
    )
    out_ref[pl.ds(base, size), pl.ds(j * units, units)] = placed.astype(jnp.bfloat16)


def near_kernel(capacity, *refs):
    tables, tokens = refs[:2], refs[2:4]
    gate_hbm, up_hbm, hidden, gates, ups = refs[4:9]
    hots, coefs, rows, gate_sem, up_sem = refs[9:]
    local = gates.shape[0]
    copies = []
    for j in range(local):
        copies.append(pltpu.make_async_copy(gate_hbm.at[j], gates.at[j], gate_sem.at[j]))
        copies.append(pltpu.make_async_copy(up_hbm.at[j], ups.at[j], up_sem.at[j]))
    for copy in copies:
        copy.start()
    plan(tables, capacity, hots, coefs)
    pack(hots, jnp.concatenate([t[...] for t in tokens], axis=0), rows)
    for j in range(local):
        copies[2 * j].wait()
        copies[2 * j + 1].wait()
        expert_hidden(j, rows, hots, coefs, gates, ups, hidden, 0)


def near_hidden(tables, tokens, w_gate, w_up, capacity, blocks):
    count, features = tokens[0].shape
    local, _, units = w_gate.shape
    slots = slots_of(capacity, 2)
    return pl.pallas_call(
        functools.partial(near_kernel, capacity),
        out_shape=(
            pltpu.VMEM((blocks * count, local * units), jnp.bfloat16),
            pltpu.VMEM(w_gate.shape, w_gate.dtype),
            pltpu.VMEM(w_up.shape, w_up.dtype),
        ),
        in_specs=[VMEM] * 4 + [HBM] * 2,
        out_specs=(VMEM,) * 3,
        scratch_shapes=[
            pltpu.VMEM((local, slots, 2 * count), jnp.bfloat16),
            pltpu.VMEM((local, slots, 128), jnp.float32),
            pltpu.VMEM((local, slots, features), jnp.bfloat16),
            pltpu.SemaphoreType.DMA((local,)),
            pltpu.SemaphoreType.DMA((local,)),
        ],
        compiler_params=GRANT,
        cost_estimate=pl.CostEstimate(
            flops=4 * local * slots * features * units,
            bytes_accessed=4 * local * features * units,
            transcendentals=local * slots * units,
        ),
        name="near_hidden",
    )(*tables, *tokens, in_hbm(w_gate), in_hbm(w_up))


def far_plan_kernel(capacity, far_count, *refs):
    tables = refs[:far_count]
    step, _, hots, coefs, factor = refs[far_count:]
    factor[...] = jnp.full(factor.shape, step[0])
    for p in range(far_count // 2):
        plan(tables[2 * p : 2 * p + 2], capacity, hots.at[p], coefs.at[p])


def far_plan(tables, step_size, order, capacity, local):
    pairs = len(tables) // 2
    count = tables[0].shape[1]
    slots = slots_of(capacity, 2)
    return pl.pallas_call(
        functools.partial(far_plan_kernel, capacity, len(tables)),
        out_shape=(
            pltpu.VMEM((pairs, local, slots, 2 * count), jnp.bfloat16),
            pltpu.VMEM((pairs, local, slots, 128), jnp.float32),
            pltpu.VMEM((8, 128), jnp.float32),
        ),
        in_specs=[VMEM] * len(tables) + [pl.BlockSpec(memory_space=pltpu.SMEM), ANY],
        out_specs=(VMEM,) * 3,
        compiler_params=SMALL,
        cost_estimate=BRIEF,
        name="far_plan",
    )(*tables, step_size, order)


def far_kernel(far_count, *refs):
    tokens = refs[:far_count]
    hots, coefs, gates, ups, down_hbm, start_hbm, _, hidden, downs, start, rows, sems = refs[far_count:]
    copies = [
        pltpu.make_async_copy(down_hbm, downs, sems.at[0]),
        pltpu.make_async_copy(start_hbm, start, sems.at[1]),
    ]
    for copy in copies:
        copy.start()
    for p in range(far_count // 2):
        both = jnp.concatenate([tokens[2 * p][...], tokens[2 * p + 1][...]], axis=0)
        pack(hots.at[p], both, rows)
        for j in range(gates.shape[0]):
            expert_hidden(j, rows, hots.at[p], coefs.at[p], gates, ups, hidden, (p + 1) * hots.shape[3])
    for copy in copies:
        copy.wait()


def far_hidden(tokens, hots, coefs, gates, ups, w_down, start_state, hidden):
    pairs, local, slots, size = hots.shape
    features, units = gates.shape[1:]
    return pl.pallas_call(
        functools.partial(far_kernel, len(tokens)),
        out_shape=(
            pltpu.VMEM(hidden.shape, hidden.dtype),
            pltpu.VMEM(w_down.shape, w_down.dtype),
            pltpu.VMEM(start_state.shape, start_state.dtype),
        ),
        in_specs=[VMEM] * (len(tokens) + 4) + [HBM] * 2 + [VMEM],
        out_specs=(VMEM,) * 3,
        scratch_shapes=[
            pltpu.VMEM((local, slots, features), jnp.bfloat16),
            pltpu.SemaphoreType.DMA((2,)),
        ],
        input_output_aliases={len(tokens) + 6: 0},
        compiler_params=GRANT,
        cost_estimate=pl.CostEstimate(
            flops=4 * pairs * local * slots * features * units,
            bytes_accessed=6 * local * features * units,
            transcendentals=pairs * local * slots * units,
        ),
        name="far_hidden",
    )(*tokens, hots, coefs, gates, ups, in_hbm(w_down), in_hbm(start_state), hidden)


def down_kernel(core, start, hidden_ref, down_ref, _, out_ref):
    pairs, count, width = out_ref.shape
    local, units, _ = down_ref.shape
    columns = pl.ds(start, width)
    total = None
    for j in range(local):
        inner = pl.ds(j * units, units)
        parts = [hidden_ref[pl.ds((2 * p + core) * count, count), inner] for p in range(pairs)]
        term = jnp.dot(
            jnp.concatenate(parts, axis=0), down_ref[j, :, columns], preferred_element_type=jnp.float32
        )
        total = term if total is None else total + term
    for p in range(pairs):
        out_ref[p] = total[p * count : (p + 1) * count].astype(out_ref.dtype)


def down_rows(hidden, downs, order, send, count, start, width):
    pairs = hidden.shape[0] // (2 * count)
    return pl.pallas_call(
        functools.partial(down_kernel, int(send), start),
        out_shape=pltpu.VMEM((pairs, count, width), jnp.bfloat16 if send else jnp.float32),
        in_specs=[VMEM, VMEM, ANY],
        out_specs=VMEM,
        compiler_params=GRANT,
        cost_estimate=BRIEF,
        name="down_rows",
    )(hidden, downs, order)


def core_sum_kernel(chunks, keep, got, factor, _, *outs):
    pairs, _, width = keep.shape
    width = width // chunks
    step = factor[0:1, 0:1]
    for i in range(chunks):
        columns = pl.ds(i * width, width)
        for p in range(pairs):
            total = step * (keep[p, :, columns] + got[p, :, columns].astype(jnp.float32))
            if p == 0:
                outs[2 * i][...] = total
            else:
                outs[2 * i + 1][p - 1] = total.astype(jnp.bfloat16)


def core_sum(keep, got, factor, order, chunks):
    pairs, count, width = keep.shape
    shapes = []
    for _ in range(chunks):
        shapes.append(pltpu.VMEM((count, width // chunks), jnp.float32))
        shapes.append(pltpu.VMEM((pairs - 1, count, width // chunks), jnp.bfloat16))
    return pl.pallas_call(
        functools.partial(core_sum_kernel, chunks),
        out_shape=tuple(shapes),
        in_specs=[VMEM, VMEM, VMEM, ANY],
        out_specs=(VMEM,) * len(shapes),
        compiler_params=SMALL,
        cost_estimate=BRIEF,
        name="core_sum",
    )(keep, got, factor, order)


def lane_total(wave, i, backs, refs, got):
    own, *more = refs[: 1 + backs]
    total = own[...]
    for ref in more:
        total = total + ref[...].astype(jnp.float32)
    return total if got is None or wave == i else total + got[...].astype(jnp.float32)


def wave_kernel(wave, window, backs, has_got, *refs):
    place = lax.axis_index("tm")
    send, prefix = refs[-2:]
    got = refs[len(window) * (1 + backs)] if has_got else None
    for n, i in enumerate(window):

        @pl.when(place == wave - i)
        def _(n=n, i=i):
            total = lane_total(wave, i, backs, refs[n * (1 + backs) :], got)
            prefix[...] = total
            send[...] = total.astype(jnp.bfloat16)


def lane_inputs(window, owns, backs, got):
    inputs = []
    for i in window:
        inputs += [owns[i], *backs[i]]
    return inputs + ([] if got is None else [got])


def wave_step(wave, window, owns, backs, got, order):
    inputs = lane_inputs(window, owns, backs, got)
    shape = owns[window[0]].shape
    return pl.pallas_call(
        functools.partial(wave_kernel, wave, window, len(backs[window[0]]), got is not None),
        out_shape=(pltpu.VMEM(shape, jnp.bfloat16), pltpu.VMEM(shape, jnp.float32)),
        in_specs=[VMEM] * len(inputs) + [ANY],
        out_specs=(VMEM, VMEM),
        compiler_params=SMALL,
        cost_estimate=BRIEF,
        name="wave_step",
    )(*inputs, order)


def put_columns(out, block, sem, first):
    copy = pltpu.make_async_copy(block, out.at[:, pl.ds(first, block.shape[1])], sem)
    copy.start()
    copy.wait()


def finish_kernel(wave, window, stride, lane, start, _, prefix, *refs):
    out, mark, block, sem = refs[-4:]
    mark[...] = jnp.zeros_like(mark)
    width = prefix.shape[1]
    for i in window:

        @pl.when(lax.axis_index("tm") == wave - i)
        def _(first=(i * stride + lane) * width):
            block[...] = start[:, pl.ds(first, width)] + prefix[...]
            put_columns(out, block, sem, first)


def last_kernel(wave, i, backs, first, start, order, *refs):
    out, mark, block, sem = refs[-4:]
    mark[...] = jnp.zeros_like(mark)

    @pl.when(lax.axis_index("tm") == wave - i)
    def _():
        total = lane_total(wave, i, backs, refs, refs[1 + backs])
        block[...] = start[:, pl.ds(first, block.shape[1])] + total
        put_columns(out, block, sem, first)


def write_chunk(kernel, inputs, out, width, name):
    specs = [VMEM, ANY] + [VMEM] * (len(inputs) - 2)
    if out is not None:
        inputs, specs = inputs + [out], specs + [HBM]
    start = inputs[0]
    return pl.pallas_call(
        kernel,
        out_shape=(pltpu.HBM(start.shape, jnp.float32), pltpu.VMEM((8, 128), jnp.float32)),
        in_specs=specs,
        out_specs=(HBM, VMEM),
        scratch_shapes=[pltpu.VMEM((start.shape[0], width), jnp.float32), pltpu.SemaphoreType.DMA],
        input_output_aliases={} if out is None else {len(inputs) - 1: 0},
        compiler_params=SMALL,
        cost_estimate=BRIEF,
        name=name,
    )(*inputs)


def tie_kernel(value_ref, order_ref, out_ref):
    pass


def tie(value, order):
    return pl.pallas_call(
        tie_kernel,
        out_shape=jax.ShapeDtypeStruct(value.shape, value.dtype),
        in_specs=[ANY, ANY],
        out_specs=ANY,
        input_output_aliases={0: 0},
        compiler_params=SMALL,
        cost_estimate=BRIEF,
        name="tie",
    )(value, order)


def shards(tokens, route_ids, route_probs, step_size, start_state, w_gate, w_up, w_down):
    members = lax.axis_size("expert")
    steps = lax.axis_size("tm")
    tok_count, feature_count = tokens.shape[1:]
    topk_count = route_ids.shape[2]
    expert_total = w_gate.shape[0] * members
    capacity = 3 * tok_count * topk_count // (2 * expert_total)
    chips = members // 2

    def swapped(value):
        return lax.ppermute(value, "expert", [(i, i ^ 1) for i in range(members)])

    def shifted(value, by):
        return lax.ppermute(value, "expert", [(i, (i + 2 * by) % members) for i in range(members)])

    own = tokens[0]
    far_same = [shifted(own, by) for by in range(1, chips)]
    partner = swapped(own)
    table, own = make_table(route_ids, route_probs, tokens, expert_total)
    far_table = [shifted(table, by) for by in range(1, chips)]
    hidden, gates, ups = near_hidden([table, swapped(table)], [own, partner], w_gate, w_up, capacity, members)
    far_tables, far_tokens = [], []
    for value, piece in zip(far_table, far_same):
        value = tie(value, hidden)
        piece = tie(piece, value)
        far_tables += [value, swapped(value)]
        far_tokens += [piece, swapped(piece)]
    hots, coefs, factor = far_plan(far_tables, step_size, hidden, capacity, w_gate.shape[0])
    hidden, downs, start = far_hidden(far_tokens, hots, coefs, gates, ups, w_down, start_state, hidden)

    lanes, chunks = 2, 2
    parts = lanes * chunks
    width = feature_count // parts
    groups = [(0, 1), (1, parts - 1)]
    events, ready = [], 0.0
    for g, (_, count) in enumerate(groups):
        events.append((ready, "send", g, 0))
        events.append((ready + 0.9 * count, "keep", g, 0))
        ready += max(2.5, 1.8 * count)
        events.append((ready, "core", g, 0))
    for lane in range(lanes):
        ready = 10.0 + 3.0 * lane
        for wave in range(chunks + steps - 1):
            events.append((ready, "wave", lane, wave))
            ready += 6.0
    order, out = hidden, None
    gots, keeps, owns, backs, arrived = {}, {}, {}, {}, {}
    for _, kind, c, wave in sorted(events):
        if kind in ("send", "keep"):
            first, count = groups[c]
            part = down_rows(hidden, downs, order, kind == "send", tok_count, first * width, count * width)
            if kind == "send":
                gots[c] = swapped(part)
            else:
                keeps[c] = part
            order = part
        elif kind == "core":
            first, count = groups[c]
            sums = core_sum(keeps[c], gots[c], factor, order, count)
            for i in range(count):
                owns[first + i] = sums[2 * i]
                backs[first + i] = [shifted(sums[2 * i + 1][by - 1], -by) for by in range(1, chips)]
            order = sums[0]
        else:
            window = [i for i in range(chunks) if 0 <= wave - i < steps]
            lane_owns = {i: owns[i * lanes + c] for i in window}
            lane_backs = {i: backs[i * lanes + c] for i in window}
            got = arrived.get(c)
            if wave < chunks + steps - 2:
                send, prefix = wave_step(wave, window, lane_owns, lane_backs, got, order)
                pairs = [(z, (z + 1) % steps) for z in range(steps)]
                arrived[c] = lax.ppermute(send, "tm", pairs)
                kernel = functools.partial(finish_kernel, wave, window, lanes, c)
                out, order = write_chunk(kernel, [start, order, prefix], out, width, "finish")
            else:
                i = window[0]
                kernel = functools.partial(
                    last_kernel, wave, i, len(lane_backs[i]), (i * lanes + c) * width
                )
                inputs = [start, order] + lane_inputs(window, lane_owns, lane_backs, got)
                out, order = write_chunk(kernel, inputs, out, width, "last")
    return out[None]


def solution(mesh):
    return jax.shard_map(
        shards,
        mesh=mesh,
        in_specs=(
            P("tm", ("copies", "expert"), None),
            P("tm", ("copies", "expert"), None),
            P("tm", ("copies", "expert"), None),
            P(("copies", "tm")),
            P(("copies", "expert"), None),
            P("expert", None, None),
            P("expert", None, None),
            P("expert", None, None),
        ),
        out_specs=P("tm", ("copies", "expert"), None),
        check_vma=False,
    )
```

```python
import functools

import jax
import jax.numpy as jnp
from jax import lax
from jax.experimental import pallas as pl
from jax.experimental.pallas import tpu as pltpu
from jax.sharding import PartitionSpec as P

ANY = pl.BlockSpec(memory_space=pl.ANY)
HBM = pl.BlockSpec(memory_space=pltpu.HBM)
VMEM = pl.BlockSpec(memory_space=pltpu.VMEM)
GRANT = pltpu.CompilerParams(vmem_limit_bytes=7 * 1024 * 1024)
BRIEF = pl.CostEstimate(flops=0, bytes_accessed=0, transcendentals=0)
SMALL = pltpu.CompilerParams(vmem_limit_bytes=2 * 1024 * 1024)


def in_hbm(value):
    return pltpu.with_memory_space_constraint(value, pltpu.HBM)


def slots_of(capacity, blocks):
    return -(-capacity * blocks // 16) * 16


def table_kernel(experts, ids_hbm, probs_hbm, tokens_hbm, table, tokens, ids, probs, sems):
    copy = pltpu.make_async_copy(tokens_hbm.at[0], tokens, sems.at[0])
    smalls = [
        pltpu.make_async_copy(ids_hbm, ids, sems.at[1]),
        pltpu.make_async_copy(probs_hbm, probs, sems.at[2]),
    ]
    copy.start()
    for small in smalls:
        small.start()
    for small in smalls:
        small.wait()
    choices, _, count = ids.shape
    total = probs[0]
    for k in range(1, choices):
        total = total + probs[k]
    names = lax.broadcasted_iota(jnp.int32, table.shape, 0)
    value = jnp.zeros(table.shape, jnp.float32)
    for k in range(choices):
        value = value + jnp.where(ids[k] == names, probs[k] / total, 0.0)
    copy.wait()
    rows = tokens[...].astype(jnp.float32)
    scale = lax.rsqrt(jnp.mean(rows * rows, axis=1, keepdims=True) + 1e-06)
    scale = jnp.broadcast_to(scale, (count, 128)).T[:1]
    table[...] = jnp.where(names == experts, scale, value)


def make_table(ids, probs, tokens, experts):
    count, features = tokens.shape[1:]
    height = -(-(experts + 1) // 8) * 8
    ids, probs = jnp.transpose(ids, (2, 0, 1)), jnp.transpose(probs, (2, 0, 1))
    return pl.pallas_call(
        functools.partial(table_kernel, experts),
        out_shape=(
            pltpu.VMEM((height, count), jnp.float32),
            pltpu.VMEM((count, features), tokens.dtype),
        ),
        in_specs=[HBM] * 3,
        out_specs=(VMEM, VMEM),
        scratch_shapes=[
            pltpu.VMEM(ids.shape, ids.dtype),
            pltpu.VMEM(probs.shape, probs.dtype),
            pltpu.SemaphoreType.DMA((3,)),
        ],
        compiler_params=SMALL,
        name="make_table",
    )(in_hbm(ids), in_hbm(probs), in_hbm(tokens))


def plan(tables, capacity, hots, coefs):
    local, slots, width = hots.shape
    blocks = len(tables)
    count = width // blocks
    experts = local * lax.axis_size("expert")
    first = lax.axis_index("expert") * local
    before = lax.broadcasted_iota(jnp.int32, (count, count), 0)
    after = lax.broadcasted_iota(jnp.int32, (count, count), 1)
    upto = jnp.where(before <= after, 1.0, 0.0).astype(jnp.bfloat16)
    slot_ids = lax.broadcasted_iota(jnp.int32, (slots, width), 0).astype(jnp.float32)
    weights, scales, places = [], [], []
    for b in range(blocks):
        weight = tables[b][pl.ds(first, local), :]
        ones = jnp.where(weight > 0.0, 1.0, 0.0)
        padded = jnp.concatenate([ones, jnp.zeros((-local % 16, count), jnp.float32)], axis=0)
        rank = jnp.dot(padded.astype(jnp.bfloat16), upto, preferred_element_type=jnp.float32)[:local]
        places.append(jnp.where(weight > 0.0, rank + float(b * capacity - 1), -1.0))
        weights.append(weight)
        scales.append(tables[b][pl.ds(experts, 1), :])
    weight = jnp.concatenate(weights, axis=1) if blocks > 1 else weights[0]
    scale = jnp.concatenate(scales, axis=1) if blocks > 1 else scales[0]
    place = jnp.concatenate(places, axis=1) if blocks > 1 else places[0]
    for j in range(local):
        hit = slot_ids == place[j : j + 1, :]
        hots[j] = jnp.where(hit, 1.0, 0.0).astype(jnp.bfloat16)
        coefs[j, :, 0:1] = jnp.sum(jnp.where(hit, scale, 0.0), axis=1, keepdims=True)
        coefs[j, :, 1:2] = jnp.sum(jnp.where(hit, weight[j : j + 1, :], 0.0), axis=1, keepdims=True)


def pack(hots, tokens, rows):
    for j in range(hots.shape[0]):
        rows[j] = jnp.dot(hots[j], tokens, preferred_element_type=jnp.float32).astype(jnp.bfloat16)


def expert_hidden(j, rows, hots, coefs, gates, ups, out_ref, base):
    units = gates.shape[2]
    size = hots.shape[2]
    gate = jnp.dot(rows[j], gates[j], preferred_element_type=jnp.float32)
    up = jnp.dot(rows[j], ups[j], preferred_element_type=jnp.float32)
    scale = coefs[j, :, 0:1]
    weight = coefs[j, :, 1:2]
    g = gate * scale
    h = (g / (1.0 + jnp.exp(-g))) * (up * (scale * weight))
    placed = lax.dot_general(
        hots[j], h.astype(jnp.bfloat16), (((0,), (0,)), ((), ())), preferred_element_type=jnp.float32
    )
    out_ref[pl.ds(base, size), pl.ds(j * units, units)] = placed.astype(jnp.bfloat16)


def near_kernel(capacity, *refs):
    tables, tokens = refs[:2], refs[2:4]
    gate_hbm, up_hbm, hidden, gates, ups = refs[4:9]
    hots, coefs, rows, gate_sem, up_sem = refs[9:]
    local = gates.shape[0]
    copies = []
    for j in range(local):
        copies.append(pltpu.make_async_copy(gate_hbm.at[j], gates.at[j], gate_sem.at[j]))
        copies.append(pltpu.make_async_copy(up_hbm.at[j], ups.at[j], up_sem.at[j]))
    for copy in copies:
        copy.start()
    plan(tables, capacity, hots, coefs)
    pack(hots, jnp.concatenate([t[...] for t in tokens], axis=0), rows)
    for j in range(local):
        copies[2 * j].wait()
        copies[2 * j + 1].wait()
        expert_hidden(j, rows, hots, coefs, gates, ups, hidden, 0)


def near_hidden(tables, tokens, w_gate, w_up, capacity, blocks):
    count, features = tokens[0].shape
    local, _, units = w_gate.shape
    slots = slots_of(capacity, 2)
    return pl.pallas_call(
        functools.partial(near_kernel, capacity),
        out_shape=(
            pltpu.VMEM((blocks * count, local * units), jnp.bfloat16),
            pltpu.VMEM(w_gate.shape, w_gate.dtype),
            pltpu.VMEM(w_up.shape, w_up.dtype),
        ),
        in_specs=[VMEM] * 4 + [HBM] * 2,
        out_specs=(VMEM,) * 3,
        scratch_shapes=[
            pltpu.VMEM((local, slots, 2 * count), jnp.bfloat16),
            pltpu.VMEM((local, slots, 128), jnp.float32),
            pltpu.VMEM((local, slots, features), jnp.bfloat16),
            pltpu.SemaphoreType.DMA((local,)),
            pltpu.SemaphoreType.DMA((local,)),
        ],
        compiler_params=GRANT,
        cost_estimate=pl.CostEstimate(
            flops=4 * local * slots * features * units,
            bytes_accessed=4 * local * features * units,
            transcendentals=local * slots * units,
        ),
        name="near_hidden",
    )(*tables, *tokens, in_hbm(w_gate), in_hbm(w_up))


def far_plan_kernel(capacity, far_count, *refs):
    tables = refs[:far_count]
    step, _, hots, coefs, factor = refs[far_count:]
    factor[...] = jnp.full(factor.shape, step[0])
    for p in range(far_count // 2):
        plan(tables[2 * p : 2 * p + 2], capacity, hots.at[p], coefs.at[p])


def far_plan(tables, step_size, order, capacity, local):
    pairs = len(tables) // 2
    count = tables[0].shape[1]
    slots = slots_of(capacity, 2)
    return pl.pallas_call(
        functools.partial(far_plan_kernel, capacity, len(tables)),
        out_shape=(
            pltpu.VMEM((pairs, local, slots, 2 * count), jnp.bfloat16),
            pltpu.VMEM((pairs, local, slots, 128), jnp.float32),
            pltpu.VMEM((8, 128), jnp.float32),
        ),
        in_specs=[VMEM] * len(tables) + [pl.BlockSpec(memory_space=pltpu.SMEM), ANY],
        out_specs=(VMEM,) * 3,
        compiler_params=SMALL,
        cost_estimate=BRIEF,
        name="far_plan",
    )(*tables, step_size, order)


def far_kernel(far_count, *refs):
    tokens = refs[:far_count]
    hots, coefs, gates, ups, down_hbm, start_hbm, _, hidden, downs, start, rows, sems = refs[far_count:]
    copies = [
        pltpu.make_async_copy(down_hbm, downs, sems.at[0]),
        pltpu.make_async_copy(start_hbm, start, sems.at[1]),
    ]
    for copy in copies:
        copy.start()
    for p in range(far_count // 2):
        both = jnp.concatenate([tokens[2 * p][...], tokens[2 * p + 1][...]], axis=0)
        pack(hots.at[p], both, rows)
        for j in range(gates.shape[0]):
            expert_hidden(j, rows, hots.at[p], coefs.at[p], gates, ups, hidden, (p + 1) * hots.shape[3])
    for copy in copies:
        copy.wait()


def far_hidden(tokens, hots, coefs, gates, ups, w_down, start_state, hidden):
    pairs, local, slots, size = hots.shape
    features, units = gates.shape[1:]
    return pl.pallas_call(
        functools.partial(far_kernel, len(tokens)),
        out_shape=(
            pltpu.VMEM(hidden.shape, hidden.dtype),
            pltpu.VMEM(w_down.shape, w_down.dtype),
            pltpu.VMEM(start_state.shape, start_state.dtype),
        ),
        in_specs=[VMEM] * (len(tokens) + 4) + [HBM] * 2 + [VMEM],
        out_specs=(VMEM,) * 3,
        scratch_shapes=[
            pltpu.VMEM((local, slots, features), jnp.bfloat16),
            pltpu.SemaphoreType.DMA((2,)),
        ],
        input_output_aliases={len(tokens) + 6: 0},
        compiler_params=GRANT,
        cost_estimate=pl.CostEstimate(
            flops=4 * pairs * local * slots * features * units,
            bytes_accessed=6 * local * features * units,
            transcendentals=pairs * local * slots * units,
        ),
        name="far_hidden",
    )(*tokens, hots, coefs, gates, ups, in_hbm(w_down), in_hbm(start_state), hidden)


def down_kernel(core, start, hidden_ref, down_ref, _, out_ref):
    pairs, count, width = out_ref.shape
    local, units, _ = down_ref.shape
    columns = pl.ds(start, width)
    total = None
    for j in range(local):
        inner = pl.ds(j * units, units)
        parts = [hidden_ref[pl.ds((2 * p + core) * count, count), inner] for p in range(pairs)]
        term = jnp.dot(
            jnp.concatenate(parts, axis=0), down_ref[j, :, columns], preferred_element_type=jnp.float32
        )
        total = term if total is None else total + term
    for p in range(pairs):
        out_ref[p] = total[p * count : (p + 1) * count].astype(out_ref.dtype)


def down_rows(hidden, downs, order, send, count, start, width):
    pairs = hidden.shape[0] // (2 * count)
    return pl.pallas_call(
        functools.partial(down_kernel, int(send), start),
        out_shape=pltpu.VMEM((pairs, count, width), jnp.bfloat16 if send else jnp.float32),
        in_specs=[VMEM, VMEM, ANY],
        out_specs=VMEM,
        compiler_params=GRANT,
        cost_estimate=BRIEF,
        name="down_rows",
    )(hidden, downs, order)


def core_sum_kernel(chunks, keep, got, factor, _, *outs):
    pairs, _, width = keep.shape
    width = width // chunks
    step = factor[0:1, 0:1]
    for i in range(chunks):
        columns = pl.ds(i * width, width)
        for p in range(pairs):
            total = step * (keep[p, :, columns] + got[p, :, columns].astype(jnp.float32))
            if p == 0:
                outs[2 * i][...] = total
            else:
                outs[2 * i + 1][p - 1] = total.astype(jnp.bfloat16)


def core_sum(keep, got, factor, order, chunks):
    pairs, count, width = keep.shape
    shapes = []
    for _ in range(chunks):
        shapes.append(pltpu.VMEM((count, width // chunks), jnp.float32))
        shapes.append(pltpu.VMEM((pairs - 1, count, width // chunks), jnp.bfloat16))
    return pl.pallas_call(
        functools.partial(core_sum_kernel, chunks),
        out_shape=tuple(shapes),
        in_specs=[VMEM, VMEM, VMEM, ANY],
        out_specs=(VMEM,) * len(shapes),
        compiler_params=SMALL,
        cost_estimate=BRIEF,
        name="core_sum",
    )(keep, got, factor, order)


def wave_kernel(wave, window, backs, has_got, stride, lane, send, start, _, *refs):
    inputs = refs[: len(window) * (1 + backs) + has_got]
    outs = refs[len(refs) - 1 - send :]
    result, width = outs[-1], inputs[0].shape[1]
    for n, i in enumerate(window):

        @pl.when(lax.axis_index("tm") == wave - i)
        def _(i=i, own=inputs[n * (1 + backs)], more=inputs[n * (1 + backs) + 1 : (n + 1) * (1 + backs)]):
            total = own[...]
            for ref in more:
                total = total + ref[...].astype(jnp.float32)
            if has_got and wave > i:
                total = total + inputs[-1][...].astype(jnp.float32)
            if send:
                outs[0][...] = total.astype(jnp.bfloat16)
            columns = pl.ds((i * stride + lane) * width, width)
            result[:, columns] = start[:, columns] + total


def wave_step(wave, window, owns, backs, got, stride, lane, send, start, result, order):
    inputs = [start, order]
    for i in window:
        inputs += [owns[i], *backs[i]]
    inputs += ([] if got is None else [got]) + ([] if result is None else [result])
    shape = owns[window[0]].shape
    kernel = functools.partial(
        wave_kernel, wave, window, len(backs[window[0]]), int(got is not None), stride, lane, int(send)
    )
    return pl.pallas_call(
        kernel,
        out_shape=((pltpu.VMEM(shape, jnp.bfloat16),) if send else ()) + (pltpu.VMEM(start.shape, jnp.float32),),
        in_specs=[VMEM, ANY] + [VMEM] * (len(inputs) - 2),
        out_specs=(VMEM,) * (1 + send),
        input_output_aliases={} if result is None else {len(inputs) - 1: int(send)},
        compiler_params=SMALL,
        cost_estimate=BRIEF,
        name="wave_step",
    )(*inputs)


def write_kernel(result, out, sem):
    copy = pltpu.make_async_copy(result, out, sem)
    copy.start()
    copy.wait()


def write_out(result):
    return pl.pallas_call(
        write_kernel,
        out_shape=pltpu.HBM(result.shape, result.dtype),
        in_specs=[VMEM],
        out_specs=HBM,
        scratch_shapes=[pltpu.SemaphoreType.DMA],
        compiler_params=SMALL,
        cost_estimate=BRIEF,
        name="write_out",
    )(result)


def tie_kernel(value_ref, order_ref, out_ref):
    pass


def tie(value, order):
    return pl.pallas_call(
        tie_kernel,
        out_shape=jax.ShapeDtypeStruct(value.shape, value.dtype),
        in_specs=[ANY, ANY],
        out_specs=ANY,
        input_output_aliases={0: 0},
        compiler_params=SMALL,
        cost_estimate=BRIEF,
        name="tie",
    )(value, order)


def chain_pairs(senders, steps):
    first = senders[0]
    if len(senders) == 1 and first % 2 == 0 and steps % 2 == 0:
        return [(z, z ^ 1) for z in range(steps)]
    return [(z, (z + 1) % steps) for z in range(steps)]


def shards(tokens, route_ids, route_probs, step_size, start_state, w_gate, w_up, w_down):
    members = lax.axis_size("expert")
    steps = lax.axis_size("tm")
    tok_count, feature_count = tokens.shape[1:]
    topk_count = route_ids.shape[2]
    expert_total = w_gate.shape[0] * members
    capacity = 3 * tok_count * topk_count // (2 * expert_total)
    chips = members // 2

    def swapped(value):
        return lax.ppermute(value, "expert", [(i, i ^ 1) for i in range(members)])

    def shifted(value, by):
        return lax.ppermute(value, "expert", [(i, (i + 2 * by) % members) for i in range(members)])

    own = tokens[0]
    far_same = [shifted(own, by) for by in range(1, chips)]
    partner = swapped(own)
    table, own = make_table(route_ids, route_probs, tokens, expert_total)
    far_table = [shifted(table, by) for by in range(1, chips)]
    hidden, gates, ups = near_hidden([table, swapped(table)], [own, partner], w_gate, w_up, capacity, members)
    far_tables, far_tokens = [], []
    for value, piece in zip(far_table, far_same):
        value = tie(value, hidden)
        piece = tie(piece, value)
        far_tables += [value, swapped(value)]
        far_tokens += [piece, swapped(piece)]
    hots, coefs, factor = far_plan(far_tables, step_size, hidden, capacity, w_gate.shape[0])
    hidden, downs, start = far_hidden(far_tokens, hots, coefs, gates, ups, w_down, start_state, hidden)

    lanes, chunks = 2, 2
    parts = lanes * chunks
    width = feature_count // parts
    groups = [(0, 1), (1, parts - 1)]
    events, ready = [], 0.0
    for g, (_, count) in enumerate(groups):
        events.append((ready, "send", g, 0))
        events.append((ready + 0.9 * count, "keep", g, 0))
        ready += max(2.5, 1.8 * count)
        events.append((ready, "core", g, 0))
    for lane in range(lanes):
        ready = 10.0 + 3.0 * lane
        for wave in range(chunks + steps - 1):
            events.append((ready, "wave", lane, wave))
            ready += 6.0
    order, result = hidden, None
    gots, keeps, owns, backs, arrived = {}, {}, {}, {}, {}
    for _, kind, c, wave in sorted(events):
        if kind in ("send", "keep"):
            first, count = groups[c]
            part = down_rows(hidden, downs, order, kind == "send", tok_count, first * width, count * width)
            if kind == "send":
                gots[c] = swapped(part)
            else:
                keeps[c] = part
            order = part
        elif kind == "core":
            first, count = groups[c]
            sums = core_sum(keeps[c], gots[c], factor, order, count)
            for i in range(count):
                owns[first + i] = sums[2 * i]
                backs[first + i] = [shifted(sums[2 * i + 1][by - 1], -by) for by in range(1, chips)]
            order = sums[0]
        else:
            window = [i for i in range(chunks) if 0 <= wave - i < steps]
            lane_owns = {i: owns[i * lanes + c] for i in window}
            lane_backs = {i: backs[i * lanes + c] for i in window}
            send = wave < chunks + steps - 2
            *sent, result = wave_step(
                wave, window, lane_owns, lane_backs, arrived.get(c), lanes, c, send, start, result, order
            )
            order = sent[0] if send else order
            if send:
                senders = [z for z in range(steps - 1) if wave - z in window]
                arrived[c] = lax.ppermute(sent[0], "tm", chain_pairs(senders, steps))
    return write_out(result)[None]


def solution(mesh):
    return jax.shard_map(
        shards,
        mesh=mesh,
        in_specs=(
            P("tm", ("copies", "expert"), None),
            P("tm", ("copies", "expert"), None),
            P("tm", ("copies", "expert"), None),
            P(("copies", "tm")),
            P(("copies", "expert"), None),
            P("expert", None, None),
            P("expert", None, None),
            P("expert", None, None),
        ),
        out_specs=P("tm", ("copies", "expert"), None),
        check_vma=False,
    )
```

```python
import functools

import jax
import jax.numpy as jnp
from jax import lax
from jax.experimental import pallas as pl
from jax.experimental.pallas import tpu as pltpu
from jax.sharding import PartitionSpec as P

ANY = pl.BlockSpec(memory_space=pl.ANY)
HBM = pl.BlockSpec(memory_space=pltpu.HBM)
VMEM = pl.BlockSpec(memory_space=pltpu.VMEM)
GRANT = pltpu.CompilerParams(vmem_limit_bytes=7 * 1024 * 1024)
BRIEF = pl.CostEstimate(flops=0, bytes_accessed=0, transcendentals=0)
SMALL = pltpu.CompilerParams(vmem_limit_bytes=2 * 1024 * 1024)


def in_hbm(value):
    return pltpu.with_memory_space_constraint(value, pltpu.HBM)


def slots_of(capacity, blocks):
    return -(-capacity * blocks // 16) * 16


def table_kernel(experts, ids_hbm, probs_hbm, tokens_hbm, table, tokens, ids, probs, sems):
    copy = pltpu.make_async_copy(tokens_hbm.at[0], tokens, sems.at[0])
    smalls = [
        pltpu.make_async_copy(ids_hbm, ids, sems.at[1]),
        pltpu.make_async_copy(probs_hbm, probs, sems.at[2]),
    ]
    copy.start()
    for small in smalls:
        small.start()
    for small in smalls:
        small.wait()
    choices, _, count = ids.shape
    total = probs[0]
    for k in range(1, choices):
        total = total + probs[k]
    names = lax.broadcasted_iota(jnp.int32, table.shape, 0)
    value = jnp.zeros(table.shape, jnp.float32)
    for k in range(choices):
        value = value + jnp.where(ids[k] == names, probs[k] / total, 0.0)
    copy.wait()
    rows = tokens[...].astype(jnp.float32)
    scale = lax.rsqrt(jnp.mean(rows * rows, axis=1, keepdims=True) + 1e-06)
    scale = jnp.broadcast_to(scale, (count, 128)).T[:1]
    table[...] = jnp.where(names == experts, scale, value)


def make_table(ids, probs, tokens, experts):
    count, features = tokens.shape[1:]
    height = -(-(experts + 1) // 8) * 8
    ids, probs = jnp.transpose(ids, (2, 0, 1)), jnp.transpose(probs, (2, 0, 1))
    return pl.pallas_call(
        functools.partial(table_kernel, experts),
        out_shape=(
            pltpu.VMEM((height, count), jnp.float32),
            pltpu.VMEM((count, features), tokens.dtype),
        ),
        in_specs=[HBM] * 3,
        out_specs=(VMEM, VMEM),
        scratch_shapes=[
            pltpu.VMEM(ids.shape, ids.dtype),
            pltpu.VMEM(probs.shape, probs.dtype),
            pltpu.SemaphoreType.DMA((3,)),
        ],
        compiler_params=SMALL,
        name="make_table",
    )(in_hbm(ids), in_hbm(probs), in_hbm(tokens))


def plan(tables, capacity, hots, coefs):
    local, slots, width = hots.shape
    blocks = len(tables)
    count = width // blocks
    experts = local * lax.axis_size("expert")
    first = lax.axis_index("expert") * local
    before = lax.broadcasted_iota(jnp.int32, (count, count), 0)
    after = lax.broadcasted_iota(jnp.int32, (count, count), 1)
    upto = jnp.where(before <= after, 1.0, 0.0).astype(jnp.bfloat16)
    slot_ids = lax.broadcasted_iota(jnp.int32, (slots, width), 0).astype(jnp.float32)
    weights, scales, places = [], [], []
    for b in range(blocks):
        weight = tables[b][pl.ds(first, local), :]
        ones = jnp.where(weight > 0.0, 1.0, 0.0)
        padded = jnp.concatenate([ones, jnp.zeros((-local % 16, count), jnp.float32)], axis=0)
        rank = jnp.dot(padded.astype(jnp.bfloat16), upto, preferred_element_type=jnp.float32)[:local]
        places.append(jnp.where(weight > 0.0, rank + float(b * capacity - 1), -1.0))
        weights.append(weight)
        scales.append(tables[b][pl.ds(experts, 1), :])
    weight = jnp.concatenate(weights, axis=1) if blocks > 1 else weights[0]
    scale = jnp.concatenate(scales, axis=1) if blocks > 1 else scales[0]
    place = jnp.concatenate(places, axis=1) if blocks > 1 else places[0]
    for j in range(local):
        hit = slot_ids == place[j : j + 1, :]
        hots[j] = jnp.where(hit, 1.0, 0.0).astype(jnp.bfloat16)
        coefs[j, :, 0:1] = jnp.sum(jnp.where(hit, scale, 0.0), axis=1, keepdims=True)
        coefs[j, :, 1:2] = jnp.sum(jnp.where(hit, weight[j : j + 1, :], 0.0), axis=1, keepdims=True)


def pack(hots, tokens, rows):
    for j in range(hots.shape[0]):
        rows[j] = jnp.dot(hots[j], tokens, preferred_element_type=jnp.float32).astype(jnp.bfloat16)


def expert_hidden(j, rows, hots, coefs, gates, ups, out_ref, base):
    units = gates.shape[2]
    size = hots.shape[2]
    gate = jnp.dot(rows[j], gates[j], preferred_element_type=jnp.float32)
    up = jnp.dot(rows[j], ups[j], preferred_element_type=jnp.float32)
    scale = coefs[j, :, 0:1]
    weight = coefs[j, :, 1:2]
    g = gate * scale
    h = (g / (1.0 + jnp.exp(-g))) * (up * (scale * weight))
    placed = lax.dot_general(
        hots[j], h.astype(jnp.bfloat16), (((0,), (0,)), ((), ())), preferred_element_type=jnp.float32
    )
    out_ref[pl.ds(base, size), pl.ds(j * units, units)] = placed.astype(jnp.bfloat16)


def near_kernel(capacity, *refs):
    tables, tokens = refs[:2], refs[2:4]
    gate_hbm, up_hbm, hidden, gates, ups = refs[4:9]
    hots, coefs, rows, gate_sem, up_sem = refs[9:]
    local = gates.shape[0]
    copies = []
    for j in range(local):
        copies.append(pltpu.make_async_copy(gate_hbm.at[j], gates.at[j], gate_sem.at[j]))
        copies.append(pltpu.make_async_copy(up_hbm.at[j], ups.at[j], up_sem.at[j]))
    for copy in copies:
        copy.start()
    plan(tables, capacity, hots, coefs)
    pack(hots, jnp.concatenate([t[...] for t in tokens], axis=0), rows)
    for j in range(local):
        copies[2 * j].wait()
        copies[2 * j + 1].wait()
        expert_hidden(j, rows, hots, coefs, gates, ups, hidden, 0)


def near_hidden(tables, tokens, w_gate, w_up, capacity, blocks):
    count, features = tokens[0].shape
    local, _, units = w_gate.shape
    slots = slots_of(capacity, 2)
    return pl.pallas_call(
        functools.partial(near_kernel, capacity),
        out_shape=(
            pltpu.VMEM((blocks * count, local * units), jnp.bfloat16),
            pltpu.VMEM(w_gate.shape, w_gate.dtype),
            pltpu.VMEM(w_up.shape, w_up.dtype),
        ),
        in_specs=[VMEM] * 4 + [HBM] * 2,
        out_specs=(VMEM,) * 3,
        scratch_shapes=[
            pltpu.VMEM((local, slots, 2 * count), jnp.bfloat16),
            pltpu.VMEM((local, slots, 128), jnp.float32),
            pltpu.VMEM((local, slots, features), jnp.bfloat16),
            pltpu.SemaphoreType.DMA((local,)),
            pltpu.SemaphoreType.DMA((local,)),
        ],
        compiler_params=GRANT,
        cost_estimate=pl.CostEstimate(
            flops=4 * local * slots * features * units,
            bytes_accessed=4 * local * features * units,
            transcendentals=local * slots * units,
        ),
        name="near_hidden",
    )(*tables, *tokens, in_hbm(w_gate), in_hbm(w_up))


def far_plan_kernel(capacity, far_count, *refs):
    tables = refs[:far_count]
    step, _, hots, coefs, factor = refs[far_count:]
    factor[...] = jnp.full(factor.shape, step[0])
    for p in range(far_count // 2):
        plan(tables[2 * p : 2 * p + 2], capacity, hots.at[p], coefs.at[p])


def far_plan(tables, step_size, order, capacity, local):
    pairs = len(tables) // 2
    count = tables[0].shape[1]
    slots = slots_of(capacity, 2)
    return pl.pallas_call(
        functools.partial(far_plan_kernel, capacity, len(tables)),
        out_shape=(
            pltpu.VMEM((pairs, local, slots, 2 * count), jnp.bfloat16),
            pltpu.VMEM((pairs, local, slots, 128), jnp.float32),
            pltpu.VMEM((8, 128), jnp.float32),
        ),
        in_specs=[VMEM] * len(tables) + [pl.BlockSpec(memory_space=pltpu.SMEM), ANY],
        out_specs=(VMEM,) * 3,
        compiler_params=SMALL,
        cost_estimate=BRIEF,
        name="far_plan",
    )(*tables, step_size, order)


def far_kernel(far_count, *refs):
    tokens = refs[:far_count]
    hots, coefs, gates, ups, down_hbm, start_hbm, _, hidden, downs, start, rows, sems = refs[far_count:]
    copies = [
        pltpu.make_async_copy(down_hbm, downs, sems.at[0]),
        pltpu.make_async_copy(start_hbm, start, sems.at[1]),
    ]
    for copy in copies:
        copy.start()
    for p in range(far_count // 2):
        both = jnp.concatenate([tokens[2 * p][...], tokens[2 * p + 1][...]], axis=0)
        pack(hots.at[p], both, rows)
        for j in range(gates.shape[0]):
            expert_hidden(j, rows, hots.at[p], coefs.at[p], gates, ups, hidden, (p + 1) * hots.shape[3])
    for copy in copies:
        copy.wait()


def far_hidden(tokens, hots, coefs, gates, ups, w_down, start_state, hidden):
    pairs, local, slots, size = hots.shape
    features, units = gates.shape[1:]
    return pl.pallas_call(
        functools.partial(far_kernel, len(tokens)),
        out_shape=(
            pltpu.VMEM(hidden.shape, hidden.dtype),
            pltpu.VMEM(w_down.shape, w_down.dtype),
            pltpu.VMEM(start_state.shape, start_state.dtype),
        ),
        in_specs=[VMEM] * (len(tokens) + 4) + [HBM] * 2 + [VMEM],
        out_specs=(VMEM,) * 3,
        scratch_shapes=[
            pltpu.VMEM((local, slots, features), jnp.bfloat16),
            pltpu.SemaphoreType.DMA((2,)),
        ],
        input_output_aliases={len(tokens) + 6: 0},
        compiler_params=GRANT,
        cost_estimate=pl.CostEstimate(
            flops=4 * pairs * local * slots * features * units,
            bytes_accessed=6 * local * features * units,
            transcendentals=pairs * local * slots * units,
        ),
        name="far_hidden",
    )(*tokens, hots, coefs, gates, ups, in_hbm(w_down), in_hbm(start_state), hidden)


def down_kernel(core, start, hidden_ref, down_ref, _, out_ref):
    pairs, count, width = out_ref.shape
    local, units, _ = down_ref.shape
    columns = pl.ds(start, width)
    total = None
    for j in range(local):
        inner = pl.ds(j * units, units)
        parts = [hidden_ref[pl.ds((2 * p + core) * count, count), inner] for p in range(pairs)]
        term = jnp.dot(
            jnp.concatenate(parts, axis=0), down_ref[j, :, columns], preferred_element_type=jnp.float32
        )
        total = term if total is None else total + term
    for p in range(pairs):
        out_ref[p] = total[p * count : (p + 1) * count].astype(out_ref.dtype)


def down_rows(hidden, downs, order, send, count, start, width):
    pairs = hidden.shape[0] // (2 * count)
    return pl.pallas_call(
        functools.partial(down_kernel, int(send), start),
        out_shape=pltpu.VMEM((pairs, count, width), jnp.bfloat16 if send else jnp.float32),
        in_specs=[VMEM, VMEM, ANY],
        out_specs=VMEM,
        compiler_params=GRANT,
        cost_estimate=BRIEF,
        name="down_rows",
    )(hidden, downs, order)


def core_sum_kernel(chunks, keep, got, factor, _, *outs):
    pairs, _, width = keep.shape
    width = width // chunks
    step = factor[0:1, 0:1]
    for i in range(chunks):
        columns = pl.ds(i * width, width)
        for p in range(pairs):
            total = step * (keep[p, :, columns] + got[p, :, columns].astype(jnp.float32))
            if p == 0:
                outs[2 * i][...] = total
            else:
                outs[2 * i + 1][p - 1] = total.astype(jnp.bfloat16)


def core_sum(keep, got, factor, order, chunks):
    pairs, count, width = keep.shape
    shapes = []
    for _ in range(chunks):
        shapes.append(pltpu.VMEM((count, width // chunks), jnp.float32))
        shapes.append(pltpu.VMEM((pairs - 1, count, width // chunks), jnp.bfloat16))
    return pl.pallas_call(
        functools.partial(core_sum_kernel, chunks),
        out_shape=tuple(shapes),
        in_specs=[VMEM, VMEM, VMEM, ANY],
        out_specs=(VMEM,) * len(shapes),
        compiler_params=SMALL,
        cost_estimate=BRIEF,
        name="core_sum",
    )(keep, got, factor, order)


def chain_kernel(hop, backs, first, send, start, _, own, *refs):
    outs = refs[len(refs) - 1 - send :]
    result, width = outs[-1], own.shape[1]

    @pl.when(lax.axis_index("tm") == hop)
    def _():
        total = own[...]
        for ref in refs[: backs + (hop > 0)]:
            total = total + ref[...].astype(jnp.float32)
        if send:
            outs[0][...] = total.astype(jnp.bfloat16)
        columns = pl.ds(first, width)
        result[:, columns] = start[:, columns] + total


def chain_step(hop, own, backs, got, first, send, start, result, order):
    inputs = [start, order, own, *backs] + ([] if got is None else [got]) + ([] if result is None else [result])
    return pl.pallas_call(
        functools.partial(chain_kernel, hop, len(backs), first, int(send)),
        out_shape=((pltpu.VMEM(own.shape, jnp.bfloat16),) if send else ())
        + (pltpu.VMEM(start.shape, jnp.float32),),
        in_specs=[VMEM, ANY] + [VMEM] * (len(inputs) - 2),
        out_specs=(VMEM,) * (1 + send),
        input_output_aliases={} if result is None else {len(inputs) - 1: int(send)},
        compiler_params=SMALL,
        cost_estimate=BRIEF,
        name="chain_step",
    )(*inputs)


def write_kernel(result, out, sem):
    copy = pltpu.make_async_copy(result, out, sem)
    copy.start()
    copy.wait()


def write_out(result):
    return pl.pallas_call(
        write_kernel,
        out_shape=pltpu.HBM(result.shape, result.dtype),
        in_specs=[VMEM],
        out_specs=HBM,
        scratch_shapes=[pltpu.SemaphoreType.DMA],
        compiler_params=SMALL,
        cost_estimate=BRIEF,
        name="write_out",
    )(result)


def tie_kernel(value_ref, order_ref, out_ref):
    pass


def tie(value, order):
    return pl.pallas_call(
        tie_kernel,
        out_shape=jax.ShapeDtypeStruct(value.shape, value.dtype),
        in_specs=[ANY, ANY],
        out_specs=ANY,
        input_output_aliases={0: 0},
        compiler_params=SMALL,
        cost_estimate=BRIEF,
        name="tie",
    )(value, order)


def exchange(value, low, members, steps):
    pairs = []
    for e in range(members):
        for z in range(steps):
            if z in (low, low + 1):
                pairs.append((e * steps + z, e * steps + 2 * low + 1 - z))
            else:
                pairs.append((e * steps + z, (e ^ 1) * steps + z))
    return lax.ppermute(value, ("expert", "tm"), pairs)


def shards(tokens, route_ids, route_probs, step_size, start_state, w_gate, w_up, w_down):
    members = lax.axis_size("expert")
    steps = lax.axis_size("tm")
    tok_count, feature_count = tokens.shape[1:]
    topk_count = route_ids.shape[2]
    expert_total = w_gate.shape[0] * members
    capacity = 3 * tok_count * topk_count // (2 * expert_total)
    chips = members // 2

    def swapped(value):
        return lax.ppermute(value, "expert", [(i, i ^ 1) for i in range(members)])

    def shifted(value, by):
        return lax.ppermute(value, "expert", [(i, (i + 2 * by) % members) for i in range(members)])

    own = tokens[0]
    far_same = [shifted(own, by) for by in range(1, chips)]
    partner = swapped(own)
    table, own = make_table(route_ids, route_probs, tokens, expert_total)
    far_table = [shifted(table, by) for by in range(1, chips)]
    hidden, gates, ups = near_hidden([table, swapped(table)], [own, partner], w_gate, w_up, capacity, members)
    far_tables, far_tokens = [], []
    for value, piece in zip(far_table, far_same):
        value = tie(value, hidden)
        piece = tie(piece, value)
        far_tables += [value, swapped(value)]
        far_tokens += [piece, swapped(piece)]
    hots, coefs, factor = far_plan(far_tables, step_size, hidden, capacity, w_gate.shape[0])
    hidden, downs, start = far_hidden(far_tokens, hots, coefs, gates, ups, w_down, start_state, hidden)

    parts = 4
    width = feature_count // parts
    groups = [(0, 1), (1, parts - 1)]
    events, ready = [], 0.0
    for g, (_, count) in enumerate(groups):
        events.append((ready, "send", g, 0))
        events.append((ready + 0.9 * count, "keep", g, 0))
        ready += max(2.5, 1.8 * count)
        events.append((ready, "core", g, 0))
    for c in range(parts):
        for hop in range(steps):
            events.append((12.0 + 3.3 * c + 5.0 * hop, "chain", c, hop))
    order, result = hidden, None
    gots, keeps, owns, backs, arrived = {}, {}, {}, {}, {}
    for _, kind, c, hop in sorted(events):
        if kind in ("send", "keep"):
            first, count = groups[c]
            part = down_rows(hidden, downs, order, kind == "send", tok_count, first * width, count * width)
            if kind == "send":
                gots[c] = swapped(part)
            else:
                keeps[c] = part
            order = part
        elif kind == "core":
            first, count = groups[c]
            sums = core_sum(keeps[c], gots[c], factor, order, count)
            for i in range(count):
                owns[first + i] = sums[2 * i]
                backs[first + i] = [shifted(sums[2 * i + 1][by - 1], -by) for by in range(1, chips)]
            order = sums[0]
        else:
            send = hop < steps - 1
            *sent, result = chain_step(
                hop, owns[c], backs[c], arrived.get(c), c * width, send, start, result, order
            )
            if send:
                order = sent[0]
                arrived[c] = exchange(sent[0], hop, members, steps)
    return write_out(result)[None]


def solution(mesh):
    return jax.shard_map(
        shards,
        mesh=mesh,
        in_specs=(
            P("tm", ("copies", "expert"), None),
            P("tm", ("copies", "expert"), None),
            P("tm", ("copies", "expert"), None),
            P(("copies", "tm")),
            P(("copies", "expert"), None),
            P("expert", None, None),
            P("expert", None, None),
            P("expert", None, None),
        ),
        out_specs=P("tm", ("copies", "expert"), None),
        check_vma=False,
    )
```

```python
import functools

import jax
import jax.numpy as jnp
from jax import lax
from jax.experimental import pallas as pl
from jax.experimental.pallas import tpu as pltpu
from jax.sharding import PartitionSpec as P

ANY = pl.BlockSpec(memory_space=pl.ANY)
HBM = pl.BlockSpec(memory_space=pltpu.HBM)
VMEM = pl.BlockSpec(memory_space=pltpu.VMEM)
GRANT = pltpu.CompilerParams(vmem_limit_bytes=7 * 1024 * 1024)
BRIEF = pl.CostEstimate(flops=0, bytes_accessed=0, transcendentals=0)
SMALL = pltpu.CompilerParams(vmem_limit_bytes=2 * 1024 * 1024)


SHARES = (4, 4, 4, 4)
GROUPS = ((0,), (1,), (2,), (3,))


def in_hbm(value):
    return pltpu.with_memory_space_constraint(value, pltpu.HBM)


def slots_of(capacity, blocks):
    return -(-capacity * blocks // 16) * 16


def table_kernel(experts, ids_hbm, probs_hbm, tokens_hbm, table, tokens, ids, probs, sems):
    copy = pltpu.make_async_copy(tokens_hbm.at[0], tokens, sems.at[0])
    smalls = [
        pltpu.make_async_copy(ids_hbm, ids, sems.at[1]),
        pltpu.make_async_copy(probs_hbm, probs, sems.at[2]),
    ]
    copy.start()
    for small in smalls:
        small.start()
    for small in smalls:
        small.wait()
    choices, _, count = ids.shape
    total = probs[0]
    for k in range(1, choices):
        total = total + probs[k]
    names = lax.broadcasted_iota(jnp.int32, table.shape, 0)
    value = jnp.zeros(table.shape, jnp.float32)
    for k in range(choices):
        value = value + jnp.where(ids[k] == names, probs[k] / total, 0.0)
    copy.wait()
    rows = tokens[...].astype(jnp.float32)
    scale = lax.rsqrt(jnp.mean(rows * rows, axis=1, keepdims=True) + 1e-06)
    scale = jnp.broadcast_to(scale, (count, 128)).T[:1]
    table[...] = jnp.where(names == experts, scale, value)


def make_table(ids, probs, tokens, experts):
    count, features = tokens.shape[1:]
    height = -(-(experts + 1) // 8) * 8
    ids, probs = jnp.transpose(ids, (2, 0, 1)), jnp.transpose(probs, (2, 0, 1))
    return pl.pallas_call(
        functools.partial(table_kernel, experts),
        out_shape=(
            pltpu.VMEM((height, count), jnp.float32),
            pltpu.VMEM((count, features), tokens.dtype),
        ),
        in_specs=[HBM] * 3,
        out_specs=(VMEM, VMEM),
        scratch_shapes=[
            pltpu.VMEM(ids.shape, ids.dtype),
            pltpu.VMEM(probs.shape, probs.dtype),
            pltpu.SemaphoreType.DMA((3,)),
        ],
        compiler_params=SMALL,
        name="make_table",
    )(in_hbm(ids), in_hbm(probs), in_hbm(tokens))


def plan(tables, capacity, hots, coefs):
    local, slots, width = hots.shape
    blocks = len(tables)
    count = width // blocks
    experts = local * lax.axis_size("expert")
    first = lax.axis_index("expert") * local
    before = lax.broadcasted_iota(jnp.int32, (count, count), 0)
    after = lax.broadcasted_iota(jnp.int32, (count, count), 1)
    upto = jnp.where(before <= after, 1.0, 0.0).astype(jnp.bfloat16)
    slot_ids = lax.broadcasted_iota(jnp.int32, (slots, width), 0).astype(jnp.float32)
    weights, scales, places = [], [], []
    for b in range(blocks):
        weight = tables[b][pl.ds(first, local), :]
        ones = jnp.where(weight > 0.0, 1.0, 0.0)
        padded = jnp.concatenate([ones, jnp.zeros((-local % 16, count), jnp.float32)], axis=0)
        rank = jnp.dot(padded.astype(jnp.bfloat16), upto, preferred_element_type=jnp.float32)[:local]
        places.append(jnp.where(weight > 0.0, rank + float(b * capacity - 1), -1.0))
        weights.append(weight)
        scales.append(tables[b][pl.ds(experts, 1), :])
    weight = jnp.concatenate(weights, axis=1) if blocks > 1 else weights[0]
    scale = jnp.concatenate(scales, axis=1) if blocks > 1 else scales[0]
    place = jnp.concatenate(places, axis=1) if blocks > 1 else places[0]
    for j in range(local):
        hit = slot_ids == place[j : j + 1, :]
        hots[j] = jnp.where(hit, 1.0, 0.0).astype(jnp.bfloat16)
        coefs[j, :, 0:1] = jnp.sum(jnp.where(hit, scale, 0.0), axis=1, keepdims=True)
        coefs[j, :, 1:2] = jnp.sum(jnp.where(hit, weight[j : j + 1, :], 0.0), axis=1, keepdims=True)


def pack(hots, tokens, rows):
    for j in range(hots.shape[0]):
        rows[j] = jnp.dot(hots[j], tokens, preferred_element_type=jnp.float32).astype(jnp.bfloat16)


def expert_hidden(j, rows, hots, coefs, gates, ups, out_ref, base):
    units = gates.shape[2]
    size = hots.shape[2]
    gate = jnp.dot(rows[j], gates[j], preferred_element_type=jnp.float32)
    up = jnp.dot(rows[j], ups[j], preferred_element_type=jnp.float32)
    scale = coefs[j, :, 0:1]
    weight = coefs[j, :, 1:2]
    g = gate * scale
    h = (g / (1.0 + jnp.exp(-g))) * (up * (scale * weight))
    placed = lax.dot_general(
        hots[j], h.astype(jnp.bfloat16), (((0,), (0,)), ((), ())), preferred_element_type=jnp.float32
    )
    out_ref[pl.ds(base, size), pl.ds(j * units, units)] = placed.astype(jnp.bfloat16)


def near_kernel(capacity, *refs):
    tables, tokens = refs[:2], refs[2:4]
    gate_hbm, up_hbm, hidden, gates, ups = refs[4:9]
    hots, coefs, rows, gate_sem, up_sem = refs[9:]
    local = gates.shape[0]
    copies = []
    for j in range(local):
        copies.append(pltpu.make_async_copy(gate_hbm.at[j], gates.at[j], gate_sem.at[j]))
        copies.append(pltpu.make_async_copy(up_hbm.at[j], ups.at[j], up_sem.at[j]))
    for copy in copies:
        copy.start()
    plan(tables, capacity, hots, coefs)
    pack(hots, jnp.concatenate([t[...] for t in tokens], axis=0), rows)
    for j in range(local):
        copies[2 * j].wait()
        copies[2 * j + 1].wait()
        expert_hidden(j, rows, hots, coefs, gates, ups, hidden, 0)


def near_hidden(tables, tokens, w_gate, w_up, capacity, blocks):
    count, features = tokens[0].shape
    local, _, units = w_gate.shape
    slots = slots_of(capacity, 2)
    return pl.pallas_call(
        functools.partial(near_kernel, capacity),
        out_shape=(
            pltpu.VMEM((blocks * count, local * units), jnp.bfloat16),
            pltpu.VMEM(w_gate.shape, w_gate.dtype),
            pltpu.VMEM(w_up.shape, w_up.dtype),
        ),
        in_specs=[VMEM] * 4 + [HBM] * 2,
        out_specs=(VMEM,) * 3,
        scratch_shapes=[
            pltpu.VMEM((local, slots, 2 * count), jnp.bfloat16),
            pltpu.VMEM((local, slots, 128), jnp.float32),
            pltpu.VMEM((local, slots, features), jnp.bfloat16),
            pltpu.SemaphoreType.DMA((local,)),
            pltpu.SemaphoreType.DMA((local,)),
        ],
        compiler_params=GRANT,
        cost_estimate=pl.CostEstimate(
            flops=4 * local * slots * features * units,
            bytes_accessed=4 * local * features * units,
            transcendentals=local * slots * units,
        ),
        name="near_hidden",
    )(*tables, *tokens, in_hbm(w_gate), in_hbm(w_up))


def far_plan_kernel(capacity, far_count, *refs):
    tables = refs[:far_count]
    step, _, hots, coefs, factor = refs[far_count:]
    factor[...] = jnp.full(factor.shape, step[0])
    for p in range(far_count // 2):
        plan(tables[2 * p : 2 * p + 2], capacity, hots.at[p], coefs.at[p])


def far_plan(tables, step_size, order, capacity, local):
    pairs = len(tables) // 2
    count = tables[0].shape[1]
    slots = slots_of(capacity, 2)
    return pl.pallas_call(
        functools.partial(far_plan_kernel, capacity, len(tables)),
        out_shape=(
            pltpu.VMEM((pairs, local, slots, 2 * count), jnp.bfloat16),
            pltpu.VMEM((pairs, local, slots, 128), jnp.float32),
            pltpu.VMEM((8, 128), jnp.float32),
        ),
        in_specs=[VMEM] * len(tables) + [pl.BlockSpec(memory_space=pltpu.SMEM), ANY],
        out_specs=(VMEM,) * 3,
        compiler_params=SMALL,
        cost_estimate=BRIEF,
        name="far_plan",
    )(*tables, step_size, order)


def far_kernel(far_count, *refs):
    tokens = refs[:far_count]
    hots, coefs, gates, ups, down_hbm, start_hbm, _, hidden, downs, start, rows, sems = refs[far_count:]
    copies = [
        pltpu.make_async_copy(down_hbm, downs, sems.at[0]),
        pltpu.make_async_copy(start_hbm, start, sems.at[1]),
    ]
    for copy in copies:
        copy.start()
    for p in range(far_count // 2):
        both = jnp.concatenate([tokens[2 * p][...], tokens[2 * p + 1][...]], axis=0)
        pack(hots.at[p], both, rows)
        for j in range(gates.shape[0]):
            expert_hidden(j, rows, hots.at[p], coefs.at[p], gates, ups, hidden, (p + 1) * hots.shape[3])
    for copy in copies:
        copy.wait()


def far_hidden(tokens, hots, coefs, gates, ups, w_down, start_state, hidden):
    pairs, local, slots, size = hots.shape
    features, units = gates.shape[1:]
    return pl.pallas_call(
        functools.partial(far_kernel, len(tokens)),
        out_shape=(
            pltpu.VMEM(hidden.shape, hidden.dtype),
            pltpu.VMEM(w_down.shape, w_down.dtype),
            pltpu.VMEM(start_state.shape, start_state.dtype),
        ),
        in_specs=[VMEM] * (len(tokens) + 4) + [HBM] * 2 + [VMEM],
        out_specs=(VMEM,) * 3,
        scratch_shapes=[
            pltpu.VMEM((local, slots, features), jnp.bfloat16),
            pltpu.SemaphoreType.DMA((2,)),
        ],
        input_output_aliases={len(tokens) + 6: 0},
        compiler_params=GRANT,
        cost_estimate=pl.CostEstimate(
            flops=4 * pairs * local * slots * features * units,
            bytes_accessed=6 * local * features * units,
            transcendentals=pairs * local * slots * units,
        ),
        name="far_hidden",
    )(*tokens, hots, coefs, gates, ups, in_hbm(w_down), in_hbm(start_state), hidden)


def down_kernel(core, start, hidden_ref, down_ref, _, *outs):
    count, width = outs[0].shape[1:]
    pairs = sum(ref.shape[0] for ref in outs)
    local, units, _ = down_ref.shape
    columns = pl.ds(start, width)
    total = None
    for j in range(local):
        inner = pl.ds(j * units, units)
        parts = [hidden_ref[pl.ds((2 * p + core) * count, count), inner] for p in range(pairs)]
        term = jnp.dot(
            jnp.concatenate(parts, axis=0), down_ref[j, :, columns], preferred_element_type=jnp.float32
        )
        total = term if total is None else total + term
    rows = [total[p * count : (p + 1) * count] for p in range(pairs)]
    for ref in outs:
        for p in range(ref.shape[0]):
            ref[p] = rows.pop(0).astype(ref.dtype)


def down_rows(hidden, downs, order, send, count, start, width):
    pairs = hidden.shape[0] // (2 * count)
    dtype = jnp.bfloat16 if send else jnp.float32
    return pl.pallas_call(
        functools.partial(down_kernel, int(send), start),
        out_shape=(pltpu.VMEM((1, count, width), dtype), pltpu.VMEM((pairs - 1, count, width), dtype)),
        in_specs=[VMEM, VMEM, ANY],
        out_specs=(VMEM, VMEM),
        compiler_params=GRANT,
        cost_estimate=BRIEF,
        name="down_rows",
    )(hidden, downs, order)


def core_sum_kernel(widths, near_keep, far_keep, near_got, far_got, factor, _, *outs):
    step = factor[0:1, 0:1]
    first = 0
    for n, width in enumerate(widths):
        columns = pl.ds(first, width)
        first += width
        outs[2 * n][...] = step * (near_keep[0, :, columns] + near_got[0, :, columns].astype(jnp.float32))
        for p in range(far_keep.shape[0]):
            total = step * (far_keep[p, :, columns] + far_got[p, :, columns].astype(jnp.float32))
            outs[2 * n + 1][p] = total.astype(jnp.bfloat16)


def core_sum(keeps, gots, factor, order, widths):
    others, count, _ = keeps[1].shape
    shapes = []
    for width in widths:
        shapes.append(pltpu.VMEM((count, width), jnp.float32))
        shapes.append(pltpu.VMEM((others, count, width), jnp.bfloat16))
    return pl.pallas_call(
        functools.partial(core_sum_kernel, widths),
        out_shape=tuple(shapes),
        in_specs=[VMEM] * 5 + [ANY],
        out_specs=(VMEM,) * len(shapes),
        compiler_params=SMALL,
        cost_estimate=BRIEF,
        name="core_sum",
    )(*keeps, *gots, factor, order)


def chain_kernel(hop, backs, first, send, start, _, own, *refs):
    outs = refs[len(refs) - 1 - send :]
    result, width = outs[-1], own.shape[1]

    @pl.when(lax.axis_index("tm") == hop)
    def _():
        total = own[...]
        for ref in refs[: backs + (hop > 0)]:
            total = total + ref[...].astype(jnp.float32)
        if send:
            outs[0][...] = total.astype(jnp.bfloat16)
        columns = pl.ds(first, width)
        result[:, columns] = start[:, columns] + total


def chain_step(hop, own, backs, got, first, send, start, result, order):
    inputs = [start, order, own, *backs] + ([] if got is None else [got]) + ([] if result is None else [result])
    return pl.pallas_call(
        functools.partial(chain_kernel, hop, len(backs), first, int(send)),
        out_shape=((pltpu.VMEM(own.shape, jnp.bfloat16),) if send else ())
        + (pltpu.VMEM(start.shape, jnp.float32),),
        in_specs=[VMEM, ANY] + [VMEM] * (len(inputs) - 2),
        out_specs=(VMEM,) * (1 + send),
        input_output_aliases={} if result is None else {len(inputs) - 1: int(send)},
        compiler_params=SMALL,
        cost_estimate=BRIEF,
        name="chain_step",
    )(*inputs)


def write_kernel(result, out, sem):
    copy = pltpu.make_async_copy(result, out, sem)
    copy.start()
    copy.wait()


def write_out(result):
    return pl.pallas_call(
        write_kernel,
        out_shape=pltpu.HBM(result.shape, result.dtype),
        in_specs=[VMEM],
        out_specs=HBM,
        scratch_shapes=[pltpu.SemaphoreType.DMA],
        compiler_params=SMALL,
        cost_estimate=BRIEF,
        name="write_out",
    )(result)


def tie_kernel(value_ref, order_ref, out_ref):
    pass


def tie(value, order):
    return pl.pallas_call(
        tie_kernel,
        out_shape=jax.ShapeDtypeStruct(value.shape, value.dtype),
        in_specs=[ANY, ANY],
        out_specs=ANY,
        input_output_aliases={0: 0},
        compiler_params=SMALL,
        cost_estimate=BRIEF,
        name="tie",
    )(value, order)


def exchange(value, low, members, steps):
    pairs = []
    for e in range(members):
        for z in range(steps):
            if z in (low, low + 1):
                pairs.append((e * steps + z, e * steps + 2 * low + 1 - z))
            else:
                pairs.append((e * steps + z, (e ^ 1) * steps + z))
    return lax.ppermute(value, ("expert", "tm"), pairs)


def shards(tokens, route_ids, route_probs, step_size, start_state, w_gate, w_up, w_down):
    members = lax.axis_size("expert")
    steps = lax.axis_size("tm")
    tok_count, feature_count = tokens.shape[1:]
    topk_count = route_ids.shape[2]
    expert_total = w_gate.shape[0] * members
    capacity = 3 * tok_count * topk_count // (2 * expert_total)
    chips = members // 2

    def swapped(value):
        return lax.ppermute(value, "expert", [(i, i ^ 1) for i in range(members)])

    def shifted(value, by):
        return lax.ppermute(value, "expert", [(i, (i + 2 * by) % members) for i in range(members)])

    own = tokens[0]
    far_same = [shifted(own, by) for by in range(1, chips)]
    partner = swapped(own)
    table, own = make_table(route_ids, route_probs, tokens, expert_total)
    far_table = [shifted(table, by) for by in range(1, chips)]
    hidden, gates, ups = near_hidden([table, swapped(table)], [own, partner], w_gate, w_up, capacity, members)
    far_tables, far_tokens = [], []
    for value, piece in zip(far_table, far_same):
        value = tie(value, hidden)
        piece = tie(piece, value)
        far_tables += [value, swapped(value)]
        far_tokens += [piece, swapped(piece)]
    hots, coefs, factor = far_plan(far_tables, step_size, hidden, capacity, w_gate.shape[0])
    hidden, downs, start = far_hidden(far_tokens, hots, coefs, gates, ups, w_down, start_state, hidden)

    widths = [feature_count * share // 16 for share in SHARES]
    parts = len(widths)
    firsts = [sum(widths[:c]) for c in range(parts)]
    events, ready = [], 0.0
    for g, group in enumerate(GROUPS):
        share = sum(SHARES[c] for c in group) / 4
        events.append((ready, "send", g, 0))
        events.append((ready + 0.9 * share, "keep", g, 0))
        ready += 2.5 if g == 0 else 1.8 * share
        events.append((2.5, 10.05, 10.1, 13.35)[g] if g < 4 else ready + 8.0)
        events[-1] = (events[-1], "core", g, 0)
    for c in range(parts):
        for hop in range(steps):
            events.append((10.0 + 3.3 * c + 5.0 * hop, "chain", c, hop))
    order, result = hidden, None
    gots, keeps, owns, backs, arrived = {}, {}, {}, {}, {}
    for _, kind, c, hop in sorted(events):
        if kind in ("send", "keep"):
            group = GROUPS[c]
            width = sum(widths[i] for i in group)
            part = down_rows(hidden, downs, order, kind == "send", tok_count, firsts[group[0]], width)
            if kind == "send":
                gots[c] = [swapped(piece) for piece in reversed(part)][::-1]
            else:
                keeps[c] = part
            order = part[0]
        elif kind == "core":
            group = GROUPS[c]
            sums = core_sum(keeps[c], gots[c], factor, order, [widths[i] for i in group])
            for n, i in enumerate(group):
                owns[i] = sums[2 * n]
                backs[i] = [shifted(sums[2 * n + 1][by - 1], -by) for by in range(1, chips)]
            order = sums[0]
        else:
            send = hop < steps - 1
            *sent, result = chain_step(
                hop, owns[c], backs[c], arrived.get(c), firsts[c], send, start, result, order
            )
            if send:
                order = sent[0]
                arrived[c] = exchange(sent[0], hop, members, steps)
    return write_out(result)[None]


def solution(mesh):
    return jax.shard_map(
        shards,
        mesh=mesh,
        in_specs=(
            P("tm", ("copies", "expert"), None),
            P("tm", ("copies", "expert"), None),
            P("tm", ("copies", "expert"), None),
            P(("copies", "tm")),
            P(("copies", "expert"), None),
            P("expert", None, None),
            P("expert", None, None),
            P("expert", None, None),
        ),
        out_specs=P("tm", ("copies", "expert"), None),
        check_vma=False,
    )
```

```python
import functools

import jax
import jax.numpy as jnp
from jax import lax
from jax.experimental import pallas as pl
from jax.experimental.pallas import tpu as pltpu
from jax.sharding import PartitionSpec as P

ANY = pl.BlockSpec(memory_space=pl.ANY)
HBM = pl.BlockSpec(memory_space=pltpu.HBM)
VMEM = pl.BlockSpec(memory_space=pltpu.VMEM)
GRANT = pltpu.CompilerParams(vmem_limit_bytes=7 * 1024 * 1024)
BRIEF = pl.CostEstimate(flops=0, bytes_accessed=0, transcendentals=0)
SMALL = pltpu.CompilerParams(vmem_limit_bytes=2 * 1024 * 1024)


SHARES = (5, 4, 4, 3)
GROUPS = ((0,), (1,), (2,), (3,))


def in_hbm(value):
    return pltpu.with_memory_space_constraint(value, pltpu.HBM)


def slots_of(capacity, blocks):
    return -(-capacity * blocks // 16) * 16


def table_kernel(experts, ids_hbm, probs_hbm, tokens_hbm, table, tokens, ids, probs, sems):
    copy = pltpu.make_async_copy(tokens_hbm.at[0], tokens, sems.at[0])
    smalls = [
        pltpu.make_async_copy(ids_hbm, ids, sems.at[1]),
        pltpu.make_async_copy(probs_hbm, probs, sems.at[2]),
    ]
    copy.start()
    for small in smalls:
        small.start()
    for small in smalls:
        small.wait()
    choices, _, count = ids.shape
    total = probs[0]
    for k in range(1, choices):
        total = total + probs[k]
    names = lax.broadcasted_iota(jnp.int32, table.shape, 0)
    value = jnp.zeros(table.shape, jnp.float32)
    for k in range(choices):
        value = value + jnp.where(ids[k] == names, probs[k] / total, 0.0)
    copy.wait()
    rows = tokens[...].astype(jnp.float32)
    scale = lax.rsqrt(jnp.mean(rows * rows, axis=1, keepdims=True) + 1e-06)
    scale = jnp.broadcast_to(scale, (count, 128)).T[:1]
    table[...] = jnp.where(names == experts, scale, value)


def make_table(ids, probs, tokens, experts):
    count, features = tokens.shape[1:]
    height = -(-(experts + 1) // 8) * 8
    ids, probs = jnp.transpose(ids, (2, 0, 1)), jnp.transpose(probs, (2, 0, 1))
    return pl.pallas_call(
        functools.partial(table_kernel, experts),
        out_shape=(
            pltpu.VMEM((height, count), jnp.float32),
            pltpu.VMEM((count, features), tokens.dtype),
        ),
        in_specs=[HBM] * 3,
        out_specs=(VMEM, VMEM),
        scratch_shapes=[
            pltpu.VMEM(ids.shape, ids.dtype),
            pltpu.VMEM(probs.shape, probs.dtype),
            pltpu.SemaphoreType.DMA((3,)),
        ],
        compiler_params=SMALL,
        name="make_table",
    )(in_hbm(ids), in_hbm(probs), in_hbm(tokens))


def plan(tables, capacity, hots, coefs):
    local, slots, width = hots.shape
    blocks = len(tables)
    count = width // blocks
    experts = local * lax.axis_size("expert")
    first = lax.axis_index("expert") * local
    before = lax.broadcasted_iota(jnp.int32, (count, count), 0)
    after = lax.broadcasted_iota(jnp.int32, (count, count), 1)
    upto = jnp.where(before <= after, 1.0, 0.0).astype(jnp.bfloat16)
    slot_ids = lax.broadcasted_iota(jnp.int32, (slots, width), 0).astype(jnp.float32)
    weights, scales, places = [], [], []
    for b in range(blocks):
        weight = tables[b][pl.ds(first, local), :]
        ones = jnp.where(weight > 0.0, 1.0, 0.0)
        padded = jnp.concatenate([ones, jnp.zeros((-local % 16, count), jnp.float32)], axis=0)
        rank = jnp.dot(padded.astype(jnp.bfloat16), upto, preferred_element_type=jnp.float32)[:local]
        places.append(jnp.where(weight > 0.0, rank + float(b * capacity - 1), -1.0))
        weights.append(weight)
        scales.append(tables[b][pl.ds(experts, 1), :])
    weight = jnp.concatenate(weights, axis=1) if blocks > 1 else weights[0]
    scale = jnp.concatenate(scales, axis=1) if blocks > 1 else scales[0]
    place = jnp.concatenate(places, axis=1) if blocks > 1 else places[0]
    for j in range(local):
        hit = slot_ids == place[j : j + 1, :]
        hots[j] = jnp.where(hit, 1.0, 0.0).astype(jnp.bfloat16)
        coefs[j, :, 0:1] = jnp.sum(jnp.where(hit, scale, 0.0), axis=1, keepdims=True)
        coefs[j, :, 1:2] = jnp.sum(jnp.where(hit, weight[j : j + 1, :], 0.0), axis=1, keepdims=True)


def pack(hots, tokens, rows):
    for j in range(hots.shape[0]):
        rows[j] = jnp.dot(hots[j], tokens, preferred_element_type=jnp.float32).astype(jnp.bfloat16)


def expert_hidden(j, rows, hots, coefs, gates, ups, out_ref, base):
    units = gates.shape[2]
    size = hots.shape[2]
    gate = jnp.dot(rows[j], gates[j], preferred_element_type=jnp.float32)
    up = jnp.dot(rows[j], ups[j], preferred_element_type=jnp.float32)
    scale = coefs[j, :, 0:1]
    weight = coefs[j, :, 1:2]
    g = gate * scale
    h = (g / (1.0 + jnp.exp(-g))) * (up * (scale * weight))
    placed = lax.dot_general(
        hots[j], h.astype(jnp.bfloat16), (((0,), (0,)), ((), ())), preferred_element_type=jnp.float32
    )
    out_ref[pl.ds(base, size), pl.ds(j * units, units)] = placed.astype(jnp.bfloat16)


def near_kernel(capacity, *refs):
    tables, tokens = refs[:2], refs[2:4]
    gate_hbm, up_hbm, hidden, gates, ups = refs[4:9]
    hots, coefs, rows, gate_sem, up_sem = refs[9:]
    local = gates.shape[0]
    copies = []
    for j in range(local):
        copies.append(pltpu.make_async_copy(gate_hbm.at[j], gates.at[j], gate_sem.at[j]))
        copies.append(pltpu.make_async_copy(up_hbm.at[j], ups.at[j], up_sem.at[j]))
    for copy in copies:
        copy.start()
    plan(tables, capacity, hots, coefs)
    pack(hots, jnp.concatenate([t[...] for t in tokens], axis=0), rows)
    for j in range(local):
        copies[2 * j].wait()
        copies[2 * j + 1].wait()
        expert_hidden(j, rows, hots, coefs, gates, ups, hidden, 0)


def near_hidden(tables, tokens, w_gate, w_up, capacity, blocks):
    count, features = tokens[0].shape
    local, _, units = w_gate.shape
    slots = slots_of(capacity, 2)
    return pl.pallas_call(
        functools.partial(near_kernel, capacity),
        out_shape=(
            pltpu.VMEM((blocks * count, local * units), jnp.bfloat16),
            pltpu.VMEM(w_gate.shape, w_gate.dtype),
            pltpu.VMEM(w_up.shape, w_up.dtype),
        ),
        in_specs=[VMEM] * 4 + [HBM] * 2,
        out_specs=(VMEM,) * 3,
        scratch_shapes=[
            pltpu.VMEM((local, slots, 2 * count), jnp.bfloat16),
            pltpu.VMEM((local, slots, 128), jnp.float32),
            pltpu.VMEM((local, slots, features), jnp.bfloat16),
            pltpu.SemaphoreType.DMA((local,)),
            pltpu.SemaphoreType.DMA((local,)),
        ],
        compiler_params=GRANT,
        cost_estimate=pl.CostEstimate(
            flops=4 * local * slots * features * units,
            bytes_accessed=4 * local * features * units,
            transcendentals=local * slots * units,
        ),
        name="near_hidden",
    )(*tables, *tokens, in_hbm(w_gate), in_hbm(w_up))


def far_plan_kernel(capacity, far_count, *refs):
    tables = refs[:far_count]
    step, _, hots, coefs, factor = refs[far_count:]
    factor[...] = jnp.full(factor.shape, step[0])
    for p in range(far_count // 2):
        plan(tables[2 * p : 2 * p + 2], capacity, hots.at[p], coefs.at[p])


def far_plan(tables, step_size, order, capacity, local):
    pairs = len(tables) // 2
    count = tables[0].shape[1]
    slots = slots_of(capacity, 2)
    return pl.pallas_call(
        functools.partial(far_plan_kernel, capacity, len(tables)),
        out_shape=(
            pltpu.VMEM((pairs, local, slots, 2 * count), jnp.bfloat16),
            pltpu.VMEM((pairs, local, slots, 128), jnp.float32),
            pltpu.VMEM((8, 128), jnp.float32),
        ),
        in_specs=[VMEM] * len(tables) + [pl.BlockSpec(memory_space=pltpu.SMEM), ANY],
        out_specs=(VMEM,) * 3,
        compiler_params=SMALL,
        cost_estimate=BRIEF,
        name="far_plan",
    )(*tables, step_size, order)


def far_kernel(far_count, *refs):
    tokens = refs[:far_count]
    hots, coefs, gates, ups, down_hbm, start_hbm, _, hidden, downs, start, rows, sems = refs[far_count:]
    copies = [
        pltpu.make_async_copy(down_hbm, downs, sems.at[0]),
        pltpu.make_async_copy(start_hbm, start, sems.at[1]),
    ]
    for copy in copies:
        copy.start()
    for p in range(far_count // 2):
        both = jnp.concatenate([tokens[2 * p][...], tokens[2 * p + 1][...]], axis=0)
        pack(hots.at[p], both, rows)
        for j in range(gates.shape[0]):
            expert_hidden(j, rows, hots.at[p], coefs.at[p], gates, ups, hidden, (p + 1) * hots.shape[3])
    for copy in copies:
        copy.wait()


def far_hidden(tokens, hots, coefs, gates, ups, w_down, start_state, hidden):
    pairs, local, slots, size = hots.shape
    features, units = gates.shape[1:]
    return pl.pallas_call(
        functools.partial(far_kernel, len(tokens)),
        out_shape=(
            pltpu.VMEM(hidden.shape, hidden.dtype),
            pltpu.VMEM(w_down.shape, w_down.dtype),
            pltpu.VMEM(start_state.shape, start_state.dtype),
        ),
        in_specs=[VMEM] * (len(tokens) + 4) + [HBM] * 2 + [VMEM],
        out_specs=(VMEM,) * 3,
        scratch_shapes=[
            pltpu.VMEM((local, slots, features), jnp.bfloat16),
            pltpu.SemaphoreType.DMA((2,)),
        ],
        input_output_aliases={len(tokens) + 6: 0},
        compiler_params=GRANT,
        cost_estimate=pl.CostEstimate(
            flops=4 * pairs * local * slots * features * units,
            bytes_accessed=6 * local * features * units,
            transcendentals=pairs * local * slots * units,
        ),
        name="far_hidden",
    )(*tokens, hots, coefs, gates, ups, in_hbm(w_down), in_hbm(start_state), hidden)


def down_kernel(core, start, hidden_ref, down_ref, _, *outs):
    count, width = outs[0].shape[1:]
    pairs = sum(ref.shape[0] for ref in outs)
    local, units, _ = down_ref.shape
    columns = pl.ds(start, width)
    total = None
    for j in range(local):
        inner = pl.ds(j * units, units)
        parts = [hidden_ref[pl.ds((2 * p + core) * count, count), inner] for p in range(pairs)]
        term = jnp.dot(
            jnp.concatenate(parts, axis=0), down_ref[j, :, columns], preferred_element_type=jnp.float32
        )
        total = term if total is None else total + term
    rows = [total[p * count : (p + 1) * count] for p in range(pairs)]
    for ref in outs:
        for p in range(ref.shape[0]):
            ref[p] = rows.pop(0).astype(ref.dtype)


def down_rows(hidden, downs, order, send, count, start, width):
    pairs = hidden.shape[0] // (2 * count)
    dtype = jnp.bfloat16 if send else jnp.float32
    return pl.pallas_call(
        functools.partial(down_kernel, int(send), start),
        out_shape=(pltpu.VMEM((1, count, width), dtype), pltpu.VMEM((pairs - 1, count, width), dtype)),
        in_specs=[VMEM, VMEM, ANY],
        out_specs=(VMEM, VMEM),
        compiler_params=GRANT,
        cost_estimate=BRIEF,
        name="down_rows",
    )(hidden, downs, order)


def core_sum_kernel(widths, near_keep, far_keep, near_got, far_got, factor, _, *outs):
    step = factor[0:1, 0:1]
    first = 0
    for n, width in enumerate(widths):
        columns = pl.ds(first, width)
        first += width
        outs[2 * n][...] = step * (near_keep[0, :, columns] + near_got[0, :, columns].astype(jnp.float32))
        for p in range(far_keep.shape[0]):
            total = step * (far_keep[p, :, columns] + far_got[p, :, columns].astype(jnp.float32))
            outs[2 * n + 1][p] = total.astype(jnp.bfloat16)


def core_sum(keeps, gots, factor, order, widths):
    others, count, _ = keeps[1].shape
    shapes = []
    for width in widths:
        shapes.append(pltpu.VMEM((count, width), jnp.float32))
        shapes.append(pltpu.VMEM((others, count, width), jnp.bfloat16))
    return pl.pallas_call(
        functools.partial(core_sum_kernel, widths),
        out_shape=tuple(shapes),
        in_specs=[VMEM] * 5 + [ANY],
        out_specs=(VMEM,) * len(shapes),
        compiler_params=SMALL,
        cost_estimate=BRIEF,
        name="core_sum",
    )(*keeps, *gots, factor, order)


def chain_kernel(hop, backs, first, send, start, _, own, *refs):
    outs = refs[len(refs) - 1 - send :]
    result, width = outs[-1], own.shape[1]

    @pl.when(lax.axis_index("tm") == hop)
    def _():
        total = own[...]
        for ref in refs[: backs + (hop > 0)]:
            total = total + ref[...].astype(jnp.float32)
        if send:
            outs[0][...] = total.astype(jnp.bfloat16)
        columns = pl.ds(first, width)
        result[:, columns] = start[:, columns] + total


def chain_step(hop, own, backs, got, first, send, start, result, order):
    inputs = [start, order, own, *backs] + ([] if got is None else [got]) + ([] if result is None else [result])
    return pl.pallas_call(
        functools.partial(chain_kernel, hop, len(backs), first, int(send)),
        out_shape=((pltpu.VMEM(own.shape, jnp.bfloat16),) if send else ())
        + (pltpu.VMEM(start.shape, jnp.float32),),
        in_specs=[VMEM, ANY] + [VMEM] * (len(inputs) - 2),
        out_specs=(VMEM,) * (1 + send),
        input_output_aliases={} if result is None else {len(inputs) - 1: int(send)},
        compiler_params=SMALL,
        cost_estimate=BRIEF,
        name="chain_step",
    )(*inputs)


def write_kernel(result, out, sem):
    copy = pltpu.make_async_copy(result, out, sem)
    copy.start()
    copy.wait()


def write_out(result):
    return pl.pallas_call(
        write_kernel,
        out_shape=pltpu.HBM(result.shape, result.dtype),
        in_specs=[VMEM],
        out_specs=HBM,
        scratch_shapes=[pltpu.SemaphoreType.DMA],
        compiler_params=SMALL,
        cost_estimate=BRIEF,
        name="write_out",
    )(result)


def tie_kernel(value_ref, order_ref, out_ref):
    pass


def tie(value, order):
    return pl.pallas_call(
        tie_kernel,
        out_shape=jax.ShapeDtypeStruct(value.shape, value.dtype),
        in_specs=[ANY, ANY],
        out_specs=ANY,
        input_output_aliases={0: 0},
        compiler_params=SMALL,
        cost_estimate=BRIEF,
        name="tie",
    )(value, order)


def exchange(value, low, members, steps):
    pairs = []
    for e in range(members):
        for z in range(steps):
            if z in (low, low + 1):
                pairs.append((e * steps + z, e * steps + 2 * low + 1 - z))
            else:
                pairs.append((e * steps + z, (e ^ 1) * steps + z))
    return lax.ppermute(value, ("expert", "tm"), pairs)


def shards(tokens, route_ids, route_probs, step_size, start_state, w_gate, w_up, w_down):
    members = lax.axis_size("expert")
    steps = lax.axis_size("tm")
    tok_count, feature_count = tokens.shape[1:]
    topk_count = route_ids.shape[2]
    expert_total = w_gate.shape[0] * members
    capacity = 3 * tok_count * topk_count // (2 * expert_total)
    chips = members // 2

    def swapped(value):
        return lax.ppermute(value, "expert", [(i, i ^ 1) for i in range(members)])

    def shifted(value, by):
        return lax.ppermute(value, "expert", [(i, (i + 2 * by) % members) for i in range(members)])

    own = tokens[0]
    far_same = [shifted(own, by) for by in range(1, chips)]
    partner = swapped(own)
    table, own = make_table(route_ids, route_probs, tokens, expert_total)
    far_table = [shifted(table, by) for by in range(1, chips)]
    hidden, gates, ups = near_hidden([table, swapped(table)], [own, partner], w_gate, w_up, capacity, members)
    far_tables, far_tokens = [], []
    for value, piece in zip(far_table, far_same):
        value = tie(value, hidden)
        piece = tie(piece, value)
        far_tables += [value, swapped(value)]
        far_tokens += [piece, swapped(piece)]
    hots, coefs, factor = far_plan(far_tables, step_size, hidden, capacity, w_gate.shape[0])
    hidden, downs, start = far_hidden(far_tokens, hots, coefs, gates, ups, w_down, start_state, hidden)

    widths = [feature_count * share // 16 for share in SHARES]
    parts = len(widths)
    firsts = [sum(widths[:c]) for c in range(parts)]
    events, ready = [], 0.0
    for g, group in enumerate(GROUPS):
        share = sum(SHARES[c] for c in group) / 4
        ready = max(ready, 8.0 if g == len(GROUPS) - 1 else 0.0)
        events.append((ready, "send", g, 0))
        events.append((ready + share, "keep", g, 0))
        ready += 2.2 * share if g == 0 else 2.0 * share
        events.append((ready if g == 0 else (7.8, 9.1, 13.0)[min(g, 3) - 1], "core", g, 0))
    for c, ready in enumerate((7.7, 12.6, 15.4, 17.9)):
        for hop in range(steps):
            events.append((ready + (5.4 if c < 3 else 4.6) * hop, "chain", c, hop))
    order, result = hidden, None
    gots, keeps, owns, backs, arrived = {}, {}, {}, {}, {}
    for _, kind, c, hop in sorted(events):
        if kind in ("send", "keep"):
            group = GROUPS[c]
            width = sum(widths[i] for i in group)
            part = down_rows(hidden, downs, order, kind == "send", tok_count, firsts[group[0]], width)
            if kind == "send":
                gots[c] = [swapped(piece) for piece in reversed(part)][::-1]
            else:
                keeps[c] = part
            order = part[0]
        elif kind == "core":
            group = GROUPS[c]
            sums = core_sum(keeps[c], gots[c], factor, order, [widths[i] for i in group])
            for n, i in enumerate(group):
                owns[i] = sums[2 * n]
                backs[i] = [shifted(sums[2 * n + 1][by - 1], -by) for by in range(1, chips)]
            order = sums[0]
        else:
            send = hop < steps - 1
            *sent, result = chain_step(
                hop, owns[c], backs[c], arrived.get(c), firsts[c], send, start, result, order
            )
            if send:
                order = sent[0]
                arrived[c] = exchange(sent[0], hop, members, steps)
    return write_out(result)[None]


def solution(mesh):
    return jax.shard_map(
        shards,
        mesh=mesh,
        in_specs=(
            P("tm", ("copies", "expert"), None),
            P("tm", ("copies", "expert"), None),
            P("tm", ("copies", "expert"), None),
            P(("copies", "tm")),
            P(("copies", "expert"), None),
            P("expert", None, None),
            P("expert", None, None),
            P("expert", None, None),
        ),
        out_specs=P("tm", ("copies", "expert"), None),
        check_vma=False,
    )
```

```python
import functools

import jax
import jax.numpy as jnp
from jax import lax
from jax.experimental import pallas as pl
from jax.experimental.pallas import tpu as pltpu
from jax.sharding import PartitionSpec as P

ANY = pl.BlockSpec(memory_space=pl.ANY)
HBM = pl.BlockSpec(memory_space=pltpu.HBM)
VMEM = pl.BlockSpec(memory_space=pltpu.VMEM)
GRANT = pltpu.CompilerParams(vmem_limit_bytes=7 * 1024 * 1024)
BRIEF = pl.CostEstimate(flops=0, bytes_accessed=0, transcendentals=0)
SMALL = pltpu.CompilerParams(vmem_limit_bytes=2 * 1024 * 1024)


SHARES = (4, 5, 4, 3)
GROUPS = ((0,), (1, 2, 3))
DOWN_TIMES = ((0.0, 1.2, 2.8), (3.0, 5.7, 9.7))
CHAIN_TIMES = ((12.1, 6.2, 5.7), (16.3, 6.1, 6.0), (19.7, 5.5, 5.5), (22.3, 4.8, 4.8))


def in_hbm(value):
    return pltpu.with_memory_space_constraint(value, pltpu.HBM)


def slots_of(capacity, blocks):
    return -(-capacity * blocks // 16) * 16


def table_kernel(experts, ids_hbm, probs_hbm, tokens_hbm, table, tokens, ids, probs, sems):
    copy = pltpu.make_async_copy(tokens_hbm.at[0], tokens, sems.at[0])
    smalls = [
        pltpu.make_async_copy(ids_hbm, ids, sems.at[1]),
        pltpu.make_async_copy(probs_hbm, probs, sems.at[2]),
    ]
    copy.start()
    for small in smalls:
        small.start()
    for small in smalls:
        small.wait()
    choices, _, count = ids.shape
    total = probs[0]
    for k in range(1, choices):
        total = total + probs[k]
    names = lax.broadcasted_iota(jnp.int32, table.shape, 0)
    value = jnp.zeros(table.shape, jnp.float32)
    for k in range(choices):
        value = value + jnp.where(ids[k] == names, probs[k] / total, 0.0)
    copy.wait()
    rows = tokens[...].astype(jnp.float32)
    scale = lax.rsqrt(jnp.mean(rows * rows, axis=1, keepdims=True) + 1e-06)
    scale = jnp.broadcast_to(scale, (count, 128)).T[:1]
    table[...] = jnp.where(names == experts, scale, value)


def make_table(ids, probs, tokens, experts):
    count, features = tokens.shape[1:]
    height = -(-(experts + 1) // 8) * 8
    ids, probs = jnp.transpose(ids, (2, 0, 1)), jnp.transpose(probs, (2, 0, 1))
    return pl.pallas_call(
        functools.partial(table_kernel, experts),
        out_shape=(
            pltpu.VMEM((height, count), jnp.float32),
            pltpu.VMEM((count, features), tokens.dtype),
        ),
        in_specs=[HBM] * 3,
        out_specs=(VMEM, VMEM),
        scratch_shapes=[
            pltpu.VMEM(ids.shape, ids.dtype),
            pltpu.VMEM(probs.shape, probs.dtype),
            pltpu.SemaphoreType.DMA((3,)),
        ],
        compiler_params=SMALL,
        name="make_table",
    )(in_hbm(ids), in_hbm(probs), in_hbm(tokens))


def plan(tables, capacity, hots, coefs):
    local, slots, width = hots.shape
    blocks = len(tables)
    count = width // blocks
    experts = local * lax.axis_size("expert")
    first = lax.axis_index("expert") * local
    before = lax.broadcasted_iota(jnp.int32, (count, count), 0)
    after = lax.broadcasted_iota(jnp.int32, (count, count), 1)
    upto = jnp.where(before <= after, 1.0, 0.0).astype(jnp.bfloat16)
    slot_ids = lax.broadcasted_iota(jnp.int32, (slots, width), 0).astype(jnp.float32)
    weights, scales, places = [], [], []
    for b in range(blocks):
        weight = tables[b][pl.ds(first, local), :]
        ones = jnp.where(weight > 0.0, 1.0, 0.0)
        padded = jnp.concatenate([ones, jnp.zeros((-local % 16, count), jnp.float32)], axis=0)
        rank = jnp.dot(padded.astype(jnp.bfloat16), upto, preferred_element_type=jnp.float32)[:local]
        places.append(jnp.where(weight > 0.0, rank + float(b * capacity - 1), -1.0))
        weights.append(weight)
        scales.append(tables[b][pl.ds(experts, 1), :])
    weight = jnp.concatenate(weights, axis=1) if blocks > 1 else weights[0]
    scale = jnp.concatenate(scales, axis=1) if blocks > 1 else scales[0]
    place = jnp.concatenate(places, axis=1) if blocks > 1 else places[0]
    for j in range(local):
        hit = slot_ids == place[j : j + 1, :]
        hots[j] = jnp.where(hit, 1.0, 0.0).astype(jnp.bfloat16)
        coefs[j, :, 0:1] = jnp.sum(jnp.where(hit, scale, 0.0), axis=1, keepdims=True)
        coefs[j, :, 1:2] = jnp.sum(jnp.where(hit, weight[j : j + 1, :], 0.0), axis=1, keepdims=True)


def pack(hots, tokens, rows):
    for j in range(hots.shape[0]):
        rows[j] = jnp.dot(hots[j], tokens, preferred_element_type=jnp.float32).astype(jnp.bfloat16)


def expert_hidden(j, rows, hots, coefs, gates, ups, out_ref, base):
    units = gates.shape[2]
    size = hots.shape[2]
    gate = jnp.dot(rows[j], gates[j], preferred_element_type=jnp.float32)
    up = jnp.dot(rows[j], ups[j], preferred_element_type=jnp.float32)
    scale = coefs[j, :, 0:1]
    weight = coefs[j, :, 1:2]
    g = gate * scale
    h = (g / (1.0 + jnp.exp(-g))) * (up * (scale * weight))
    placed = lax.dot_general(
        hots[j], h.astype(jnp.bfloat16), (((0,), (0,)), ((), ())), preferred_element_type=jnp.float32
    )
    out_ref[pl.ds(base, size), pl.ds(j * units, units)] = placed.astype(jnp.bfloat16)


def near_kernel(capacity, *refs):
    tables, tokens = refs[:2], refs[2:4]
    gate_hbm, up_hbm, hidden, gates, ups = refs[4:9]
    hots, coefs, rows, gate_sem, up_sem = refs[9:]
    local = gates.shape[0]
    copies = []
    for j in range(local):
        copies.append(pltpu.make_async_copy(gate_hbm.at[j], gates.at[j], gate_sem.at[j]))
        copies.append(pltpu.make_async_copy(up_hbm.at[j], ups.at[j], up_sem.at[j]))
    for copy in copies:
        copy.start()
    plan(tables, capacity, hots, coefs)
    pack(hots, jnp.concatenate([t[...] for t in tokens], axis=0), rows)
    for j in range(local):
        copies[2 * j].wait()
        copies[2 * j + 1].wait()
        expert_hidden(j, rows, hots, coefs, gates, ups, hidden, 0)


def near_hidden(tables, tokens, w_gate, w_up, capacity, blocks):
    count, features = tokens[0].shape
    local, _, units = w_gate.shape
    slots = slots_of(capacity, 2)
    return pl.pallas_call(
        functools.partial(near_kernel, capacity),
        out_shape=(
            pltpu.VMEM((blocks * count, local * units), jnp.bfloat16),
            pltpu.VMEM(w_gate.shape, w_gate.dtype),
            pltpu.VMEM(w_up.shape, w_up.dtype),
        ),
        in_specs=[VMEM] * 4 + [HBM] * 2,
        out_specs=(VMEM,) * 3,
        scratch_shapes=[
            pltpu.VMEM((local, slots, 2 * count), jnp.bfloat16),
            pltpu.VMEM((local, slots, 128), jnp.float32),
            pltpu.VMEM((local, slots, features), jnp.bfloat16),
            pltpu.SemaphoreType.DMA((local,)),
            pltpu.SemaphoreType.DMA((local,)),
        ],
        compiler_params=GRANT,
        cost_estimate=pl.CostEstimate(
            flops=4 * local * slots * features * units,
            bytes_accessed=4 * local * features * units,
            transcendentals=local * slots * units,
        ),
        name="near_hidden",
    )(*tables, *tokens, in_hbm(w_gate), in_hbm(w_up))


def far_plan_kernel(capacity, far_count, *refs):
    tables = refs[:far_count]
    step, _, hots, coefs, factor = refs[far_count:]
    factor[...] = jnp.full(factor.shape, step[0])
    for p in range(far_count // 2):
        plan(tables[2 * p : 2 * p + 2], capacity, hots.at[p], coefs.at[p])


def far_plan(tables, step_size, order, capacity, local):
    pairs = len(tables) // 2
    count = tables[0].shape[1]
    slots = slots_of(capacity, 2)
    return pl.pallas_call(
        functools.partial(far_plan_kernel, capacity, len(tables)),
        out_shape=(
            pltpu.VMEM((pairs, local, slots, 2 * count), jnp.bfloat16),
            pltpu.VMEM((pairs, local, slots, 128), jnp.float32),
            pltpu.VMEM((8, 128), jnp.float32),
        ),
        in_specs=[VMEM] * len(tables) + [pl.BlockSpec(memory_space=pltpu.SMEM), ANY],
        out_specs=(VMEM,) * 3,
        compiler_params=SMALL,
        cost_estimate=BRIEF,
        name="far_plan",
    )(*tables, step_size, order)


def far_kernel(far_count, *refs):
    tokens = refs[:far_count]
    hots, coefs, gates, ups, down_hbm, start_hbm, _, hidden, downs, start, rows, sems = refs[far_count:]
    copies = [
        pltpu.make_async_copy(down_hbm, downs, sems.at[0]),
        pltpu.make_async_copy(start_hbm, start, sems.at[1]),
    ]
    for copy in copies:
        copy.start()
    for p in range(far_count // 2):
        both = jnp.concatenate([tokens[2 * p][...], tokens[2 * p + 1][...]], axis=0)
        pack(hots.at[p], both, rows)
        for j in range(gates.shape[0]):
            expert_hidden(j, rows, hots.at[p], coefs.at[p], gates, ups, hidden, (p + 1) * hots.shape[3])
    for copy in copies:
        copy.wait()


def far_hidden(tokens, hots, coefs, gates, ups, w_down, start_state, hidden):
    pairs, local, slots, size = hots.shape
    features, units = gates.shape[1:]
    return pl.pallas_call(
        functools.partial(far_kernel, len(tokens)),
        out_shape=(
            pltpu.VMEM(hidden.shape, hidden.dtype),
            pltpu.VMEM(w_down.shape, w_down.dtype),
            pltpu.VMEM(start_state.shape, start_state.dtype),
        ),
        in_specs=[VMEM] * (len(tokens) + 4) + [HBM] * 2 + [VMEM],
        out_specs=(VMEM,) * 3,
        scratch_shapes=[
            pltpu.VMEM((local, slots, features), jnp.bfloat16),
            pltpu.SemaphoreType.DMA((2,)),
        ],
        input_output_aliases={len(tokens) + 6: 0},
        compiler_params=GRANT,
        cost_estimate=pl.CostEstimate(
            flops=4 * pairs * local * slots * features * units,
            bytes_accessed=6 * local * features * units,
            transcendentals=pairs * local * slots * units,
        ),
        name="far_hidden",
    )(*tokens, hots, coefs, gates, ups, in_hbm(w_down), in_hbm(start_state), hidden)


def down_kernel(core, start, hidden_ref, down_ref, _, out_ref):
    pairs, count, width = out_ref.shape
    local, units, _ = down_ref.shape
    columns = pl.ds(start, width)
    total = None
    for j in range(local):
        inner = pl.ds(j * units, units)
        parts = [hidden_ref[pl.ds((2 * p + core) * count, count), inner] for p in range(pairs)]
        term = jnp.dot(
            jnp.concatenate(parts, axis=0), down_ref[j, :, columns], preferred_element_type=jnp.float32
        )
        total = term if total is None else total + term
    for p in range(pairs):
        out_ref[p] = total[p * count : (p + 1) * count].astype(out_ref.dtype)


def down_rows(hidden, downs, order, send, count, start, width):
    pairs = hidden.shape[0] // (2 * count)
    return pl.pallas_call(
        functools.partial(down_kernel, int(send), start),
        out_shape=pltpu.VMEM((pairs, count, width), jnp.bfloat16 if send else jnp.float32),
        in_specs=[VMEM, VMEM, ANY],
        out_specs=VMEM,
        compiler_params=GRANT,
        cost_estimate=BRIEF,
        name="down_rows",
    )(hidden, downs, order)


def core_sum_kernel(widths, keep, got, factor, _, *outs):
    step = factor[0:1, 0:1]
    first = 0
    for n, width in enumerate(widths):
        columns = pl.ds(first, width)
        first += width
        for p in range(keep.shape[0]):
            total = step * (keep[p, :, columns] + got[p, :, columns].astype(jnp.float32))
            if p == 0:
                outs[2 * n][...] = total
            else:
                outs[2 * n + 1][p - 1] = total.astype(jnp.bfloat16)


def core_sum(keep, got, factor, order, widths):
    pairs, count, _ = keep.shape
    shapes = []
    for width in widths:
        shapes.append(pltpu.VMEM((count, width), jnp.float32))
        shapes.append(pltpu.VMEM((pairs - 1, count, width), jnp.bfloat16))
    return pl.pallas_call(
        functools.partial(core_sum_kernel, widths),
        out_shape=tuple(shapes),
        in_specs=[VMEM, VMEM, VMEM, ANY],
        out_specs=(VMEM,) * len(shapes),
        compiler_params=SMALL,
        cost_estimate=BRIEF,
        name="core_sum",
    )(keep, got, factor, order)


def chain_kernel(hop, backs, first, send, start, _, own, *refs):
    outs = refs[len(refs) - 1 - send :]
    result, width = outs[-1], own.shape[1]

    @pl.when(lax.axis_index("tm") == hop)
    def _():
        total = own[...]
        for ref in refs[: backs + (hop > 0)]:
            total = total + ref[...].astype(jnp.float32)
        if send:
            outs[0][...] = total.astype(jnp.bfloat16)
        columns = pl.ds(first, width)
        result[:, columns] = start[:, columns] + total


def chain_step(hop, own, backs, got, first, send, start, result, order):
    inputs = [start, order, own, *backs] + ([] if got is None else [got]) + ([] if result is None else [result])
    return pl.pallas_call(
        functools.partial(chain_kernel, hop, len(backs), first, int(send)),
        out_shape=((pltpu.VMEM(own.shape, jnp.bfloat16),) if send else ())
        + (pltpu.VMEM(start.shape, jnp.float32),),
        in_specs=[VMEM, ANY] + [VMEM] * (len(inputs) - 2),
        out_specs=(VMEM,) * (1 + send),
        input_output_aliases={} if result is None else {len(inputs) - 1: int(send)},
        compiler_params=SMALL,
        cost_estimate=BRIEF,
        name="chain_step",
    )(*inputs)


def write_kernel(result, out, sem):
    copy = pltpu.make_async_copy(result, out, sem)
    copy.start()
    copy.wait()


def write_out(result):
    return pl.pallas_call(
        write_kernel,
        out_shape=pltpu.HBM(result.shape, result.dtype),
        in_specs=[VMEM],
        out_specs=HBM,
        scratch_shapes=[pltpu.SemaphoreType.DMA],
        compiler_params=SMALL,
        cost_estimate=BRIEF,
        name="write_out",
    )(result)


def tie_kernel(value_ref, order_ref, out_ref):
    pass


def tie(value, order):
    return pl.pallas_call(
        tie_kernel,
        out_shape=jax.ShapeDtypeStruct(value.shape, value.dtype),
        in_specs=[ANY, ANY],
        out_specs=ANY,
        input_output_aliases={0: 0},
        compiler_params=SMALL,
        cost_estimate=BRIEF,
        name="tie",
    )(value, order)


def exchange(value, low, members, steps):
    pairs = []
    for e in range(members):
        for z in range(steps):
            if z in (low, low + 1):
                pairs.append((e * steps + z, e * steps + 2 * low + 1 - z))
            else:
                pairs.append((e * steps + z, (e ^ 1) * steps + z))
    return lax.ppermute(value, ("expert", "tm"), pairs)


def shards(tokens, route_ids, route_probs, step_size, start_state, w_gate, w_up, w_down):
    members = lax.axis_size("expert")
    steps = lax.axis_size("tm")
    tok_count, feature_count = tokens.shape[1:]
    topk_count = route_ids.shape[2]
    expert_total = w_gate.shape[0] * members
    capacity = 3 * tok_count * topk_count // (2 * expert_total)
    chips = members // 2

    def swapped(value):
        return lax.ppermute(value, "expert", [(i, i ^ 1) for i in range(members)])

    def shifted(value, by):
        return lax.ppermute(value, "expert", [(i, (i + 2 * by) % members) for i in range(members)])

    own = tokens[0]
    far_same = [shifted(own, by) for by in range(1, chips)]
    partner = swapped(own)
    table, own = make_table(route_ids, route_probs, tokens, expert_total)
    far_table = [shifted(table, by) for by in range(1, chips)]
    hidden, gates, ups = near_hidden([table, swapped(table)], [own, partner], w_gate, w_up, capacity, members)
    far_tables, far_tokens = [], []
    for value, piece in zip(far_table, far_same):
        value = tie(value, hidden)
        piece = tie(piece, value)
        far_tables += [value, swapped(value)]
        far_tokens += [piece, swapped(piece)]
    hots, coefs, factor = far_plan(far_tables, step_size, hidden, capacity, w_gate.shape[0])
    hidden, downs, start = far_hidden(far_tokens, hots, coefs, gates, ups, w_down, start_state, hidden)

    widths = [feature_count * share // 16 for share in SHARES]
    parts = len(widths)
    firsts = [sum(widths[:c]) for c in range(parts)]
    events = []
    for g, times in enumerate(DOWN_TIMES):
        for kind, ready in zip(("send", "keep", "core"), times):
            events.append((ready, kind, g, 0))
    for c, times in enumerate(CHAIN_TIMES):
        for hop in range(steps):
            events.append((times[0] + (times[1] + times[2] * (hop - 1) if hop else 0.0), "chain", c, hop))
    order, result = hidden, None
    gots, keeps, owns, backs, arrived = {}, {}, {}, {}, {}
    for _, kind, c, hop in sorted(events):
        if kind in ("send", "keep"):
            group = GROUPS[c]
            width = sum(widths[i] for i in group)
            part = down_rows(hidden, downs, order, kind == "send", tok_count, firsts[group[0]], width)
            if kind == "send":
                gots[c] = swapped(part)
            else:
                keeps[c] = part
            order = part
        elif kind == "core":
            group = GROUPS[c]
            sums = core_sum(keeps[c], gots[c], factor, order, [widths[i] for i in group])
            for n, i in enumerate(group):
                owns[i] = sums[2 * n]
                backs[i] = [shifted(sums[2 * n + 1][by - 1], -by) for by in range(1, chips)]
            order = sums[0]
        else:
            send = hop < steps - 1
            *sent, result = chain_step(
                hop, owns[c], backs[c], arrived.get(c), firsts[c], send, start, result, order
            )
            if send:
                order = sent[0]
                arrived[c] = exchange(sent[0], hop, members, steps)
    return write_out(result)[None]


def solution(mesh):
    return jax.shard_map(
        shards,
        mesh=mesh,
        in_specs=(
            P("tm", ("copies", "expert"), None),
            P("tm", ("copies", "expert"), None),
            P("tm", ("copies", "expert"), None),
            P(("copies", "tm")),
            P(("copies", "expert"), None),
            P("expert", None, None),
            P("expert", None, None),
            P("expert", None, None),
        ),
        out_specs=P("tm", ("copies", "expert"), None),
        check_vma=False,
    )
```

```python
import functools

import jax
import jax.numpy as jnp
from jax import lax
from jax.experimental import pallas as pl
from jax.experimental.pallas import tpu as pltpu
from jax.sharding import PartitionSpec as P

ANY = pl.BlockSpec(memory_space=pl.ANY)
HBM = pl.BlockSpec(memory_space=pltpu.HBM)
VMEM = pl.BlockSpec(memory_space=pltpu.VMEM)
GRANT = pltpu.CompilerParams(vmem_limit_bytes=7 * 1024 * 1024)
BRIEF = pl.CostEstimate(flops=0, bytes_accessed=0, transcendentals=0)
SMALL = pltpu.CompilerParams(vmem_limit_bytes=2 * 1024 * 1024)


def in_hbm(value):
    return pltpu.with_memory_space_constraint(value, pltpu.HBM)


def slots_of(capacity, blocks):
    return -(-capacity * blocks // 16) * 16


def table_kernel(experts, ids_hbm, probs_hbm, tokens_hbm, table, tokens, ids, probs, sems):
    copy = pltpu.make_async_copy(tokens_hbm.at[0], tokens, sems.at[0])
    smalls = [
        pltpu.make_async_copy(ids_hbm, ids, sems.at[1]),
        pltpu.make_async_copy(probs_hbm, probs, sems.at[2]),
    ]
    copy.start()
    for small in smalls:
        small.start()
    for small in smalls:
        small.wait()
    choices, _, count = ids.shape
    total = probs[0]
    for k in range(1, choices):
        total = total + probs[k]
    names = lax.broadcasted_iota(jnp.int32, table.shape, 0)
    value = jnp.zeros(table.shape, jnp.float32)
    for k in range(choices):
        value = value + jnp.where(ids[k] == names, probs[k] / total, 0.0)
    copy.wait()
    rows = tokens[...].astype(jnp.float32)
    scale = lax.rsqrt(jnp.mean(rows * rows, axis=1, keepdims=True) + 1e-06)
    scale = jnp.broadcast_to(scale, (count, 128)).T[:1]
    table[...] = jnp.where(names == experts, scale, value)


def make_table(ids, probs, tokens, experts):
    count, features = tokens.shape[1:]
    height = -(-(experts + 1) // 8) * 8
    ids, probs = jnp.transpose(ids, (2, 0, 1)), jnp.transpose(probs, (2, 0, 1))
    return pl.pallas_call(
        functools.partial(table_kernel, experts),
        out_shape=(
            pltpu.VMEM((height, count), jnp.float32),
            pltpu.VMEM((count, features), tokens.dtype),
        ),
        in_specs=[HBM] * 3,
        out_specs=(VMEM, VMEM),
        scratch_shapes=[
            pltpu.VMEM(ids.shape, ids.dtype),
            pltpu.VMEM(probs.shape, probs.dtype),
            pltpu.SemaphoreType.DMA((3,)),
        ],
        compiler_params=SMALL,
        name="make_table",
    )(in_hbm(ids), in_hbm(probs), in_hbm(tokens))


def plan(tables, capacity, hots, coefs):
    local, slots, width = hots.shape
    blocks = len(tables)
    count = width // blocks
    experts = local * lax.axis_size("expert")
    first = lax.axis_index("expert") * local
    before = lax.broadcasted_iota(jnp.int32, (count, count), 0)
    after = lax.broadcasted_iota(jnp.int32, (count, count), 1)
    upto = jnp.where(before <= after, 1.0, 0.0).astype(jnp.bfloat16)
    slot_ids = lax.broadcasted_iota(jnp.int32, (slots, width), 0).astype(jnp.float32)
    weights, scales, places = [], [], []
    for b in range(blocks):
        weight = tables[b][pl.ds(first, local), :]
        ones = jnp.where(weight > 0.0, 1.0, 0.0)
        padded = jnp.concatenate([ones, jnp.zeros((-local % 16, count), jnp.float32)], axis=0)
        rank = jnp.dot(padded.astype(jnp.bfloat16), upto, preferred_element_type=jnp.float32)[:local]
        places.append(jnp.where(weight > 0.0, rank + float(b * capacity - 1), -1.0))
        weights.append(weight)
        scales.append(tables[b][pl.ds(experts, 1), :])
    weight = jnp.concatenate(weights, axis=1) if blocks > 1 else weights[0]
    scale = jnp.concatenate(scales, axis=1) if blocks > 1 else scales[0]
    place = jnp.concatenate(places, axis=1) if blocks > 1 else places[0]
    for j in range(local):
        hit = slot_ids == place[j : j + 1, :]
        hots[j] = jnp.where(hit, 1.0, 0.0).astype(jnp.bfloat16)
        coefs[j, :, 0:1] = jnp.sum(jnp.where(hit, scale, 0.0), axis=1, keepdims=True)
        coefs[j, :, 1:2] = jnp.sum(jnp.where(hit, weight[j : j + 1, :], 0.0), axis=1, keepdims=True)


def pack(hots, tokens, rows):
    for j in range(hots.shape[0]):
        rows[j] = jnp.dot(hots[j], tokens, preferred_element_type=jnp.float32).astype(jnp.bfloat16)


def expert_hidden(j, rows, hots, coefs, gates, ups, out_ref, base):
    units = gates.shape[2]
    size = hots.shape[2]
    gate = jnp.dot(rows[j], gates[j], preferred_element_type=jnp.float32)
    up = jnp.dot(rows[j], ups[j], preferred_element_type=jnp.float32)
    scale = coefs[j, :, 0:1]
    weight = coefs[j, :, 1:2]
    g = gate * scale
    h = (g / (1.0 + jnp.exp(-g))) * (up * (scale * weight))
    placed = lax.dot_general(
        hots[j], h.astype(jnp.bfloat16), (((0,), (0,)), ((), ())), preferred_element_type=jnp.float32
    )
    out_ref[pl.ds(base, size), pl.ds(j * units, units)] = placed.astype(jnp.bfloat16)


def near_kernel(capacity, *refs):
    tables, tokens = refs[:2], refs[2:4]
    gate_hbm, up_hbm, hidden, gates, ups = refs[4:9]
    hots, coefs, rows, gate_sem, up_sem = refs[9:]
    local = gates.shape[0]
    copies = []
    for j in range(local):
        copies.append(pltpu.make_async_copy(gate_hbm.at[j], gates.at[j], gate_sem.at[j]))
        copies.append(pltpu.make_async_copy(up_hbm.at[j], ups.at[j], up_sem.at[j]))
    for copy in copies:
        copy.start()
    plan(tables, capacity, hots, coefs)
    pack(hots, jnp.concatenate([t[...] for t in tokens], axis=0), rows)
    for j in range(local):
        copies[2 * j].wait()
        copies[2 * j + 1].wait()
        expert_hidden(j, rows, hots, coefs, gates, ups, hidden, 0)


def near_hidden(tables, tokens, w_gate, w_up, capacity, blocks):
    count, features = tokens[0].shape
    local, _, units = w_gate.shape
    slots = slots_of(capacity, 2)
    return pl.pallas_call(
        functools.partial(near_kernel, capacity),
        out_shape=(
            pltpu.VMEM((blocks * count, local * units), jnp.bfloat16),
            pltpu.VMEM(w_gate.shape, w_gate.dtype),
            pltpu.VMEM(w_up.shape, w_up.dtype),
        ),
        in_specs=[VMEM] * 4 + [HBM] * 2,
        out_specs=(VMEM,) * 3,
        scratch_shapes=[
            pltpu.VMEM((local, slots, 2 * count), jnp.bfloat16),
            pltpu.VMEM((local, slots, 128), jnp.float32),
            pltpu.VMEM((local, slots, features), jnp.bfloat16),
            pltpu.SemaphoreType.DMA((local,)),
            pltpu.SemaphoreType.DMA((local,)),
        ],
        compiler_params=GRANT,
        cost_estimate=pl.CostEstimate(
            flops=4 * local * slots * features * units,
            bytes_accessed=4 * local * features * units,
            transcendentals=local * slots * units,
        ),
        name="near_hidden",
    )(*tables, *tokens, in_hbm(w_gate), in_hbm(w_up))


def far_plan_kernel(capacity, far_count, *refs):
    tables = refs[:far_count]
    step, _, hots, coefs, factor = refs[far_count:]
    factor[...] = jnp.full(factor.shape, step[0])
    for p in range(far_count // 2):
        plan(tables[2 * p : 2 * p + 2], capacity, hots.at[p], coefs.at[p])


def far_plan(tables, step_size, order, capacity, local):
    pairs = len(tables) // 2
    count = tables[0].shape[1]
    slots = slots_of(capacity, 2)
    return pl.pallas_call(
        functools.partial(far_plan_kernel, capacity, len(tables)),
        out_shape=(
            pltpu.VMEM((pairs, local, slots, 2 * count), jnp.bfloat16),
            pltpu.VMEM((pairs, local, slots, 128), jnp.float32),
            pltpu.VMEM((8, 128), jnp.float32),
        ),
        in_specs=[VMEM] * len(tables) + [pl.BlockSpec(memory_space=pltpu.SMEM), ANY],
        out_specs=(VMEM,) * 3,
        compiler_params=SMALL,
        cost_estimate=BRIEF,
        name="far_plan",
    )(*tables, step_size, order)


def far_kernel(far_count, *refs):
    tokens = refs[:far_count]
    hots, coefs, gates, ups, down_hbm, start_hbm, _, hidden, downs, start, rows, sems = refs[far_count:]
    copies = [
        pltpu.make_async_copy(down_hbm, downs, sems.at[0]),
        pltpu.make_async_copy(start_hbm, start, sems.at[1]),
    ]
    for copy in copies:
        copy.start()
    for p in range(far_count // 2):
        both = jnp.concatenate([tokens[2 * p][...], tokens[2 * p + 1][...]], axis=0)
        pack(hots.at[p], both, rows)
        for j in range(gates.shape[0]):
            expert_hidden(j, rows, hots.at[p], coefs.at[p], gates, ups, hidden, (p + 1) * hots.shape[3])
    for copy in copies:
        copy.wait()


def far_hidden(tokens, hots, coefs, gates, ups, w_down, start_state, hidden):
    pairs, local, slots, size = hots.shape
    features, units = gates.shape[1:]
    return pl.pallas_call(
        functools.partial(far_kernel, len(tokens)),
        out_shape=(
            pltpu.VMEM(hidden.shape, hidden.dtype),
            pltpu.VMEM(w_down.shape, w_down.dtype),
            pltpu.VMEM(start_state.shape, start_state.dtype),
        ),
        in_specs=[VMEM] * (len(tokens) + 4) + [HBM] * 2 + [VMEM],
        out_specs=(VMEM,) * 3,
        scratch_shapes=[
            pltpu.VMEM((local, slots, features), jnp.bfloat16),
            pltpu.SemaphoreType.DMA((2,)),
        ],
        input_output_aliases={len(tokens) + 6: 0},
        compiler_params=GRANT,
        cost_estimate=pl.CostEstimate(
            flops=4 * pairs * local * slots * features * units,
            bytes_accessed=6 * local * features * units,
            transcendentals=pairs * local * slots * units,
        ),
        name="far_hidden",
    )(*tokens, hots, coefs, gates, ups, in_hbm(w_down), in_hbm(start_state), hidden)


def down_kernel(core, start, hidden_ref, down_ref, _, out_ref):
    pairs, count, width = out_ref.shape
    local, units, _ = down_ref.shape
    columns = pl.ds(start, width)
    total = None
    for j in range(local):
        inner = pl.ds(j * units, units)
        parts = [hidden_ref[pl.ds((2 * p + core) * count, count), inner] for p in range(pairs)]
        term = jnp.dot(
            jnp.concatenate(parts, axis=0), down_ref[j, :, columns], preferred_element_type=jnp.float32
        )
        total = term if total is None else total + term
    for p in range(pairs):
        out_ref[p] = total[p * count : (p + 1) * count].astype(out_ref.dtype)


def down_rows(hidden, downs, order, send, count, start, width):
    pairs = hidden.shape[0] // (2 * count)
    return pl.pallas_call(
        functools.partial(down_kernel, int(send), start),
        out_shape=pltpu.VMEM((pairs, count, width), jnp.bfloat16 if send else jnp.float32),
        in_specs=[VMEM, VMEM, ANY],
        out_specs=VMEM,
        compiler_params=GRANT,
        cost_estimate=BRIEF,
        name="down_rows",
    )(hidden, downs, order)


def core_sum_kernel(chunks, keep, got, factor, _, *outs):
    pairs, _, width = keep.shape
    width = width // chunks
    step = factor[0:1, 0:1]
    for i in range(chunks):
        columns = pl.ds(i * width, width)
        for p in range(pairs):
            total = step * (keep[p, :, columns] + got[p, :, columns].astype(jnp.float32))
            if p == 0:
                outs[2 * i][...] = total
            else:
                outs[2 * i + 1][p - 1] = total.astype(jnp.bfloat16)


def core_sum(keep, got, factor, order, chunks):
    pairs, count, width = keep.shape
    shapes = []
    for _ in range(chunks):
        shapes.append(pltpu.VMEM((count, width // chunks), jnp.float32))
        shapes.append(pltpu.VMEM((pairs - 1, count, width // chunks), jnp.bfloat16))
    return pl.pallas_call(
        functools.partial(core_sum_kernel, chunks),
        out_shape=tuple(shapes),
        in_specs=[VMEM, VMEM, VMEM, ANY],
        out_specs=(VMEM,) * len(shapes),
        compiler_params=SMALL,
        cost_estimate=BRIEF,
        name="core_sum",
    )(keep, got, factor, order)


def chain_kernel(hop, backs, first, send, start, _, own, *refs):
    outs = refs[len(refs) - 1 - send :]
    result, width = outs[-1], own.shape[1]

    @pl.when(lax.axis_index("tm") == hop)
    def _():
        total = own[...]
        for ref in refs[: backs + (hop > 0)]:
            total = total + ref[...].astype(jnp.float32)
        if send:
            outs[0][...] = total.astype(jnp.bfloat16)
        columns = pl.ds(first, width)
        result[:, columns] = start[:, columns] + total


def chain_step(hop, own, backs, got, first, send, start, result, order):
    inputs = [start, order, own, *backs] + ([] if got is None else [got]) + ([] if result is None else [result])
    return pl.pallas_call(
        functools.partial(chain_kernel, hop, len(backs), first, int(send)),
        out_shape=((pltpu.VMEM(own.shape, jnp.bfloat16),) if send else ())
        + (pltpu.VMEM(start.shape, jnp.float32),),
        in_specs=[VMEM, ANY] + [VMEM] * (len(inputs) - 2),
        out_specs=(VMEM,) * (1 + send),
        input_output_aliases={} if result is None else {len(inputs) - 1: int(send)},
        compiler_params=SMALL,
        cost_estimate=BRIEF,
        name="chain_step",
    )(*inputs)


def write_kernel(first, result, _, out, mark, sems):
    mark[...] = jnp.zeros_like(mark)
    last = lax.axis_index("tm") == lax.axis_size("tm") - 1
    head, tail = pl.ds(0, first), pl.ds(first, result.shape[1] - first)
    copies = [pltpu.make_async_copy(result.at[:, part], out.at[:, part], sems.at[i]) for i, part in enumerate((head, tail))]
    copies[0].start()

    @pl.when(jnp.logical_not(last))
    def _():
        copies[1].start()
        copies[1].wait()

    copies[0].wait()


def write_most(result, first, order):
    return pl.pallas_call(
        functools.partial(write_kernel, first),
        out_shape=(pltpu.HBM(result.shape, result.dtype), pltpu.VMEM((8, 128), jnp.float32)),
        in_specs=[VMEM, ANY],
        out_specs=(HBM, VMEM),
        scratch_shapes=[pltpu.SemaphoreType.DMA((2,))],
        compiler_params=SMALL,
        cost_estimate=BRIEF,
        name="write_most",
    )(result, order)


def last_kernel(first, backs, start, _, own, *refs):
    out, block, sem = refs[-3:]

    @pl.when(lax.axis_index("tm") == lax.axis_size("tm") - 1)
    def _():
        columns = pl.ds(first, own.shape[1])
        total = start[:, columns] + own[...]
        for ref in refs[: backs + 1]:
            total = total + ref[...].astype(jnp.float32)
        block[...] = total
        copy = pltpu.make_async_copy(block, out.at[:, columns], sem)
        copy.start()
        copy.wait()


def last_step(own, backs, got, first, start, out, order):
    inputs = [start, order, own, *backs, got, out]
    return pl.pallas_call(
        functools.partial(last_kernel, first, len(backs)),
        out_shape=pltpu.HBM(out.shape, out.dtype),
        in_specs=[VMEM, ANY] + [VMEM] * (len(inputs) - 3) + [HBM],
        out_specs=HBM,
        scratch_shapes=[pltpu.VMEM(own.shape, jnp.float32), pltpu.SemaphoreType.DMA],
        input_output_aliases={len(inputs) - 1: 0},
        compiler_params=SMALL,
        cost_estimate=BRIEF,
        name="last_step",
    )(*inputs)


def tie_kernel(value_ref, order_ref, out_ref):
    pass


def tie(value, order):
    return pl.pallas_call(
        tie_kernel,
        out_shape=jax.ShapeDtypeStruct(value.shape, value.dtype),
        in_specs=[ANY, ANY],
        out_specs=ANY,
        input_output_aliases={0: 0},
        compiler_params=SMALL,
        cost_estimate=BRIEF,
        name="tie",
    )(value, order)


def exchange(value, low, members, steps):
    pairs = []
    for e in range(members):
        for z in range(steps):
            if z in (low, low + 1):
                pairs.append((e * steps + z, e * steps + 2 * low + 1 - z))
            else:
                pairs.append((e * steps + z, (e ^ 1) * steps + z))
    return lax.ppermute(value, ("expert", "tm"), pairs)


def shards(tokens, route_ids, route_probs, step_size, start_state, w_gate, w_up, w_down):
    members = lax.axis_size("expert")
    steps = lax.axis_size("tm")
    tok_count, feature_count = tokens.shape[1:]
    topk_count = route_ids.shape[2]
    expert_total = w_gate.shape[0] * members
    capacity = 3 * tok_count * topk_count // (2 * expert_total)
    chips = members // 2

    def swapped(value):
        return lax.ppermute(value, "expert", [(i, i ^ 1) for i in range(members)])

    def shifted(value, by):
        return lax.ppermute(value, "expert", [(i, (i + 2 * by) % members) for i in range(members)])

    own = tokens[0]
    far_same = [shifted(own, by) for by in range(1, chips)]
    partner = swapped(own)
    table, own = make_table(route_ids, route_probs, tokens, expert_total)
    far_table = [shifted(table, by) for by in range(1, chips)]
    hidden, gates, ups = near_hidden([table, swapped(table)], [own, partner], w_gate, w_up, capacity, members)
    far_tables, far_tokens = [], []
    for value, piece in zip(far_table, far_same):
        value = tie(value, hidden)
        piece = tie(piece, value)
        far_tables += [value, swapped(value)]
        far_tokens += [piece, swapped(piece)]
    hots, coefs, factor = far_plan(far_tables, step_size, hidden, capacity, w_gate.shape[0])
    hidden, downs, start = far_hidden(far_tokens, hots, coefs, gates, ups, w_down, start_state, hidden)

    parts = 4
    width = feature_count // parts
    groups = [(0, 1), (1, parts - 1)]
    events, ready = [], 0.0
    for g, (_, count) in enumerate(groups):
        events.append((ready, "send", g, 0))
        events.append((ready + 0.9 * count, "keep", g, 0))
        ready += max(2.5, 1.8 * count)
        events.append((ready, "core", g, 0))
    for c in range(parts):
        for hop in range(steps):
            events.append((12.0 + 3.3 * c + 5.0 * hop, "chain", c, hop))
    order, result = hidden, None
    gots, keeps, owns, backs, arrived = {}, {}, {}, {}, {}
    for _, kind, c, hop in sorted(events):
        if kind in ("send", "keep"):
            first, count = groups[c]
            part = down_rows(hidden, downs, order, kind == "send", tok_count, first * width, count * width)
            if kind == "send":
                gots[c] = swapped(part)
            else:
                keeps[c] = part
            order = part
        elif kind == "core":
            first, count = groups[c]
            sums = core_sum(keeps[c], gots[c], factor, order, count)
            for i in range(count):
                owns[first + i] = sums[2 * i]
                backs[first + i] = [shifted(sums[2 * i + 1][by - 1], -by) for by in range(1, chips)]
            order = sums[0]
        else:
            if c == parts - 1 and hop == steps - 1:
                out, order = write_most(result, c * width, order)
                out = last_step(owns[c], backs[c], arrived[c], c * width, start, out, order)
                continue
            send = hop < steps - 1
            *sent, result = chain_step(
                hop, owns[c], backs[c], arrived.get(c), c * width, send, start, result, order
            )
            if send:
                order = sent[0]
                arrived[c] = exchange(sent[0], hop, members, steps)
    return out[None]


def solution(mesh):
    return jax.shard_map(
        shards,
        mesh=mesh,
        in_specs=(
            P("tm", ("copies", "expert"), None),
            P("tm", ("copies", "expert"), None),
            P("tm", ("copies", "expert"), None),
            P(("copies", "tm")),
            P(("copies", "expert"), None),
            P("expert", None, None),
            P("expert", None, None),
            P("expert", None, None),
        ),
        out_specs=P("tm", ("copies", "expert"), None),
        check_vma=False,
    )
```

```python
import functools

import jax
import jax.numpy as jnp
from jax import lax
from jax.experimental import pallas as pl
from jax.experimental.pallas import tpu as pltpu
from jax.sharding import PartitionSpec as P

ANY = pl.BlockSpec(memory_space=pl.ANY)
HBM = pl.BlockSpec(memory_space=pltpu.HBM)
VMEM = pl.BlockSpec(memory_space=pltpu.VMEM)
GRANT = pltpu.CompilerParams(vmem_limit_bytes=7 * 1024 * 1024)
BRIEF = pl.CostEstimate(flops=0, bytes_accessed=0, transcendentals=0)
SMALL = pltpu.CompilerParams(vmem_limit_bytes=2 * 1024 * 1024)


FAR_TIMES = ((0.0, 4.05), (1.0, 4.1), (2.0, 4.15), (3.0, 4.2))
NEAR_TIMES = ((6.0, 10.6), (7.0, 10.65), (8.0, 14.1), (9.0, 14.2))
ARRIVAL = 10.5
CHAIN_TIMES = ((10.9, 5.0), (14.0, 5.0), (17.3, 5.0), (20.6, 5.0))


def in_hbm(value):
    return pltpu.with_memory_space_constraint(value, pltpu.HBM)


def slots_of(capacity, blocks):
    return -(-capacity * blocks // 16) * 16


def table_kernel(experts, ids_hbm, probs_hbm, tokens_hbm, table, tokens, ids, probs, sems):
    copy = pltpu.make_async_copy(tokens_hbm.at[0], tokens, sems.at[0])
    smalls = [
        pltpu.make_async_copy(ids_hbm, ids, sems.at[1]),
        pltpu.make_async_copy(probs_hbm, probs, sems.at[2]),
    ]
    copy.start()
    for small in smalls:
        small.start()
    for small in smalls:
        small.wait()
    choices, _, count = ids.shape
    total = probs[0]
    for k in range(1, choices):
        total = total + probs[k]
    names = lax.broadcasted_iota(jnp.int32, table.shape, 0)
    value = jnp.zeros(table.shape, jnp.float32)
    for k in range(choices):
        value = value + jnp.where(ids[k] == names, probs[k] / total, 0.0)
    copy.wait()
    rows = tokens[...].astype(jnp.float32)
    scale = lax.rsqrt(jnp.mean(rows * rows, axis=1, keepdims=True) + 1e-06)
    scale = jnp.broadcast_to(scale, (count, 128)).T[:1]
    table[...] = jnp.where(names == experts, scale, value)


def make_table(ids, probs, tokens, experts):
    count, features = tokens.shape[1:]
    height = -(-(experts + 1) // 8) * 8
    ids, probs = jnp.transpose(ids, (2, 0, 1)), jnp.transpose(probs, (2, 0, 1))
    return pl.pallas_call(
        functools.partial(table_kernel, experts),
        out_shape=(
            pltpu.VMEM((height, count), jnp.float32),
            pltpu.VMEM((count, features), tokens.dtype),
        ),
        in_specs=[HBM] * 3,
        out_specs=(VMEM, VMEM),
        scratch_shapes=[
            pltpu.VMEM(ids.shape, ids.dtype),
            pltpu.VMEM(probs.shape, probs.dtype),
            pltpu.SemaphoreType.DMA((3,)),
        ],
        compiler_params=SMALL,
        name="make_table",
    )(in_hbm(ids), in_hbm(probs), in_hbm(tokens))


def plan(tables, capacity, hots, coefs):
    local, slots, width = hots.shape
    blocks = len(tables)
    count = width // blocks
    experts = local * lax.axis_size("expert")
    first = lax.axis_index("expert") * local
    before = lax.broadcasted_iota(jnp.int32, (count, count), 0)
    after = lax.broadcasted_iota(jnp.int32, (count, count), 1)
    upto = jnp.where(before <= after, 1.0, 0.0).astype(jnp.bfloat16)
    slot_ids = lax.broadcasted_iota(jnp.int32, (slots, width), 0).astype(jnp.float32)
    weights, scales, places = [], [], []
    for b in range(blocks):
        weight = tables[b][pl.ds(first, local), :]
        ones = jnp.where(weight > 0.0, 1.0, 0.0)
        padded = jnp.concatenate([ones, jnp.zeros((-local % 16, count), jnp.float32)], axis=0)
        rank = jnp.dot(padded.astype(jnp.bfloat16), upto, preferred_element_type=jnp.float32)[:local]
        places.append(jnp.where(weight > 0.0, rank + float(b * capacity - 1), -1.0))
        weights.append(weight)
        scales.append(tables[b][pl.ds(experts, 1), :])
    weight = jnp.concatenate(weights, axis=1) if blocks > 1 else weights[0]
    scale = jnp.concatenate(scales, axis=1) if blocks > 1 else scales[0]
    place = jnp.concatenate(places, axis=1) if blocks > 1 else places[0]
    for j in range(local):
        hit = slot_ids == place[j : j + 1, :]
        hots[j] = jnp.where(hit, 1.0, 0.0).astype(jnp.bfloat16)
        coefs[j, :, 0:1] = jnp.sum(jnp.where(hit, scale, 0.0), axis=1, keepdims=True)
        coefs[j, :, 1:2] = jnp.sum(jnp.where(hit, weight[j : j + 1, :], 0.0), axis=1, keepdims=True)


def pack(hots, tokens, rows):
    for j in range(hots.shape[0]):
        rows[j] = jnp.dot(hots[j], tokens, preferred_element_type=jnp.float32).astype(jnp.bfloat16)


def expert_hidden(j, rows, hots, coefs, gates, ups, out_ref, base):
    units = gates.shape[2]
    size = hots.shape[2]
    gate = jnp.dot(rows[j], gates[j], preferred_element_type=jnp.float32)
    up = jnp.dot(rows[j], ups[j], preferred_element_type=jnp.float32)
    scale = coefs[j, :, 0:1]
    weight = coefs[j, :, 1:2]
    g = gate * scale
    h = (g / (1.0 + jnp.exp(-g))) * (up * (scale * weight))
    placed = lax.dot_general(
        hots[j], h.astype(jnp.bfloat16), (((0,), (0,)), ((), ())), preferred_element_type=jnp.float32
    )
    out_ref[pl.ds(base, size), pl.ds(j * units, units)] = placed.astype(jnp.bfloat16)


def near_kernel(capacity, *refs):
    tables, tokens = refs[:2], refs[2:4]
    gate_hbm, up_hbm, hidden, gates, ups = refs[4:9]
    hots, coefs, rows, gate_sem, up_sem = refs[9:]
    local = gates.shape[0]
    copies = []
    for j in range(local):
        copies.append(pltpu.make_async_copy(gate_hbm.at[j], gates.at[j], gate_sem.at[j]))
        copies.append(pltpu.make_async_copy(up_hbm.at[j], ups.at[j], up_sem.at[j]))
    for copy in copies:
        copy.start()
    plan(tables, capacity, hots, coefs)
    pack(hots, jnp.concatenate([t[...] for t in tokens], axis=0), rows)
    for j in range(local):
        copies[2 * j].wait()
        copies[2 * j + 1].wait()
        expert_hidden(j, rows, hots, coefs, gates, ups, hidden, 0)


def near_hidden(tables, tokens, w_gate, w_up, capacity, blocks):
    count, features = tokens[0].shape
    local, _, units = w_gate.shape
    slots = slots_of(capacity, 2)
    return pl.pallas_call(
        functools.partial(near_kernel, capacity),
        out_shape=(
            pltpu.VMEM((blocks * count, local * units), jnp.bfloat16),
            pltpu.VMEM(w_gate.shape, w_gate.dtype),
            pltpu.VMEM(w_up.shape, w_up.dtype),
        ),
        in_specs=[VMEM] * 4 + [HBM] * 2,
        out_specs=(VMEM,) * 3,
        scratch_shapes=[
            pltpu.VMEM((local, slots, 2 * count), jnp.bfloat16),
            pltpu.VMEM((local, slots, 128), jnp.float32),
            pltpu.VMEM((local, slots, features), jnp.bfloat16),
            pltpu.SemaphoreType.DMA((local,)),
            pltpu.SemaphoreType.DMA((local,)),
        ],
        compiler_params=GRANT,
        cost_estimate=pl.CostEstimate(
            flops=4 * local * slots * features * units,
            bytes_accessed=4 * local * features * units,
            transcendentals=local * slots * units,
        ),
        name="near_hidden",
    )(*tables, *tokens, in_hbm(w_gate), in_hbm(w_up))


def far_plan_kernel(capacity, far_count, *refs):
    tables = refs[:far_count]
    step, _, hots, coefs, factor = refs[far_count:]
    factor[...] = jnp.full(factor.shape, step[0])
    for p in range(far_count // 2):
        plan(tables[2 * p : 2 * p + 2], capacity, hots.at[p], coefs.at[p])


def far_plan(tables, step_size, order, capacity, local):
    pairs = len(tables) // 2
    count = tables[0].shape[1]
    slots = slots_of(capacity, 2)
    return pl.pallas_call(
        functools.partial(far_plan_kernel, capacity, len(tables)),
        out_shape=(
            pltpu.VMEM((pairs, local, slots, 2 * count), jnp.bfloat16),
            pltpu.VMEM((pairs, local, slots, 128), jnp.float32),
            pltpu.VMEM((8, 128), jnp.float32),
        ),
        in_specs=[VMEM] * len(tables) + [pl.BlockSpec(memory_space=pltpu.SMEM), ANY],
        out_specs=(VMEM,) * 3,
        compiler_params=SMALL,
        cost_estimate=BRIEF,
        name="far_plan",
    )(*tables, step_size, order)


def far_kernel(far_count, *refs):
    tokens = refs[:far_count]
    hots, coefs, gates, ups, down_hbm, start_hbm, _, hidden, downs, start, rows, sems = refs[far_count:]
    copies = [
        pltpu.make_async_copy(down_hbm, downs, sems.at[0]),
        pltpu.make_async_copy(start_hbm, start, sems.at[1]),
    ]
    for copy in copies:
        copy.start()
    for p in range(far_count // 2):
        both = jnp.concatenate([tokens[2 * p][...], tokens[2 * p + 1][...]], axis=0)
        pack(hots.at[p], both, rows)
        for j in range(gates.shape[0]):
            expert_hidden(j, rows, hots.at[p], coefs.at[p], gates, ups, hidden, (p + 1) * hots.shape[3])
    for copy in copies:
        copy.wait()


def far_hidden(tokens, hots, coefs, gates, ups, w_down, start_state, hidden):
    pairs, local, slots, size = hots.shape
    features, units = gates.shape[1:]
    return pl.pallas_call(
        functools.partial(far_kernel, len(tokens)),
        out_shape=(
            pltpu.VMEM(hidden.shape, hidden.dtype),
            pltpu.VMEM(w_down.shape, w_down.dtype),
            pltpu.VMEM(start_state.shape, start_state.dtype),
        ),
        in_specs=[VMEM] * (len(tokens) + 4) + [HBM] * 2 + [VMEM],
        out_specs=(VMEM,) * 3,
        scratch_shapes=[
            pltpu.VMEM((local, slots, features), jnp.bfloat16),
            pltpu.SemaphoreType.DMA((2,)),
        ],
        input_output_aliases={len(tokens) + 6: 0},
        compiler_params=GRANT,
        cost_estimate=pl.CostEstimate(
            flops=4 * pairs * local * slots * features * units,
            bytes_accessed=6 * local * features * units,
            transcendentals=pairs * local * slots * units,
        ),
        name="far_hidden",
    )(*tokens, hots, coefs, gates, ups, in_hbm(w_down), in_hbm(start_state), hidden)


def down_kernel(first_pair, start, hidden_ref, down_ref, _, keep, send):
    pairs, count, width = keep.shape
    local, units, _ = down_ref.shape
    rows, columns = pl.ds(2 * first_pair * count, 2 * pairs * count), pl.ds(start, width)
    total = None
    for j in range(local):
        term = jnp.dot(
            hidden_ref[rows, pl.ds(j * units, units)], down_ref[j, :, columns], preferred_element_type=jnp.float32
        )
        total = term if total is None else total + term
    for p in range(pairs):
        keep[p] = total[2 * p * count : (2 * p + 1) * count]
        send[p] = total[(2 * p + 1) * count : (2 * p + 2) * count].astype(jnp.bfloat16)


def down_rows(hidden, downs, order, far, count, start, width):
    pairs = hidden.shape[0] // (2 * count) - 1 if far else 1
    return pl.pallas_call(
        functools.partial(down_kernel, int(far), start),
        out_shape=(
            pltpu.VMEM((pairs, count, width), jnp.float32),
            pltpu.VMEM((pairs, count, width), jnp.bfloat16),
        ),
        in_specs=[VMEM, VMEM, ANY],
        out_specs=(VMEM, VMEM),
        compiler_params=GRANT,
        cost_estimate=BRIEF,
        name="far_down" if far else "near_down",
    )(hidden, downs, order)


def core_sum_kernel(keep, got, factor, _, *outs):
    step = factor[0:1, 0:1]
    first = 0
    for out in outs:
        columns = pl.ds(first, out.shape[2])
        first += out.shape[2]
        for p in range(out.shape[0]):
            total = step * (keep[p, :, columns] + got[p, :, columns].astype(jnp.float32))
            out[p] = total.astype(out.dtype)


def core_sum(keep, got, factor, order, chunks, dtype):
    pairs, count, width = keep.shape
    return pl.pallas_call(
        core_sum_kernel,
        out_shape=(pltpu.VMEM((pairs, count, width // chunks), dtype),) * chunks,
        in_specs=[VMEM, VMEM, VMEM, ANY],
        out_specs=(VMEM,) * chunks,
        compiler_params=SMALL,
        cost_estimate=BRIEF,
        name="core_sum",
    )(keep, got, factor, order)


def chain_kernel(hop, backs, first, send, start, _, own, *refs):
    outs = refs[len(refs) - 1 - send :]
    result, width = outs[-1], own.shape[2]

    @pl.when(lax.axis_index("tm") == hop)
    def _():
        total = own[0]
        for ref in refs[: backs + (hop > 0)]:
            total = total + ref[...].astype(jnp.float32)
        if send:
            outs[0][...] = total.astype(jnp.bfloat16)
        columns = pl.ds(first, width)
        result[:, columns] = start[:, columns] + total


def chain_step(hop, own, backs, got, first, send, start, result, order):
    inputs = [start, order, own, *backs] + ([] if got is None else [got]) + ([] if result is None else [result])
    return pl.pallas_call(
        functools.partial(chain_kernel, hop, len(backs), first, int(send)),
        out_shape=((pltpu.VMEM(own.shape[1:], jnp.bfloat16),) if send else ())
        + (pltpu.VMEM(start.shape, jnp.float32),),
        in_specs=[VMEM, ANY] + [VMEM] * (len(inputs) - 2),
        out_specs=(VMEM,) * (1 + send),
        input_output_aliases={} if result is None else {len(inputs) - 1: int(send)},
        compiler_params=SMALL,
        cost_estimate=BRIEF,
        name="chain_step",
    )(*inputs)


def write_kernel(first, result, _, out, mark, sems):
    mark[...] = jnp.zeros_like(mark)
    last = lax.axis_index("tm") == lax.axis_size("tm") - 1
    head, tail = pl.ds(0, first), pl.ds(first, result.shape[1] - first)
    copies = [pltpu.make_async_copy(result.at[:, part], out.at[:, part], sems.at[i]) for i, part in enumerate((head, tail))]
    copies[0].start()

    @pl.when(jnp.logical_not(last))
    def _():
        copies[1].start()
        copies[1].wait()

    copies[0].wait()


def write_most(result, first, order):
    return pl.pallas_call(
        functools.partial(write_kernel, first),
        out_shape=(pltpu.HBM(result.shape, result.dtype), pltpu.VMEM((8, 128), jnp.float32)),
        in_specs=[VMEM, ANY],
        out_specs=(HBM, VMEM),
        scratch_shapes=[pltpu.SemaphoreType.DMA((2,))],
        compiler_params=SMALL,
        cost_estimate=BRIEF,
        name="write_most",
    )(result, order)


def last_kernel(first, backs, start, _, own, *refs):
    out, block, sem = refs[-3:]

    @pl.when(lax.axis_index("tm") == lax.axis_size("tm") - 1)
    def _():
        columns = pl.ds(first, own.shape[2])
        total = start[:, columns] + own[0]
        for ref in refs[: backs + 1]:
            total = total + ref[...].astype(jnp.float32)
        block[...] = total
        copy = pltpu.make_async_copy(block, out.at[:, columns], sem)
        copy.start()
        copy.wait()


def last_step(own, backs, got, first, start, out, order):
    inputs = [start, order, own, *backs, got, out]
    return pl.pallas_call(
        functools.partial(last_kernel, first, len(backs)),
        out_shape=pltpu.HBM(out.shape, out.dtype),
        in_specs=[VMEM, ANY] + [VMEM] * (len(inputs) - 3) + [HBM],
        out_specs=HBM,
        scratch_shapes=[pltpu.VMEM(own.shape[1:], jnp.float32), pltpu.SemaphoreType.DMA],
        input_output_aliases={len(inputs) - 1: 0},
        compiler_params=SMALL,
        cost_estimate=BRIEF,
        name="last_step",
    )(*inputs)


def tie_kernel(value_ref, order_ref, out_ref):
    pass


def tie(value, order):
    return pl.pallas_call(
        tie_kernel,
        out_shape=jax.ShapeDtypeStruct(value.shape, value.dtype),
        in_specs=[ANY, ANY],
        out_specs=ANY,
        input_output_aliases={0: 0},
        compiler_params=SMALL,
        cost_estimate=BRIEF,
        name="tie",
    )(value, order)


def exchange(value, low, members, steps):
    pairs = []
    for e in range(members):
        for z in range(steps):
            if z in (low, low + 1):
                pairs.append((e * steps + z, e * steps + 2 * low + 1 - z))
            else:
                pairs.append((e * steps + z, (e ^ 1) * steps + z))
    return lax.ppermute(value, ("expert", "tm"), pairs)


def shards(tokens, route_ids, route_probs, step_size, start_state, w_gate, w_up, w_down):
    members = lax.axis_size("expert")
    steps = lax.axis_size("tm")
    tok_count, feature_count = tokens.shape[1:]
    topk_count = route_ids.shape[2]
    expert_total = w_gate.shape[0] * members
    capacity = 3 * tok_count * topk_count // (2 * expert_total)
    chips = members // 2

    def swapped(value):
        return lax.ppermute(value, "expert", [(i, i ^ 1) for i in range(members)])

    def shifted(value, by):
        return lax.ppermute(value, "expert", [(i, (i + 2 * by) % members) for i in range(members)])

    own = tokens[0]
    far_same = [shifted(own, by) for by in range(1, chips)]
    partner = swapped(own)
    table, own = make_table(route_ids, route_probs, tokens, expert_total)
    far_table = [shifted(table, by) for by in range(1, chips)]
    hidden, gates, ups = near_hidden([table, swapped(table)], [own, partner], w_gate, w_up, capacity, members)
    far_tables, far_tokens = [], []
    for value, piece in zip(far_table, far_same):
        value = tie(value, hidden)
        piece = tie(piece, value)
        far_tables += [value, swapped(value)]
        far_tokens += [piece, swapped(piece)]
    hots, coefs, factor = far_plan(far_tables, step_size, hidden, capacity, w_gate.shape[0])
    hidden, downs, start = far_hidden(far_tokens, hots, coefs, gates, ups, w_down, start_state, hidden)

    parts = 4
    width = feature_count // parts
    groups = {kind: [(c, 1) for c in range(parts)] for kind in ("far", "near")}
    events = []
    for kind, times in (("far", FAR_TIMES), ("near", NEAR_TIMES)):
        for g, (ready, summed) in enumerate(times):
            events += [(ready, kind, g, 0), (summed, kind + "_sum", g, 0)]
    events.append((ARRIVAL, "arrival", 0, 0))
    for c, (ready, period) in enumerate(CHAIN_TIMES):
        for hop in range(steps):
            events.append((ready + period * hop, "chain", c, hop))
    order, result = hidden, None
    keeps, gots, owns, backs, arrived = {}, {}, {}, {}, {}
    for _, kind, c, hop in sorted(events):
        if kind in ("far", "near"):
            first, count = groups[kind][c]
            keep, send = down_rows(
                hidden, downs, order, kind == "far", tok_count, first * width, count * width
            )
            keeps[kind, c], gots[kind, c] = keep, swapped(send)
            order = send
        elif kind == "far_sum":
            first, count = groups["far"][c]
            sums = core_sum(keeps["far", c], gots["far", c], factor, order, count, jnp.bfloat16)
            for i, far in enumerate(sums):
                backs[first + i] = [shifted(far[by - 1], -by) for by in range(1, chips)]
            order = sums[0]
        elif kind == "near_sum":
            first, count = groups["near"][c]
            sums = core_sum(keeps["near", c], gots["near", c], factor, order, count, jnp.float32)
            for i, near in enumerate(sums):
                owns[first + i] = near
            order = sums[0]
        elif kind == "arrival":
            backs[0] = [tie(back, order) for back in backs[0]]
            order = backs[0][0]
        else:
            if c == parts - 1 and hop == steps - 1:
                out, order = write_most(result, c * width, order)
                out = last_step(owns[c], backs[c], arrived[c], c * width, start, out, order)
                continue
            send = hop < steps - 1
            *sent, result = chain_step(
                hop, owns[c], backs[c], arrived.get(c), c * width, send, start, result, order
            )
            if send:
                order = sent[0]
                arrived[c] = exchange(sent[0], hop, members, steps)
    return out[None]


def solution(mesh):
    return jax.shard_map(
        shards,
        mesh=mesh,
        in_specs=(
            P("tm", ("copies", "expert"), None),
            P("tm", ("copies", "expert"), None),
            P("tm", ("copies", "expert"), None),
            P(("copies", "tm")),
            P(("copies", "expert"), None),
            P("expert", None, None),
            P("expert", None, None),
            P("expert", None, None),
        ),
        out_specs=P("tm", ("copies", "expert"), None),
        check_vma=False,
    )
```

```python
import functools

import jax
import jax.numpy as jnp
from jax import lax
from jax.experimental import pallas as pl
from jax.experimental.pallas import tpu as pltpu
from jax.sharding import PartitionSpec as P

ANY = pl.BlockSpec(memory_space=pl.ANY)
HBM = pl.BlockSpec(memory_space=pltpu.HBM)
VMEM = pl.BlockSpec(memory_space=pltpu.VMEM)
GRANT = pltpu.CompilerParams(vmem_limit_bytes=7 * 1024 * 1024)
BRIEF = pl.CostEstimate(flops=0, bytes_accessed=0, transcendentals=0)
SMALL = pltpu.CompilerParams(vmem_limit_bytes=2 * 1024 * 1024)


SHARES = (3, 4, 4, 3, 2)
GROUPS = ((0,), (1, 2, 3, 4))
DOWN_TIMES = ((0.0, 1.2, 2.8), (3.0, 5.7, 9.7))
CHAIN_TIMES = ((10.9, 4.8), (14.9, 5.4), (18.2, 5.4), (20.8, 4.7), (23.7, 4.6))


def in_hbm(value):
    return pltpu.with_memory_space_constraint(value, pltpu.HBM)


def slots_of(capacity, blocks):
    return -(-capacity * blocks // 16) * 16


def table_kernel(experts, ids_hbm, probs_hbm, tokens_hbm, table, tokens, ids, probs, sems):
    copy = pltpu.make_async_copy(tokens_hbm.at[0], tokens, sems.at[0])
    smalls = [
        pltpu.make_async_copy(ids_hbm, ids, sems.at[1]),
        pltpu.make_async_copy(probs_hbm, probs, sems.at[2]),
    ]
    copy.start()
    for small in smalls:
        small.start()
    for small in smalls:
        small.wait()
    choices, _, count = ids.shape
    total = probs[0]
    for k in range(1, choices):
        total = total + probs[k]
    names = lax.broadcasted_iota(jnp.int32, table.shape, 0)
    value = jnp.zeros(table.shape, jnp.float32)
    for k in range(choices):
        value = value + jnp.where(ids[k] == names, probs[k] / total, 0.0)
    copy.wait()
    rows = tokens[...].astype(jnp.float32)
    scale = lax.rsqrt(jnp.mean(rows * rows, axis=1, keepdims=True) + 1e-06)
    scale = jnp.broadcast_to(scale, (count, 128)).T[:1]
    table[...] = jnp.where(names == experts, scale, value)


def make_table(ids, probs, tokens, experts):
    count, features = tokens.shape[1:]
    height = -(-(experts + 1) // 8) * 8
    ids, probs = jnp.transpose(ids, (2, 0, 1)), jnp.transpose(probs, (2, 0, 1))
    return pl.pallas_call(
        functools.partial(table_kernel, experts),
        out_shape=(
            pltpu.VMEM((height, count), jnp.float32),
            pltpu.VMEM((count, features), tokens.dtype),
        ),
        in_specs=[HBM] * 3,
        out_specs=(VMEM, VMEM),
        scratch_shapes=[
            pltpu.VMEM(ids.shape, ids.dtype),
            pltpu.VMEM(probs.shape, probs.dtype),
            pltpu.SemaphoreType.DMA((3,)),
        ],
        compiler_params=SMALL,
        name="make_table",
    )(in_hbm(ids), in_hbm(probs), in_hbm(tokens))


def plan(tables, capacity, hots, coefs):
    local, slots, width = hots.shape
    blocks = len(tables)
    count = width // blocks
    experts = local * lax.axis_size("expert")
    first = lax.axis_index("expert") * local
    before = lax.broadcasted_iota(jnp.int32, (count, count), 0)
    after = lax.broadcasted_iota(jnp.int32, (count, count), 1)
    upto = jnp.where(before <= after, 1.0, 0.0).astype(jnp.bfloat16)
    slot_ids = lax.broadcasted_iota(jnp.int32, (slots, width), 0).astype(jnp.float32)
    weights, scales, places = [], [], []
    for b in range(blocks):
        weight = tables[b][pl.ds(first, local), :]
        ones = jnp.where(weight > 0.0, 1.0, 0.0)
        padded = jnp.concatenate([ones, jnp.zeros((-local % 16, count), jnp.float32)], axis=0)
        rank = jnp.dot(padded.astype(jnp.bfloat16), upto, preferred_element_type=jnp.float32)[:local]
        places.append(jnp.where(weight > 0.0, rank + float(b * capacity - 1), -1.0))
        weights.append(weight)
        scales.append(tables[b][pl.ds(experts, 1), :])
    weight = jnp.concatenate(weights, axis=1) if blocks > 1 else weights[0]
    scale = jnp.concatenate(scales, axis=1) if blocks > 1 else scales[0]
    place = jnp.concatenate(places, axis=1) if blocks > 1 else places[0]
    for j in range(local):
        hit = slot_ids == place[j : j + 1, :]
        hots[j] = jnp.where(hit, 1.0, 0.0).astype(jnp.bfloat16)
        coefs[j, :, 0:1] = jnp.sum(jnp.where(hit, scale, 0.0), axis=1, keepdims=True)
        coefs[j, :, 1:2] = jnp.sum(jnp.where(hit, weight[j : j + 1, :], 0.0), axis=1, keepdims=True)


def pack(hots, tokens, rows):
    for j in range(hots.shape[0]):
        rows[j] = jnp.dot(hots[j], tokens, preferred_element_type=jnp.float32).astype(jnp.bfloat16)


def expert_hidden(j, rows, hots, coefs, gates, ups, out_ref, base):
    units = gates.shape[2]
    size = hots.shape[2]
    gate = jnp.dot(rows[j], gates[j], preferred_element_type=jnp.float32)
    up = jnp.dot(rows[j], ups[j], preferred_element_type=jnp.float32)
    scale = coefs[j, :, 0:1]
    weight = coefs[j, :, 1:2]
    g = gate * scale
    h = (g / (1.0 + jnp.exp(-g))) * (up * (scale * weight))
    placed = lax.dot_general(
        hots[j], h.astype(jnp.bfloat16), (((0,), (0,)), ((), ())), preferred_element_type=jnp.float32
    )
    out_ref[pl.ds(base, size), pl.ds(j * units, units)] = placed.astype(jnp.bfloat16)


def near_kernel(capacity, *refs):
    tables, tokens = refs[:2], refs[2:4]
    gate_hbm, up_hbm, hidden, gates, ups = refs[4:9]
    hots, coefs, rows, gate_sem, up_sem = refs[9:]
    local = gates.shape[0]
    copies = []
    for j in range(local):
        copies.append(pltpu.make_async_copy(gate_hbm.at[j], gates.at[j], gate_sem.at[j]))
        copies.append(pltpu.make_async_copy(up_hbm.at[j], ups.at[j], up_sem.at[j]))
    for copy in copies:
        copy.start()
    plan(tables, capacity, hots, coefs)
    pack(hots, jnp.concatenate([t[...] for t in tokens], axis=0), rows)
    for j in range(local):
        copies[2 * j].wait()
        copies[2 * j + 1].wait()
        expert_hidden(j, rows, hots, coefs, gates, ups, hidden, 0)


def near_hidden(tables, tokens, w_gate, w_up, capacity, blocks):
    count, features = tokens[0].shape
    local, _, units = w_gate.shape
    slots = slots_of(capacity, 2)
    return pl.pallas_call(
        functools.partial(near_kernel, capacity),
        out_shape=(
            pltpu.VMEM((blocks * count, local * units), jnp.bfloat16),
            pltpu.VMEM(w_gate.shape, w_gate.dtype),
            pltpu.VMEM(w_up.shape, w_up.dtype),
        ),
        in_specs=[VMEM] * 4 + [HBM] * 2,
        out_specs=(VMEM,) * 3,
        scratch_shapes=[
            pltpu.VMEM((local, slots, 2 * count), jnp.bfloat16),
            pltpu.VMEM((local, slots, 128), jnp.float32),
            pltpu.VMEM((local, slots, features), jnp.bfloat16),
            pltpu.SemaphoreType.DMA((local,)),
            pltpu.SemaphoreType.DMA((local,)),
        ],
        compiler_params=GRANT,
        cost_estimate=pl.CostEstimate(
            flops=4 * local * slots * features * units,
            bytes_accessed=4 * local * features * units,
            transcendentals=local * slots * units,
        ),
        name="near_hidden",
    )(*tables, *tokens, in_hbm(w_gate), in_hbm(w_up))


def far_plan_kernel(capacity, far_count, *refs):
    tables = refs[:far_count]
    step, _, hots, coefs, factor = refs[far_count:]
    factor[...] = jnp.full(factor.shape, step[0])
    for p in range(far_count // 2):
        plan(tables[2 * p : 2 * p + 2], capacity, hots.at[p], coefs.at[p])


def far_plan(tables, step_size, order, capacity, local):
    pairs = len(tables) // 2
    count = tables[0].shape[1]
    slots = slots_of(capacity, 2)
    return pl.pallas_call(
        functools.partial(far_plan_kernel, capacity, len(tables)),
        out_shape=(
            pltpu.VMEM((pairs, local, slots, 2 * count), jnp.bfloat16),
            pltpu.VMEM((pairs, local, slots, 128), jnp.float32),
            pltpu.VMEM((8, 128), jnp.float32),
        ),
        in_specs=[VMEM] * len(tables) + [pl.BlockSpec(memory_space=pltpu.SMEM), ANY],
        out_specs=(VMEM,) * 3,
        compiler_params=SMALL,
        cost_estimate=BRIEF,
        name="far_plan",
    )(*tables, step_size, order)


def far_kernel(far_count, *refs):
    tokens = refs[:far_count]
    hots, coefs, gates, ups, down_hbm, start_hbm, _, hidden, downs, start, rows, sems = refs[far_count:]
    copies = [
        pltpu.make_async_copy(down_hbm, downs, sems.at[0]),
        pltpu.make_async_copy(start_hbm, start, sems.at[1]),
    ]
    for copy in copies:
        copy.start()
    for p in range(far_count // 2):
        both = jnp.concatenate([tokens[2 * p][...], tokens[2 * p + 1][...]], axis=0)
        pack(hots.at[p], both, rows)
        for j in range(gates.shape[0]):
            expert_hidden(j, rows, hots.at[p], coefs.at[p], gates, ups, hidden, (p + 1) * hots.shape[3])
    for copy in copies:
        copy.wait()


def far_hidden(tokens, hots, coefs, gates, ups, w_down, start_state, hidden):
    pairs, local, slots, size = hots.shape
    features, units = gates.shape[1:]
    return pl.pallas_call(
        functools.partial(far_kernel, len(tokens)),
        out_shape=(
            pltpu.VMEM(hidden.shape, hidden.dtype),
            pltpu.VMEM(w_down.shape, w_down.dtype),
            pltpu.VMEM(start_state.shape, start_state.dtype),
        ),
        in_specs=[VMEM] * (len(tokens) + 4) + [HBM] * 2 + [VMEM],
        out_specs=(VMEM,) * 3,
        scratch_shapes=[
            pltpu.VMEM((local, slots, features), jnp.bfloat16),
            pltpu.SemaphoreType.DMA((2,)),
        ],
        input_output_aliases={len(tokens) + 6: 0},
        compiler_params=GRANT,
        cost_estimate=pl.CostEstimate(
            flops=4 * pairs * local * slots * features * units,
            bytes_accessed=6 * local * features * units,
            transcendentals=pairs * local * slots * units,
        ),
        name="far_hidden",
    )(*tokens, hots, coefs, gates, ups, in_hbm(w_down), in_hbm(start_state), hidden)


def down_kernel(core, start, hidden_ref, down_ref, _, out_ref):
    pairs, count, width = out_ref.shape
    local, units, _ = down_ref.shape
    columns = pl.ds(start, width)
    total = None
    for j in range(local):
        inner = pl.ds(j * units, units)
        parts = [hidden_ref[pl.ds((2 * p + core) * count, count), inner] for p in range(pairs)]
        term = jnp.dot(
            jnp.concatenate(parts, axis=0), down_ref[j, :, columns], preferred_element_type=jnp.float32
        )
        total = term if total is None else total + term
    for p in range(pairs):
        out_ref[p] = total[p * count : (p + 1) * count].astype(out_ref.dtype)


def down_rows(hidden, downs, order, send, count, start, width):
    pairs = hidden.shape[0] // (2 * count)
    return pl.pallas_call(
        functools.partial(down_kernel, int(send), start),
        out_shape=pltpu.VMEM((pairs, count, width), jnp.bfloat16 if send else jnp.float32),
        in_specs=[VMEM, VMEM, ANY],
        out_specs=VMEM,
        compiler_params=GRANT,
        cost_estimate=BRIEF,
        name="down_rows",
    )(hidden, downs, order)


def core_sum_kernel(widths, keep, got, factor, _, *outs):
    step = factor[0:1, 0:1]
    first = 0
    for n, width in enumerate(widths):
        columns = pl.ds(first, width)
        first += width
        for p in range(keep.shape[0]):
            total = step * (keep[p, :, columns] + got[p, :, columns].astype(jnp.float32))
            if p == 0:
                outs[2 * n][...] = total
            else:
                outs[2 * n + 1][p - 1] = total.astype(jnp.bfloat16)


def core_sum(keep, got, factor, order, widths):
    pairs, count, _ = keep.shape
    shapes = []
    for width in widths:
        shapes.append(pltpu.VMEM((count, width), jnp.float32))
        shapes.append(pltpu.VMEM((pairs - 1, count, width), jnp.bfloat16))
    return pl.pallas_call(
        functools.partial(core_sum_kernel, widths),
        out_shape=tuple(shapes),
        in_specs=[VMEM, VMEM, VMEM, ANY],
        out_specs=(VMEM,) * len(shapes),
        compiler_params=SMALL,
        cost_estimate=BRIEF,
        name="core_sum",
    )(keep, got, factor, order)


def chain_kernel(hop, backs, first, send, start, _, own, *refs):
    outs = refs[len(refs) - 1 - send :]
    result, width = outs[-1], own.shape[1]

    @pl.when(lax.axis_index("tm") == hop)
    def _():
        total = own[...]
        for ref in refs[: backs + (hop > 0)]:
            total = total + ref[...].astype(jnp.float32)
        if send:
            outs[0][...] = total.astype(jnp.bfloat16)
        columns = pl.ds(first, width)
        result[:, columns] = start[:, columns] + total


def chain_step(hop, own, backs, got, first, send, start, result, order):
    inputs = [start, order, own, *backs] + ([] if got is None else [got]) + ([] if result is None else [result])
    return pl.pallas_call(
        functools.partial(chain_kernel, hop, len(backs), first, int(send)),
        out_shape=((pltpu.VMEM(own.shape, jnp.bfloat16),) if send else ())
        + (pltpu.VMEM(start.shape, jnp.float32),),
        in_specs=[VMEM, ANY] + [VMEM] * (len(inputs) - 2),
        out_specs=(VMEM,) * (1 + send),
        input_output_aliases={} if result is None else {len(inputs) - 1: int(send)},
        compiler_params=SMALL,
        cost_estimate=BRIEF,
        name="chain_step",
    )(*inputs)


def write_kernel(first, result, _, out, mark, sems):
    mark[...] = jnp.zeros_like(mark)
    last = lax.axis_index("tm") == lax.axis_size("tm") - 1
    head, tail = pl.ds(0, first), pl.ds(first, result.shape[1] - first)
    copies = [pltpu.make_async_copy(result.at[:, part], out.at[:, part], sems.at[i]) for i, part in enumerate((head, tail))]
    copies[0].start()

    @pl.when(jnp.logical_not(last))
    def _():
        copies[1].start()
        copies[1].wait()

    copies[0].wait()


def write_most(result, first, order):
    return pl.pallas_call(
        functools.partial(write_kernel, first),
        out_shape=(pltpu.HBM(result.shape, result.dtype), pltpu.VMEM((8, 128), jnp.float32)),
        in_specs=[VMEM, ANY],
        out_specs=(HBM, VMEM),
        scratch_shapes=[pltpu.SemaphoreType.DMA((2,))],
        compiler_params=SMALL,
        cost_estimate=BRIEF,
        name="write_most",
    )(result, order)


def last_kernel(first, backs, start, _, own, *refs):
    out, block, sem = refs[-3:]

    @pl.when(lax.axis_index("tm") == lax.axis_size("tm") - 1)
    def _():
        columns = pl.ds(first, own.shape[1])
        total = start[:, columns] + own[...]
        for ref in refs[: backs + 1]:
            total = total + ref[...].astype(jnp.float32)
        block[...] = total
        copy = pltpu.make_async_copy(block, out.at[:, columns], sem)
        copy.start()
        copy.wait()


def last_step(own, backs, got, first, start, out, order):
    inputs = [start, order, own, *backs, got, out]
    return pl.pallas_call(
        functools.partial(last_kernel, first, len(backs)),
        out_shape=pltpu.HBM(out.shape, out.dtype),
        in_specs=[VMEM, ANY] + [VMEM] * (len(inputs) - 3) + [HBM],
        out_specs=HBM,
        scratch_shapes=[pltpu.VMEM(own.shape, jnp.float32), pltpu.SemaphoreType.DMA],
        input_output_aliases={len(inputs) - 1: 0},
        compiler_params=SMALL,
        cost_estimate=BRIEF,
        name="last_step",
    )(*inputs)


def tie_kernel(value_ref, order_ref, out_ref):
    pass


def tie(value, order):
    return pl.pallas_call(
        tie_kernel,
        out_shape=jax.ShapeDtypeStruct(value.shape, value.dtype),
        in_specs=[ANY, ANY],
        out_specs=ANY,
        input_output_aliases={0: 0},
        compiler_params=SMALL,
        cost_estimate=BRIEF,
        name="tie",
    )(value, order)


def exchange(value, low, members, steps):
    pairs = []
    for e in range(members):
        for z in range(steps):
            if z in (low, low + 1):
                pairs.append((e * steps + z, e * steps + 2 * low + 1 - z))
            else:
                pairs.append((e * steps + z, (e ^ 1) * steps + z))
    return lax.ppermute(value, ("expert", "tm"), pairs)


def shards(tokens, route_ids, route_probs, step_size, start_state, w_gate, w_up, w_down):
    members = lax.axis_size("expert")
    steps = lax.axis_size("tm")
    tok_count, feature_count = tokens.shape[1:]
    topk_count = route_ids.shape[2]
    expert_total = w_gate.shape[0] * members
    capacity = 3 * tok_count * topk_count // (2 * expert_total)
    chips = members // 2

    def swapped(value):
        return lax.ppermute(value, "expert", [(i, i ^ 1) for i in range(members)])

    def shifted(value, by):
        return lax.ppermute(value, "expert", [(i, (i + 2 * by) % members) for i in range(members)])

    own = tokens[0]
    far_same = [shifted(own, by) for by in range(1, chips)]
    partner = swapped(own)
    table, own = make_table(route_ids, route_probs, tokens, expert_total)
    far_table = [shifted(table, by) for by in range(1, chips)]
    hidden, gates, ups = near_hidden([table, swapped(table)], [own, partner], w_gate, w_up, capacity, members)
    far_tables, far_tokens = [], []
    for value, piece in zip(far_table, far_same):
        value = tie(value, hidden)
        piece = tie(piece, value)
        far_tables += [value, swapped(value)]
        far_tokens += [piece, swapped(piece)]
    hots, coefs, factor = far_plan(far_tables, step_size, hidden, capacity, w_gate.shape[0])
    hidden, downs, start = far_hidden(far_tokens, hots, coefs, gates, ups, w_down, start_state, hidden)

    widths = [feature_count * share // 16 for share in SHARES]
    parts = len(widths)
    firsts = [sum(widths[:c]) for c in range(parts)]
    events = []
    for g, times in enumerate(DOWN_TIMES):
        for kind, ready in zip(("send", "keep", "core"), times):
            events.append((ready, kind, g, 0))
    for c, times in enumerate(CHAIN_TIMES):
        for hop in range(steps):
            events.append((times[0] + times[1] * hop, "chain", c, hop))
    events.append((max(events)[0] + 1.0,) + events.pop()[1:])
    order, result = hidden, None
    gots, keeps, owns, backs, arrived = {}, {}, {}, {}, {}
    for _, kind, c, hop in sorted(events):
        if kind in ("send", "keep"):
            group = GROUPS[c]
            width = sum(widths[i] for i in group)
            part = down_rows(hidden, downs, order, kind == "send", tok_count, firsts[group[0]], width)
            if kind == "send":
                gots[c] = swapped(part)
            else:
                keeps[c] = part
            order = part
        elif kind == "core":
            group = GROUPS[c]
            sums = core_sum(keeps[c], gots[c], factor, order, [widths[i] for i in group])
            for n, i in enumerate(group):
                owns[i] = sums[2 * n]
                backs[i] = [shifted(sums[2 * n + 1][by - 1], -by) for by in range(1, chips)]
            order = sums[0]
        else:
            if c == parts - 1 and hop == steps - 1:
                out, order = write_most(result, firsts[c], order)
                out = last_step(owns[c], backs[c], arrived[c], firsts[c], start, out, order)
                continue
            send = hop < steps - 1
            *sent, result = chain_step(
                hop, owns[c], backs[c], arrived.get(c), firsts[c], send, start, result, order
            )
            if send:
                order = sent[0]
                arrived[c] = exchange(sent[0], hop, members, steps)
    return out[None]


def solution(mesh):
    return jax.shard_map(
        shards,
        mesh=mesh,
        in_specs=(
            P("tm", ("copies", "expert"), None),
            P("tm", ("copies", "expert"), None),
            P("tm", ("copies", "expert"), None),
            P(("copies", "tm")),
            P(("copies", "expert"), None),
            P("expert", None, None),
            P("expert", None, None),
            P("expert", None, None),
        ),
        out_specs=P("tm", ("copies", "expert"), None),
        check_vma=False,
    )
```

```python
import functools

import jax
import jax.numpy as jnp
from jax import lax
from jax.experimental import pallas as pl
from jax.experimental.pallas import tpu as pltpu
from jax.sharding import PartitionSpec as P

ANY = pl.BlockSpec(memory_space=pl.ANY)
HBM = pl.BlockSpec(memory_space=pltpu.HBM)
VMEM = pl.BlockSpec(memory_space=pltpu.VMEM)
GRANT = pltpu.CompilerParams(vmem_limit_bytes=7 * 1024 * 1024)
BRIEF = pl.CostEstimate(flops=0, bytes_accessed=0, transcendentals=0)
SMALL = pltpu.CompilerParams(vmem_limit_bytes=2 * 1024 * 1024)


FAR_TIMES = ((0.0, 4.05), (1.0, 4.1), (2.0, 4.15), (3.0, 4.2))
NEAR_TIMES = ((6.0, 10.6), (7.0, 10.65), (11.0, 16.0), (12.0, 16.1))
ARRIVAL = 10.5
CHAIN_TIMES = ((10.9, 5.0), (14.0, 5.0), (17.3, 5.0), (20.6, 5.0))


def in_hbm(value):
    return pltpu.with_memory_space_constraint(value, pltpu.HBM)


def slots_of(capacity, blocks):
    return -(-capacity * blocks // 16) * 16


def table_kernel(experts, ids_hbm, probs_hbm, tokens_hbm, table, tokens, ids, probs, sems):
    copy = pltpu.make_async_copy(tokens_hbm.at[0], tokens, sems.at[0])
    smalls = [
        pltpu.make_async_copy(ids_hbm, ids, sems.at[1]),
        pltpu.make_async_copy(probs_hbm, probs, sems.at[2]),
    ]
    copy.start()
    for small in smalls:
        small.start()
    for small in smalls:
        small.wait()
    choices, _, count = ids.shape
    total = probs[0]
    for k in range(1, choices):
        total = total + probs[k]
    names = lax.broadcasted_iota(jnp.int32, table.shape, 0)
    value = jnp.zeros(table.shape, jnp.float32)
    for k in range(choices):
        value = value + jnp.where(ids[k] == names, probs[k] / total, 0.0)
    copy.wait()
    rows = tokens[...].astype(jnp.float32)
    scale = lax.rsqrt(jnp.mean(rows * rows, axis=1, keepdims=True) + 1e-06)
    scale = jnp.broadcast_to(scale, (count, 128)).T[:1]
    table[...] = jnp.where(names == experts, scale, value)


def make_table(ids, probs, tokens, experts):
    count, features = tokens.shape[1:]
    height = -(-(experts + 1) // 8) * 8
    ids, probs = jnp.transpose(ids, (2, 0, 1)), jnp.transpose(probs, (2, 0, 1))
    return pl.pallas_call(
        functools.partial(table_kernel, experts),
        out_shape=(
            pltpu.VMEM((height, count), jnp.float32),
            pltpu.VMEM((count, features), tokens.dtype),
        ),
        in_specs=[HBM] * 3,
        out_specs=(VMEM, VMEM),
        scratch_shapes=[
            pltpu.VMEM(ids.shape, ids.dtype),
            pltpu.VMEM(probs.shape, probs.dtype),
            pltpu.SemaphoreType.DMA((3,)),
        ],
        compiler_params=SMALL,
        name="make_table",
    )(in_hbm(ids), in_hbm(probs), in_hbm(tokens))


def plan(tables, capacity, hots, coefs):
    local, slots, width = hots.shape
    blocks = len(tables)
    count = width // blocks
    experts = local * lax.axis_size("expert")
    first = lax.axis_index("expert") * local
    before = lax.broadcasted_iota(jnp.int32, (count, count), 0)
    after = lax.broadcasted_iota(jnp.int32, (count, count), 1)
    upto = jnp.where(before <= after, 1.0, 0.0).astype(jnp.bfloat16)
    slot_ids = lax.broadcasted_iota(jnp.int32, (slots, width), 0).astype(jnp.float32)
    weights, scales, places = [], [], []
    for b in range(blocks):
        weight = tables[b][pl.ds(first, local), :]
        ones = jnp.where(weight > 0.0, 1.0, 0.0)
        padded = jnp.concatenate([ones, jnp.zeros((-local % 16, count), jnp.float32)], axis=0)
        rank = jnp.dot(padded.astype(jnp.bfloat16), upto, preferred_element_type=jnp.float32)[:local]
        places.append(jnp.where(weight > 0.0, rank + float(b * capacity - 1), -1.0))
        weights.append(weight)
        scales.append(tables[b][pl.ds(experts, 1), :])
    weight = jnp.concatenate(weights, axis=1) if blocks > 1 else weights[0]
    scale = jnp.concatenate(scales, axis=1) if blocks > 1 else scales[0]
    place = jnp.concatenate(places, axis=1) if blocks > 1 else places[0]
    for j in range(local):
        hit = slot_ids == place[j : j + 1, :]
        hots[j] = jnp.where(hit, 1.0, 0.0).astype(jnp.bfloat16)
        coefs[j, :, 0:1] = jnp.sum(jnp.where(hit, scale, 0.0), axis=1, keepdims=True)
        coefs[j, :, 1:2] = jnp.sum(jnp.where(hit, weight[j : j + 1, :], 0.0), axis=1, keepdims=True)


def pack(hots, tokens, rows):
    for j in range(hots.shape[0]):
        rows[j] = jnp.dot(hots[j], tokens, preferred_element_type=jnp.float32).astype(jnp.bfloat16)


def expert_hidden(j, rows, hots, coefs, gates, ups, out_ref, base):
    units = gates.shape[2]
    size = hots.shape[2]
    gate = jnp.dot(rows[j], gates[j], preferred_element_type=jnp.float32)
    up = jnp.dot(rows[j], ups[j], preferred_element_type=jnp.float32)
    scale = coefs[j, :, 0:1]
    weight = coefs[j, :, 1:2]
    g = gate * scale
    h = (g / (1.0 + jnp.exp(-g))) * (up * (scale * weight))
    placed = lax.dot_general(
        hots[j], h.astype(jnp.bfloat16), (((0,), (0,)), ((), ())), preferred_element_type=jnp.float32
    )
    out_ref[pl.ds(base, size), pl.ds(j * units, units)] = placed.astype(jnp.bfloat16)


def near_kernel(capacity, *refs):
    tables, tokens = refs[:2], refs[2:4]
    gate_hbm, up_hbm, hidden, gates, ups = refs[4:9]
    hots, coefs, rows, gate_sem, up_sem = refs[9:]
    local = gates.shape[0]
    copies = []
    for j in range(local):
        copies.append(pltpu.make_async_copy(gate_hbm.at[j], gates.at[j], gate_sem.at[j]))
        copies.append(pltpu.make_async_copy(up_hbm.at[j], ups.at[j], up_sem.at[j]))
    for copy in copies:
        copy.start()
    plan(tables, capacity, hots, coefs)
    pack(hots, jnp.concatenate([t[...] for t in tokens], axis=0), rows)
    for j in range(local):
        copies[2 * j].wait()
        copies[2 * j + 1].wait()
        expert_hidden(j, rows, hots, coefs, gates, ups, hidden, 0)


def near_hidden(tables, tokens, w_gate, w_up, capacity, blocks):
    count, features = tokens[0].shape
    local, _, units = w_gate.shape
    slots = slots_of(capacity, 2)
    return pl.pallas_call(
        functools.partial(near_kernel, capacity),
        out_shape=(
            pltpu.VMEM((blocks * count, local * units), jnp.bfloat16),
            pltpu.VMEM(w_gate.shape, w_gate.dtype),
            pltpu.VMEM(w_up.shape, w_up.dtype),
        ),
        in_specs=[VMEM] * 4 + [HBM] * 2,
        out_specs=(VMEM,) * 3,
        scratch_shapes=[
            pltpu.VMEM((local, slots, 2 * count), jnp.bfloat16),
            pltpu.VMEM((local, slots, 128), jnp.float32),
            pltpu.VMEM((local, slots, features), jnp.bfloat16),
            pltpu.SemaphoreType.DMA((local,)),
            pltpu.SemaphoreType.DMA((local,)),
        ],
        compiler_params=GRANT,
        cost_estimate=pl.CostEstimate(
            flops=4 * local * slots * features * units,
            bytes_accessed=4 * local * features * units,
            transcendentals=local * slots * units,
        ),
        name="near_hidden",
    )(*tables, *tokens, in_hbm(w_gate), in_hbm(w_up))


def far_plan_kernel(capacity, far_count, *refs):
    tables = refs[:far_count]
    step, _, hots, coefs, factor = refs[far_count:]
    factor[...] = jnp.full(factor.shape, step[0])
    for p in range(far_count // 2):
        plan(tables[2 * p : 2 * p + 2], capacity, hots.at[p], coefs.at[p])


def far_plan(tables, step_size, order, capacity, local):
    pairs = len(tables) // 2
    count = tables[0].shape[1]
    slots = slots_of(capacity, 2)
    return pl.pallas_call(
        functools.partial(far_plan_kernel, capacity, len(tables)),
        out_shape=(
            pltpu.VMEM((pairs, local, slots, 2 * count), jnp.bfloat16),
            pltpu.VMEM((pairs, local, slots, 128), jnp.float32),
            pltpu.VMEM((8, 128), jnp.float32),
        ),
        in_specs=[VMEM] * len(tables) + [pl.BlockSpec(memory_space=pltpu.SMEM), ANY],
        out_specs=(VMEM,) * 3,
        compiler_params=SMALL,
        cost_estimate=BRIEF,
        name="far_plan",
    )(*tables, step_size, order)


def far_kernel(far_count, *refs):
    tokens = refs[:far_count]
    hots, coefs, gates, ups, down_hbm, start_hbm, _, hidden, downs, start, rows, sems = refs[far_count:]
    copies = [
        pltpu.make_async_copy(down_hbm, downs, sems.at[0]),
        pltpu.make_async_copy(start_hbm, start, sems.at[1]),
    ]
    for copy in copies:
        copy.start()
    for p in range(far_count // 2):
        both = jnp.concatenate([tokens[2 * p][...], tokens[2 * p + 1][...]], axis=0)
        pack(hots.at[p], both, rows)
        for j in range(gates.shape[0]):
            expert_hidden(j, rows, hots.at[p], coefs.at[p], gates, ups, hidden, (p + 1) * hots.shape[3])
    for copy in copies:
        copy.wait()


def far_hidden(tokens, hots, coefs, gates, ups, w_down, start_state, hidden):
    pairs, local, slots, size = hots.shape
    features, units = gates.shape[1:]
    return pl.pallas_call(
        functools.partial(far_kernel, len(tokens)),
        out_shape=(
            pltpu.VMEM(hidden.shape, hidden.dtype),
            pltpu.VMEM(w_down.shape, w_down.dtype),
            pltpu.VMEM(start_state.shape, start_state.dtype),
        ),
        in_specs=[VMEM] * (len(tokens) + 4) + [HBM] * 2 + [VMEM],
        out_specs=(VMEM,) * 3,
        scratch_shapes=[
            pltpu.VMEM((local, slots, features), jnp.bfloat16),
            pltpu.SemaphoreType.DMA((2,)),
        ],
        input_output_aliases={len(tokens) + 6: 0},
        compiler_params=GRANT,
        cost_estimate=pl.CostEstimate(
            flops=4 * pairs * local * slots * features * units,
            bytes_accessed=6 * local * features * units,
            transcendentals=pairs * local * slots * units,
        ),
        name="far_hidden",
    )(*tokens, hots, coefs, gates, ups, in_hbm(w_down), in_hbm(start_state), hidden)


def down_kernel(first_pair, start, hidden_ref, down_ref, _, keep, send):
    pairs, count, width = keep.shape
    local, units, _ = down_ref.shape
    rows, columns = pl.ds(2 * first_pair * count, 2 * pairs * count), pl.ds(start, width)
    total = None
    for j in range(local):
        term = jnp.dot(
            hidden_ref[rows, pl.ds(j * units, units)], down_ref[j, :, columns], preferred_element_type=jnp.float32
        )
        total = term if total is None else total + term
    for p in range(pairs):
        keep[p] = total[2 * p * count : (2 * p + 1) * count]
        send[p] = total[(2 * p + 1) * count : (2 * p + 2) * count].astype(jnp.bfloat16)


def down_rows(hidden, downs, order, far, count, start, width):
    pairs = hidden.shape[0] // (2 * count) - 1 if far else 1
    return pl.pallas_call(
        functools.partial(down_kernel, int(far), start),
        out_shape=(
            pltpu.VMEM((pairs, count, width), jnp.float32),
            pltpu.VMEM((pairs, count, width), jnp.bfloat16),
        ),
        in_specs=[VMEM, VMEM, ANY],
        out_specs=(VMEM, VMEM),
        compiler_params=GRANT,
        cost_estimate=BRIEF,
        name="far_down" if far else "near_down",
    )(hidden, downs, order)


def core_sum_kernel(keep, got, factor, _, *outs):
    step = factor[0:1, 0:1]
    first = 0
    for out in outs:
        columns = pl.ds(first, out.shape[2])
        first += out.shape[2]
        for p in range(out.shape[0]):
            total = step * (keep[p, :, columns] + got[p, :, columns].astype(jnp.float32))
            out[p] = total.astype(out.dtype)


def core_sum(keep, got, factor, order, chunks, dtype):
    pairs, count, width = keep.shape
    return pl.pallas_call(
        core_sum_kernel,
        out_shape=(pltpu.VMEM((pairs, count, width // chunks), dtype),) * chunks,
        in_specs=[VMEM, VMEM, VMEM, ANY],
        out_specs=(VMEM,) * chunks,
        compiler_params=SMALL,
        cost_estimate=BRIEF,
        name="core_sum",
    )(keep, got, factor, order)


def chain_kernel(hop, backs, first, send, start, _, own, *refs):
    outs = refs[len(refs) - 1 - send :]
    result, width = outs[-1], own.shape[2]

    @pl.when(lax.axis_index("tm") == hop)
    def _():
        total = own[0]
        for ref in refs[: backs + (hop > 0)]:
            total = total + ref[...].astype(jnp.float32)
        if send:
            outs[0][...] = total.astype(jnp.bfloat16)
        columns = pl.ds(first, width)
        result[:, columns] = start[:, columns] + total


def chain_step(hop, own, backs, got, first, send, start, result, order):
    inputs = [start, order, own, *backs] + ([] if got is None else [got]) + ([] if result is None else [result])
    return pl.pallas_call(
        functools.partial(chain_kernel, hop, len(backs), first, int(send)),
        out_shape=((pltpu.VMEM(own.shape[1:], jnp.bfloat16),) if send else ())
        + (pltpu.VMEM(start.shape, jnp.float32),),
        in_specs=[VMEM, ANY] + [VMEM] * (len(inputs) - 2),
        out_specs=(VMEM,) * (1 + send),
        input_output_aliases={} if result is None else {len(inputs) - 1: int(send)},
        compiler_params=SMALL,
        cost_estimate=BRIEF,
        name="chain_step",
    )(*inputs)


def write_kernel(first, result, _, out, mark, sems):
    mark[...] = jnp.zeros_like(mark)
    last = lax.axis_index("tm") == lax.axis_size("tm") - 1
    head, tail = pl.ds(0, first), pl.ds(first, result.shape[1] - first)
    copies = [pltpu.make_async_copy(result.at[:, part], out.at[:, part], sems.at[i]) for i, part in enumerate((head, tail))]
    copies[0].start()

    @pl.when(jnp.logical_not(last))
    def _():
        copies[1].start()
        copies[1].wait()

    copies[0].wait()


def write_most(result, first, order):
    return pl.pallas_call(
        functools.partial(write_kernel, first),
        out_shape=(pltpu.HBM(result.shape, result.dtype), pltpu.VMEM((8, 128), jnp.float32)),
        in_specs=[VMEM, ANY],
        out_specs=(HBM, VMEM),
        scratch_shapes=[pltpu.SemaphoreType.DMA((2,))],
        compiler_params=SMALL,
        cost_estimate=BRIEF,
        name="write_most",
    )(result, order)


def last_kernel(first, backs, start, _, own, *refs):
    out, block, sem = refs[-3:]

    @pl.when(lax.axis_index("tm") == lax.axis_size("tm") - 1)
    def _():
        columns = pl.ds(first, own.shape[2])
        total = start[:, columns] + own[0]
        for ref in refs[: backs + 1]:
            total = total + ref[...].astype(jnp.float32)
        block[...] = total
        copy = pltpu.make_async_copy(block, out.at[:, columns], sem)
        copy.start()
        copy.wait()


def last_step(own, backs, got, first, start, out, order):
    inputs = [start, order, own, *backs, got, out]
    return pl.pallas_call(
        functools.partial(last_kernel, first, len(backs)),
        out_shape=pltpu.HBM(out.shape, out.dtype),
        in_specs=[VMEM, ANY] + [VMEM] * (len(inputs) - 3) + [HBM],
        out_specs=HBM,
        scratch_shapes=[pltpu.VMEM(own.shape[1:], jnp.float32), pltpu.SemaphoreType.DMA],
        input_output_aliases={len(inputs) - 1: 0},
        compiler_params=SMALL,
        cost_estimate=BRIEF,
        name="last_step",
    )(*inputs)


def tie_kernel(value_ref, order_ref, out_ref):
    pass


def tie(value, order):
    return pl.pallas_call(
        tie_kernel,
        out_shape=jax.ShapeDtypeStruct(value.shape, value.dtype),
        in_specs=[ANY, ANY],
        out_specs=ANY,
        input_output_aliases={0: 0},
        compiler_params=SMALL,
        cost_estimate=BRIEF,
        name="tie",
    )(value, order)


def exchange(value, low, members, steps):
    pairs = []
    for e in range(members):
        for z in range(steps):
            if z in (low, low + 1):
                pairs.append((e * steps + z, e * steps + 2 * low + 1 - z))
            else:
                pairs.append((e * steps + z, (e ^ 1) * steps + z))
    return lax.ppermute(value, ("expert", "tm"), pairs)


def shards(tokens, route_ids, route_probs, step_size, start_state, w_gate, w_up, w_down):
    members = lax.axis_size("expert")
    steps = lax.axis_size("tm")
    tok_count, feature_count = tokens.shape[1:]
    topk_count = route_ids.shape[2]
    expert_total = w_gate.shape[0] * members
    capacity = 3 * tok_count * topk_count // (2 * expert_total)
    chips = members // 2

    def swapped(value):
        return lax.ppermute(value, "expert", [(i, i ^ 1) for i in range(members)])

    def shifted(value, by):
        return lax.ppermute(value, "expert", [(i, (i + 2 * by) % members) for i in range(members)])

    own = tokens[0]
    far_same = [shifted(own, by) for by in range(1, chips)]
    partner = swapped(own)
    table, own = make_table(route_ids, route_probs, tokens, expert_total)
    far_table = [shifted(table, by) for by in range(1, chips)]
    hidden, gates, ups = near_hidden([table, swapped(table)], [own, partner], w_gate, w_up, capacity, members)
    far_tables, far_tokens = [], []
    for value, piece in zip(far_table, far_same):
        value = tie(value, hidden)
        piece = tie(piece, value)
        far_tables += [value, swapped(value)]
        far_tokens += [piece, swapped(piece)]
    hots, coefs, factor = far_plan(far_tables, step_size, hidden, capacity, w_gate.shape[0])
    hidden, downs, start = far_hidden(far_tokens, hots, coefs, gates, ups, w_down, start_state, hidden)

    parts = 4
    width = feature_count // parts
    groups = {kind: [(c, 1) for c in range(parts)] for kind in ("far", "near")}
    events = []
    for kind, times in (("far", FAR_TIMES), ("near", NEAR_TIMES)):
        for g, (ready, summed) in enumerate(times):
            events += [(ready, kind, g, 0), (summed, kind + "_sum", g, 0)]
    events.append((ARRIVAL, "arrival", 0, 0))
    for c, (ready, period) in enumerate(CHAIN_TIMES):
        for hop in range(steps):
            events.append((ready + period * hop, "chain", c, hop))
    order, result = hidden, None
    keeps, gots, owns, backs, arrived = {}, {}, {}, {}, {}
    for _, kind, c, hop in sorted(events):
        if kind in ("far", "near"):
            first, count = groups[kind][c]
            keep, send = down_rows(
                hidden, downs, order, kind == "far", tok_count, first * width, count * width
            )
            keeps[kind, c], gots[kind, c] = keep, swapped(send)
            order = send
        elif kind == "far_sum":
            first, count = groups["far"][c]
            sums = core_sum(keeps["far", c], gots["far", c], factor, order, count, jnp.bfloat16)
            for i, far in enumerate(sums):
                backs[first + i] = [shifted(far[by - 1], -by) for by in range(1, chips)]
            order = sums[0]
        elif kind == "near_sum":
            first, count = groups["near"][c]
            sums = core_sum(keeps["near", c], gots["near", c], factor, order, count, jnp.float32)
            for i, near in enumerate(sums):
                owns[first + i] = near
            order = sums[0]
        elif kind == "arrival":
            backs[0] = [tie(back, order) for back in backs[0]]
            order = backs[0][0]
        else:
            if c == parts - 1 and hop == steps - 1:
                out, order = write_most(result, c * width, order)
                out = last_step(owns[c], backs[c], arrived[c], c * width, start, out, order)
                continue
            send = hop < steps - 1
            *sent, result = chain_step(
                hop, owns[c], backs[c], arrived.get(c), c * width, send, start, result, order
            )
            if send:
                order = sent[0]
                arrived[c] = exchange(sent[0], hop, members, steps)
    return out[None]


def solution(mesh):
    return jax.shard_map(
        shards,
        mesh=mesh,
        in_specs=(
            P("tm", ("copies", "expert"), None),
            P("tm", ("copies", "expert"), None),
            P("tm", ("copies", "expert"), None),
            P(("copies", "tm")),
            P(("copies", "expert"), None),
            P("expert", None, None),
            P("expert", None, None),
            P("expert", None, None),
        ),
        out_specs=P("tm", ("copies", "expert"), None),
        check_vma=False,
    )
```

```python
import functools

import jax
import jax.numpy as jnp
from jax import lax
from jax.experimental import pallas as pl
from jax.experimental.pallas import tpu as pltpu
from jax.sharding import PartitionSpec as P

ANY = pl.BlockSpec(memory_space=pl.ANY)
HBM = pl.BlockSpec(memory_space=pltpu.HBM)
VMEM = pl.BlockSpec(memory_space=pltpu.VMEM)
GRANT = pltpu.CompilerParams(vmem_limit_bytes=7 * 1024 * 1024)
BRIEF = pl.CostEstimate(flops=0, bytes_accessed=0, transcendentals=0)
SMALL = pltpu.CompilerParams(vmem_limit_bytes=2 * 1024 * 1024)


def in_hbm(value):
    return pltpu.with_memory_space_constraint(value, pltpu.HBM)


def slots_of(capacity, blocks):
    return -(-capacity * blocks // 16) * 16


def table_kernel(experts, ids_hbm, probs_hbm, tokens_hbm, table, tokens, ids, probs, sems):
    copy = pltpu.make_async_copy(tokens_hbm.at[0], tokens, sems.at[0])
    smalls = [
        pltpu.make_async_copy(ids_hbm, ids, sems.at[1]),
        pltpu.make_async_copy(probs_hbm, probs, sems.at[2]),
    ]
    copy.start()
    for small in smalls:
        small.start()
    for small in smalls:
        small.wait()
    choices, _, count = ids.shape
    total = probs[0]
    for k in range(1, choices):
        total = total + probs[k]
    names = lax.broadcasted_iota(jnp.int32, table.shape, 0)
    value = jnp.zeros(table.shape, jnp.float32)
    for k in range(choices):
        value = value + jnp.where(ids[k] == names, probs[k] / total, 0.0)
    copy.wait()
    rows = tokens[...].astype(jnp.float32)
    scale = lax.rsqrt(jnp.mean(rows * rows, axis=1, keepdims=True) + 1e-06)
    scale = jnp.broadcast_to(scale, (count, 128)).T[:1]
    table[...] = jnp.where(names == experts, scale, value)


def make_table(ids, probs, tokens, experts):
    count, features = tokens.shape[1:]
    height = -(-(experts + 1) // 8) * 8
    ids, probs = jnp.transpose(ids, (2, 0, 1)), jnp.transpose(probs, (2, 0, 1))
    return pl.pallas_call(
        functools.partial(table_kernel, experts),
        out_shape=(
            pltpu.VMEM((height, count), jnp.float32),
            pltpu.VMEM((count, features), tokens.dtype),
        ),
        in_specs=[HBM] * 3,
        out_specs=(VMEM, VMEM),
        scratch_shapes=[
            pltpu.VMEM(ids.shape, ids.dtype),
            pltpu.VMEM(probs.shape, probs.dtype),
            pltpu.SemaphoreType.DMA((3,)),
        ],
        compiler_params=SMALL,
        name="make_table",
    )(in_hbm(ids), in_hbm(probs), in_hbm(tokens))


def plan(tables, capacity, hots, coefs):
    local, slots, width = hots.shape
    blocks = len(tables)
    count = width // blocks
    experts = local * lax.axis_size("expert")
    first = lax.axis_index("expert") * local
    before = lax.broadcasted_iota(jnp.int32, (count, count), 0)
    after = lax.broadcasted_iota(jnp.int32, (count, count), 1)
    upto = jnp.where(before <= after, 1.0, 0.0).astype(jnp.bfloat16)
    slot_ids = lax.broadcasted_iota(jnp.int32, (slots, width), 0).astype(jnp.float32)
    weights, scales, places = [], [], []
    for b in range(blocks):
        weight = tables[b][pl.ds(first, local), :]
        ones = jnp.where(weight > 0.0, 1.0, 0.0)
        padded = jnp.concatenate([ones, jnp.zeros((-local % 16, count), jnp.float32)], axis=0)
        rank = jnp.dot(padded.astype(jnp.bfloat16), upto, preferred_element_type=jnp.float32)[:local]
        places.append(jnp.where(weight > 0.0, rank + float(b * capacity - 1), -1.0))
        weights.append(weight)
        scales.append(tables[b][pl.ds(experts, 1), :])
    weight = jnp.concatenate(weights, axis=1) if blocks > 1 else weights[0]
    scale = jnp.concatenate(scales, axis=1) if blocks > 1 else scales[0]
    place = jnp.concatenate(places, axis=1) if blocks > 1 else places[0]
    for j in range(local):
        hit = slot_ids == place[j : j + 1, :]
        hots[j] = jnp.where(hit, 1.0, 0.0).astype(jnp.bfloat16)
        coefs[j, :, 0:1] = jnp.sum(jnp.where(hit, scale, 0.0), axis=1, keepdims=True)
        coefs[j, :, 1:2] = jnp.sum(jnp.where(hit, weight[j : j + 1, :], 0.0), axis=1, keepdims=True)


def pack(hots, tokens, rows):
    for j in range(hots.shape[0]):
        rows[j] = jnp.dot(hots[j], tokens, preferred_element_type=jnp.float32).astype(jnp.bfloat16)


def expert_hidden(j, rows, hots, coefs, gates, ups, out_ref, base):
    units = gates.shape[2]
    size = hots.shape[2]
    gate = jnp.dot(rows[j], gates[j], preferred_element_type=jnp.float32)
    up = jnp.dot(rows[j], ups[j], preferred_element_type=jnp.float32)
    scale = coefs[j, :, 0:1]
    weight = coefs[j, :, 1:2]
    g = gate * scale
    h = (g / (1.0 + jnp.exp(-g))) * (up * (scale * weight))
    placed = lax.dot_general(
        hots[j], h.astype(jnp.bfloat16), (((0,), (0,)), ((), ())), preferred_element_type=jnp.float32
    )
    out_ref[pl.ds(base, size), pl.ds(j * units, units)] = placed.astype(jnp.bfloat16)


def near_kernel(capacity, *refs):
    tables, tokens = refs[:2], refs[2:4]
    gate_hbm, up_hbm, hidden, gates, ups = refs[4:9]
    hots, coefs, rows, gate_sem, up_sem = refs[9:]
    local = gates.shape[0]
    copies = []
    for j in range(local):
        copies.append(pltpu.make_async_copy(gate_hbm.at[j], gates.at[j], gate_sem.at[j]))
        copies.append(pltpu.make_async_copy(up_hbm.at[j], ups.at[j], up_sem.at[j]))
    for copy in copies:
        copy.start()
    plan(tables, capacity, hots, coefs)
    pack(hots, jnp.concatenate([t[...] for t in tokens], axis=0), rows)
    for j in range(local):
        copies[2 * j].wait()
        copies[2 * j + 1].wait()
        expert_hidden(j, rows, hots, coefs, gates, ups, hidden, 0)


def near_hidden(tables, tokens, w_gate, w_up, capacity, blocks):
    count, features = tokens[0].shape
    local, _, units = w_gate.shape
    slots = slots_of(capacity, 2)
    return pl.pallas_call(
        functools.partial(near_kernel, capacity),
        out_shape=(
            pltpu.VMEM((blocks * count, local * units), jnp.bfloat16),
            pltpu.VMEM(w_gate.shape, w_gate.dtype),
            pltpu.VMEM(w_up.shape, w_up.dtype),
        ),
        in_specs=[VMEM] * 4 + [HBM] * 2,
        out_specs=(VMEM,) * 3,
        scratch_shapes=[
            pltpu.VMEM((local, slots, 2 * count), jnp.bfloat16),
            pltpu.VMEM((local, slots, 128), jnp.float32),
            pltpu.VMEM((local, slots, features), jnp.bfloat16),
            pltpu.SemaphoreType.DMA((local,)),
            pltpu.SemaphoreType.DMA((local,)),
        ],
        compiler_params=GRANT,
        cost_estimate=pl.CostEstimate(
            flops=4 * local * slots * features * units,
            bytes_accessed=4 * local * features * units,
            transcendentals=local * slots * units,
        ),
        name="near_hidden",
    )(*tables, *tokens, in_hbm(w_gate), in_hbm(w_up))


def far_plan_kernel(capacity, far_count, *refs):
    tables = refs[:far_count]
    step, _, hots, coefs, factor = refs[far_count:]
    factor[...] = jnp.full(factor.shape, step[0])
    for p in range(far_count // 2):
        plan(tables[2 * p : 2 * p + 2], capacity, hots.at[p], coefs.at[p])


def far_plan(tables, step_size, order, capacity, local):
    pairs = len(tables) // 2
    count = tables[0].shape[1]
    slots = slots_of(capacity, 2)
    return pl.pallas_call(
        functools.partial(far_plan_kernel, capacity, len(tables)),
        out_shape=(
            pltpu.VMEM((pairs, local, slots, 2 * count), jnp.bfloat16),
            pltpu.VMEM((pairs, local, slots, 128), jnp.float32),
            pltpu.VMEM((8, 128), jnp.float32),
        ),
        in_specs=[VMEM] * len(tables) + [pl.BlockSpec(memory_space=pltpu.SMEM), ANY],
        out_specs=(VMEM,) * 3,
        compiler_params=SMALL,
        cost_estimate=BRIEF,
        name="far_plan",
    )(*tables, step_size, order)


def far_kernel(far_count, *refs):
    tokens = refs[:far_count]
    hots, coefs, gates, ups, down_hbm, start_hbm, _, hidden, downs, start, rows, sems = refs[far_count:]
    copies = [
        pltpu.make_async_copy(down_hbm, downs, sems.at[0]),
        pltpu.make_async_copy(start_hbm, start, sems.at[1]),
    ]
    for copy in copies:
        copy.start()
    for p in range(far_count // 2):
        both = jnp.concatenate([tokens[2 * p][...], tokens[2 * p + 1][...]], axis=0)
        pack(hots.at[p], both, rows)
        for j in range(gates.shape[0]):
            expert_hidden(j, rows, hots.at[p], coefs.at[p], gates, ups, hidden, (p + 1) * hots.shape[3])
    for copy in copies:
        copy.wait()


def far_hidden(tokens, hots, coefs, gates, ups, w_down, start_state, hidden):
    pairs, local, slots, size = hots.shape
    features, units = gates.shape[1:]
    return pl.pallas_call(
        functools.partial(far_kernel, len(tokens)),
        out_shape=(
            pltpu.VMEM(hidden.shape, hidden.dtype),
            pltpu.VMEM(w_down.shape, w_down.dtype),
            pltpu.VMEM(start_state.shape, start_state.dtype),
        ),
        in_specs=[VMEM] * (len(tokens) + 4) + [HBM] * 2 + [VMEM],
        out_specs=(VMEM,) * 3,
        scratch_shapes=[
            pltpu.VMEM((local, slots, features), jnp.bfloat16),
            pltpu.SemaphoreType.DMA((2,)),
        ],
        input_output_aliases={len(tokens) + 6: 0},
        compiler_params=GRANT,
        cost_estimate=pl.CostEstimate(
            flops=4 * pairs * local * slots * features * units,
            bytes_accessed=6 * local * features * units,
            transcendentals=pairs * local * slots * units,
        ),
        name="far_hidden",
    )(*tokens, hots, coefs, gates, ups, in_hbm(w_down), in_hbm(start_state), hidden)


def down_kernel(core, start, hidden_ref, down_ref, _, out_ref):
    pairs, count, width = out_ref.shape
    local, units, _ = down_ref.shape
    columns = pl.ds(start, width)
    total = None
    for j in range(local):
        inner = pl.ds(j * units, units)
        parts = [hidden_ref[pl.ds((2 * p + core) * count, count), inner] for p in range(pairs)]
        term = jnp.dot(
            jnp.concatenate(parts, axis=0), down_ref[j, :, columns], preferred_element_type=jnp.float32
        )
        total = term if total is None else total + term
    for p in range(pairs):
        out_ref[p] = total[p * count : (p + 1) * count].astype(out_ref.dtype)


def down_rows(hidden, downs, order, send, count, start, width):
    pairs = hidden.shape[0] // (2 * count)
    return pl.pallas_call(
        functools.partial(down_kernel, int(send), start),
        out_shape=pltpu.VMEM((pairs, count, width), jnp.bfloat16 if send else jnp.float32),
        in_specs=[VMEM, VMEM, ANY],
        out_specs=VMEM,
        compiler_params=GRANT,
        cost_estimate=BRIEF,
        name="down_rows",
    )(hidden, downs, order)


def core_sum_kernel(chunks, keep, got, factor, _, *outs):
    pairs, _, width = keep.shape
    width = width // chunks
    step = factor[0:1, 0:1]
    for i in range(chunks):
        columns = pl.ds(i * width, width)
        for p in range(pairs):
            total = step * (keep[p, :, columns] + got[p, :, columns].astype(jnp.float32))
            if p == 0:
                outs[2 * i][...] = total
            else:
                outs[2 * i + 1][p - 1] = total.astype(jnp.bfloat16)


def core_sum(keep, got, factor, order, chunks):
    pairs, count, width = keep.shape
    shapes = []
    for _ in range(chunks):
        shapes.append(pltpu.VMEM((count, width // chunks), jnp.float32))
        shapes.append(pltpu.VMEM((pairs - 1, count, width // chunks), jnp.bfloat16))
    return pl.pallas_call(
        functools.partial(core_sum_kernel, chunks),
        out_shape=tuple(shapes),
        in_specs=[VMEM, VMEM, VMEM, ANY],
        out_specs=(VMEM,) * len(shapes),
        compiler_params=SMALL,
        cost_estimate=BRIEF,
        name="core_sum",
    )(keep, got, factor, order)


def chain_kernel(hop, backs, first, send, start, _, own, *refs):
    outs = refs[len(refs) - 1 - send :]
    result, width = outs[-1], own.shape[1]

    @pl.when(lax.axis_index("tm") == hop)
    def _():
        total = own[...]
        for ref in refs[: backs + (hop > 0)]:
            total = total + ref[...].astype(jnp.float32)
        if send:
            outs[0][...] = total.astype(jnp.bfloat16)
        columns = pl.ds(first, width)
        result[:, columns] = start[:, columns] + total


def chain_step(hop, own, backs, got, first, send, start, result, order):
    inputs = [start, order, own, *backs] + ([] if got is None else [got]) + ([] if result is None else [result])
    return pl.pallas_call(
        functools.partial(chain_kernel, hop, len(backs), first, int(send)),
        out_shape=((pltpu.VMEM(own.shape, jnp.bfloat16),) if send else ())
        + (pltpu.VMEM(start.shape, jnp.float32),),
        in_specs=[VMEM, ANY] + [VMEM] * (len(inputs) - 2),
        out_specs=(VMEM,) * (1 + send),
        input_output_aliases={} if result is None else {len(inputs) - 1: int(send)},
        compiler_params=SMALL,
        cost_estimate=BRIEF,
        name="chain_step",
    )(*inputs)


def write_kernel(first, result, _, out, mark, sems):
    mark[...] = jnp.zeros_like(mark)
    last = lax.axis_index("tm") == lax.axis_size("tm") - 1
    head, tail = pl.ds(0, first), pl.ds(first, result.shape[1] - first)
    copies = [pltpu.make_async_copy(result.at[:, part], out.at[:, part], sems.at[i]) for i, part in enumerate((head, tail))]
    copies[0].start()

    @pl.when(jnp.logical_not(last))
    def _():
        copies[1].start()
        copies[1].wait()

    copies[0].wait()


def write_most(result, first, order):
    return pl.pallas_call(
        functools.partial(write_kernel, first),
        out_shape=(pltpu.HBM(result.shape, result.dtype), pltpu.VMEM((8, 128), jnp.float32)),
        in_specs=[VMEM, ANY],
        out_specs=(HBM, VMEM),
        scratch_shapes=[pltpu.SemaphoreType.DMA((2,))],
        compiler_params=SMALL,
        cost_estimate=BRIEF,
        name="write_most",
    )(result, order)


def last_kernel(first, backs, start, _, own, *refs):
    out, block, sem = refs[-3:]

    @pl.when(lax.axis_index("tm") == lax.axis_size("tm") - 1)
    def _():
        columns = pl.ds(first, own.shape[1])
        total = start[:, columns] + own[...]
        for ref in refs[: backs + 1]:
            total = total + ref[...].astype(jnp.float32)
        block[...] = total
        copy = pltpu.make_async_copy(block, out.at[:, columns], sem)
        copy.start()
        copy.wait()


def last_step(own, backs, got, first, start, out, order):
    inputs = [start, order, own, *backs, got, out]
    return pl.pallas_call(
        functools.partial(last_kernel, first, len(backs)),
        out_shape=pltpu.HBM(out.shape, out.dtype),
        in_specs=[VMEM, ANY] + [VMEM] * (len(inputs) - 3) + [HBM],
        out_specs=HBM,
        scratch_shapes=[pltpu.VMEM(own.shape, jnp.float32), pltpu.SemaphoreType.DMA],
        input_output_aliases={len(inputs) - 1: 0},
        compiler_params=SMALL,
        cost_estimate=BRIEF,
        name="last_step",
    )(*inputs)


def tie_kernel(value_ref, order_ref, out_ref):
    pass


def tie(value, order):
    return pl.pallas_call(
        tie_kernel,
        out_shape=jax.ShapeDtypeStruct(value.shape, value.dtype),
        in_specs=[ANY, ANY],
        out_specs=ANY,
        input_output_aliases={0: 0},
        compiler_params=SMALL,
        cost_estimate=BRIEF,
        name="tie",
    )(value, order)


def exchange(value, low, members, steps):
    pairs = []
    for e in range(members):
        for z in range(steps):
            if z in (low, low + 1):
                pairs.append((e * steps + z, e * steps + 2 * low + 1 - z))
            else:
                pairs.append((e * steps + z, (e ^ 1) * steps + z))
    return lax.ppermute(value, ("expert", "tm"), pairs)


def shards(tokens, route_ids, route_probs, step_size, start_state, w_gate, w_up, w_down):
    members = lax.axis_size("expert")
    steps = lax.axis_size("tm")
    tok_count, feature_count = tokens.shape[1:]
    topk_count = route_ids.shape[2]
    expert_total = w_gate.shape[0] * members
    capacity = 3 * tok_count * topk_count // (2 * expert_total)
    chips = members // 2

    def swapped(value):
        return lax.ppermute(value, "expert", [(i, i ^ 1) for i in range(members)])

    def shifted(value, by):
        return lax.ppermute(value, "expert", [(i, (i + 2 * by) % members) for i in range(members)])

    own = tokens[0]
    far_same = [shifted(own, by) for by in range(1, chips)]
    partner = swapped(own)
    table, own = make_table(route_ids, route_probs, tokens, expert_total)
    far_table = [shifted(table, by) for by in range(1, chips)]
    hidden, gates, ups = near_hidden([table, swapped(table)], [own, partner], w_gate, w_up, capacity, members)
    far_tables, far_tokens = [], []
    for value, piece in zip(far_table, far_same):
        value = tie(value, hidden)
        piece = tie(piece, value)
        far_tables += [value, swapped(value)]
        far_tokens += [piece, swapped(piece)]
    hots, coefs, factor = far_plan(far_tables, step_size, hidden, capacity, w_gate.shape[0])
    hidden, downs, start = far_hidden(far_tokens, hots, coefs, gates, ups, w_down, start_state, hidden)

    parts = 4
    width = feature_count // parts
    groups = [(0, 1), (1, parts - 1)]
    events, ready = [], 0.0
    for g, (_, count) in enumerate(groups):
        events.append((ready, "send", g, 0))
        events.append((ready + 0.9 * count, "keep", g, 0))
        ready += max(2.5, 1.8 * count)
        events.append((ready, "core", g, 0))
    for c in range(parts):
        for hop in range(steps):
            ready = (12.0, 15.3, 18.6, 20.2)[min(c, 3)]
            events.append((ready + 5.0 * hop, "chain", c, hop))
    order, result = hidden, None
    gots, keeps, owns, backs, arrived = {}, {}, {}, {}, {}
    for _, kind, c, hop in sorted(events):
        if kind in ("send", "keep"):
            first, count = groups[c]
            part = down_rows(hidden, downs, order, kind == "send", tok_count, first * width, count * width)
            if kind == "send":
                gots[c] = swapped(part)
            else:
                keeps[c] = part
            order = part
        elif kind == "core":
            first, count = groups[c]
            sums = core_sum(keeps[c], gots[c], factor, order, count)
            for i in range(count):
                owns[first + i] = sums[2 * i]
                backs[first + i] = [shifted(sums[2 * i + 1][by - 1], -by) for by in range(1, chips)]
            order = sums[0]
        else:
            if c == parts - 1 and hop == steps - 1:
                out, order = write_most(result, c * width, order)
                out = last_step(owns[c], backs[c], arrived[c], c * width, start, out, order)
                continue
            send = hop < steps - 1
            *sent, result = chain_step(
                hop, owns[c], backs[c], arrived.get(c), c * width, send, start, result, order
            )
            if send:
                order = sent[0]
                arrived[c] = exchange(sent[0], hop, members, steps)
    return out[None]


def solution(mesh):
    return jax.shard_map(
        shards,
        mesh=mesh,
        in_specs=(
            P("tm", ("copies", "expert"), None),
            P("tm", ("copies", "expert"), None),
            P("tm", ("copies", "expert"), None),
            P(("copies", "tm")),
            P(("copies", "expert"), None),
            P("expert", None, None),
            P("expert", None, None),
            P("expert", None, None),
        ),
        out_specs=P("tm", ("copies", "expert"), None),
        check_vma=False,
    )
```

```python
import functools

import jax
import jax.numpy as jnp
from jax import lax
from jax.experimental import pallas as pl
from jax.experimental.pallas import tpu as pltpu
from jax.sharding import PartitionSpec as P

ANY = pl.BlockSpec(memory_space=pl.ANY)
HBM = pl.BlockSpec(memory_space=pltpu.HBM)
VMEM = pl.BlockSpec(memory_space=pltpu.VMEM)
GRANT = pltpu.CompilerParams(vmem_limit_bytes=7 * 1024 * 1024)
BRIEF = pl.CostEstimate(flops=0, bytes_accessed=0, transcendentals=0)
SMALL = pltpu.CompilerParams(vmem_limit_bytes=2 * 1024 * 1024)


SHARES = (5, 6, 5)
GROUPS = ((0,), (1, 2))
DOWN_TIMES = ((0.0, 1.4, 3.0), (3.2, 5.7, 9.4))
CHAIN_TIMES = ((12.6, 6.5, 6.5), (17.7, 7.0, 7.0), (22.0, 6.5, 6.5))


def in_hbm(value):
    return pltpu.with_memory_space_constraint(value, pltpu.HBM)


def slots_of(capacity, blocks):
    return -(-capacity * blocks // 16) * 16


def table_kernel(experts, ids_hbm, probs_hbm, tokens_hbm, table, tokens, ids, probs, sems):
    copy = pltpu.make_async_copy(tokens_hbm.at[0], tokens, sems.at[0])
    smalls = [
        pltpu.make_async_copy(ids_hbm, ids, sems.at[1]),
        pltpu.make_async_copy(probs_hbm, probs, sems.at[2]),
    ]
    copy.start()
    for small in smalls:
        small.start()
    for small in smalls:
        small.wait()
    choices, _, count = ids.shape
    total = probs[0]
    for k in range(1, choices):
        total = total + probs[k]
    names = lax.broadcasted_iota(jnp.int32, table.shape, 0)
    value = jnp.zeros(table.shape, jnp.float32)
    for k in range(choices):
        value = value + jnp.where(ids[k] == names, probs[k] / total, 0.0)
    copy.wait()
    rows = tokens[...].astype(jnp.float32)
    scale = lax.rsqrt(jnp.mean(rows * rows, axis=1, keepdims=True) + 1e-06)
    scale = jnp.broadcast_to(scale, (count, 128)).T[:1]
    table[...] = jnp.where(names == experts, scale, value)


def make_table(ids, probs, tokens, experts):
    count, features = tokens.shape[1:]
    height = -(-(experts + 1) // 8) * 8
    ids, probs = jnp.transpose(ids, (2, 0, 1)), jnp.transpose(probs, (2, 0, 1))
    return pl.pallas_call(
        functools.partial(table_kernel, experts),
        out_shape=(
            pltpu.VMEM((height, count), jnp.float32),
            pltpu.VMEM((count, features), tokens.dtype),
        ),
        in_specs=[HBM] * 3,
        out_specs=(VMEM, VMEM),
        scratch_shapes=[
            pltpu.VMEM(ids.shape, ids.dtype),
            pltpu.VMEM(probs.shape, probs.dtype),
            pltpu.SemaphoreType.DMA((3,)),
        ],
        compiler_params=SMALL,
        name="make_table",
    )(in_hbm(ids), in_hbm(probs), in_hbm(tokens))


def plan(tables, capacity, hots, coefs):
    local, slots, width = hots.shape
    blocks = len(tables)
    count = width // blocks
    experts = local * lax.axis_size("expert")
    first = lax.axis_index("expert") * local
    before = lax.broadcasted_iota(jnp.int32, (count, count), 0)
    after = lax.broadcasted_iota(jnp.int32, (count, count), 1)
    upto = jnp.where(before <= after, 1.0, 0.0).astype(jnp.bfloat16)
    slot_ids = lax.broadcasted_iota(jnp.int32, (slots, width), 0).astype(jnp.float32)
    weights, scales, places = [], [], []
    for b in range(blocks):
        weight = tables[b][pl.ds(first, local), :]
        ones = jnp.where(weight > 0.0, 1.0, 0.0)
        padded = jnp.concatenate([ones, jnp.zeros((-local % 16, count), jnp.float32)], axis=0)
        rank = jnp.dot(padded.astype(jnp.bfloat16), upto, preferred_element_type=jnp.float32)[:local]
        places.append(jnp.where(weight > 0.0, rank + float(b * capacity - 1), -1.0))
        weights.append(weight)
        scales.append(tables[b][pl.ds(experts, 1), :])
    weight = jnp.concatenate(weights, axis=1) if blocks > 1 else weights[0]
    scale = jnp.concatenate(scales, axis=1) if blocks > 1 else scales[0]
    place = jnp.concatenate(places, axis=1) if blocks > 1 else places[0]
    for j in range(local):
        hit = slot_ids == place[j : j + 1, :]
        hots[j] = jnp.where(hit, 1.0, 0.0).astype(jnp.bfloat16)
        coefs[j, :, 0:1] = jnp.sum(jnp.where(hit, scale, 0.0), axis=1, keepdims=True)
        coefs[j, :, 1:2] = jnp.sum(jnp.where(hit, weight[j : j + 1, :], 0.0), axis=1, keepdims=True)


def pack(hots, tokens, rows):
    for j in range(hots.shape[0]):
        rows[j] = jnp.dot(hots[j], tokens, preferred_element_type=jnp.float32).astype(jnp.bfloat16)


def expert_hidden(j, rows, hots, coefs, gates, ups, out_ref, base):
    units = gates.shape[2]
    size = hots.shape[2]
    gate = jnp.dot(rows[j], gates[j], preferred_element_type=jnp.float32)
    up = jnp.dot(rows[j], ups[j], preferred_element_type=jnp.float32)
    scale = coefs[j, :, 0:1]
    weight = coefs[j, :, 1:2]
    g = gate * scale
    h = (g / (1.0 + jnp.exp(-g))) * (up * (scale * weight))
    placed = lax.dot_general(
        hots[j], h.astype(jnp.bfloat16), (((0,), (0,)), ((), ())), preferred_element_type=jnp.float32
    )
    out_ref[pl.ds(base, size), pl.ds(j * units, units)] = placed.astype(jnp.bfloat16)


def near_kernel(capacity, *refs):
    tables, tokens = refs[:2], refs[2:4]
    gate_hbm, up_hbm, hidden, gates, ups = refs[4:9]
    hots, coefs, rows, gate_sem, up_sem = refs[9:]
    local = gates.shape[0]
    copies = []
    for j in range(local):
        copies.append(pltpu.make_async_copy(gate_hbm.at[j], gates.at[j], gate_sem.at[j]))
        copies.append(pltpu.make_async_copy(up_hbm.at[j], ups.at[j], up_sem.at[j]))
    for copy in copies:
        copy.start()
    plan(tables, capacity, hots, coefs)
    pack(hots, jnp.concatenate([t[...] for t in tokens], axis=0), rows)
    for j in range(local):
        copies[2 * j].wait()
        copies[2 * j + 1].wait()
        expert_hidden(j, rows, hots, coefs, gates, ups, hidden, 0)


def near_hidden(tables, tokens, w_gate, w_up, capacity, blocks):
    count, features = tokens[0].shape
    local, _, units = w_gate.shape
    slots = slots_of(capacity, 2)
    return pl.pallas_call(
        functools.partial(near_kernel, capacity),
        out_shape=(
            pltpu.VMEM((blocks * count, local * units), jnp.bfloat16),
            pltpu.VMEM(w_gate.shape, w_gate.dtype),
            pltpu.VMEM(w_up.shape, w_up.dtype),
        ),
        in_specs=[VMEM] * 4 + [HBM] * 2,
        out_specs=(VMEM,) * 3,
        scratch_shapes=[
            pltpu.VMEM((local, slots, 2 * count), jnp.bfloat16),
            pltpu.VMEM((local, slots, 128), jnp.float32),
            pltpu.VMEM((local, slots, features), jnp.bfloat16),
            pltpu.SemaphoreType.DMA((local,)),
            pltpu.SemaphoreType.DMA((local,)),
        ],
        compiler_params=GRANT,
        cost_estimate=pl.CostEstimate(
            flops=4 * local * slots * features * units,
            bytes_accessed=4 * local * features * units,
            transcendentals=local * slots * units,
        ),
        name="near_hidden",
    )(*tables, *tokens, in_hbm(w_gate), in_hbm(w_up))


def far_plan_kernel(capacity, far_count, *refs):
    tables = refs[:far_count]
    step, _, hots, coefs, factor = refs[far_count:]
    factor[...] = jnp.full(factor.shape, step[0])
    for p in range(far_count // 2):
        plan(tables[2 * p : 2 * p + 2], capacity, hots.at[p], coefs.at[p])


def far_plan(tables, step_size, order, capacity, local):
    pairs = len(tables) // 2
    count = tables[0].shape[1]
    slots = slots_of(capacity, 2)
    return pl.pallas_call(
        functools.partial(far_plan_kernel, capacity, len(tables)),
        out_shape=(
            pltpu.VMEM((pairs, local, slots, 2 * count), jnp.bfloat16),
            pltpu.VMEM((pairs, local, slots, 128), jnp.float32),
            pltpu.VMEM((8, 128), jnp.float32),
        ),
        in_specs=[VMEM] * len(tables) + [pl.BlockSpec(memory_space=pltpu.SMEM), ANY],
        out_specs=(VMEM,) * 3,
        compiler_params=SMALL,
        cost_estimate=BRIEF,
        name="far_plan",
    )(*tables, step_size, order)


def far_kernel(far_count, *refs):
    tokens = refs[:far_count]
    hots, coefs, gates, ups, down_hbm, start_hbm, _, hidden, downs, start, rows, sems = refs[far_count:]
    copies = [
        pltpu.make_async_copy(down_hbm, downs, sems.at[0]),
        pltpu.make_async_copy(start_hbm, start, sems.at[1]),
    ]
    for copy in copies:
        copy.start()
    for p in range(far_count // 2):
        both = jnp.concatenate([tokens[2 * p][...], tokens[2 * p + 1][...]], axis=0)
        pack(hots.at[p], both, rows)
        for j in range(gates.shape[0]):
            expert_hidden(j, rows, hots.at[p], coefs.at[p], gates, ups, hidden, (p + 1) * hots.shape[3])
    for copy in copies:
        copy.wait()


def far_hidden(tokens, hots, coefs, gates, ups, w_down, start_state, hidden):
    pairs, local, slots, size = hots.shape
    features, units = gates.shape[1:]
    return pl.pallas_call(
        functools.partial(far_kernel, len(tokens)),
        out_shape=(
            pltpu.VMEM(hidden.shape, hidden.dtype),
            pltpu.VMEM(w_down.shape, w_down.dtype),
            pltpu.VMEM(start_state.shape, start_state.dtype),
        ),
        in_specs=[VMEM] * (len(tokens) + 4) + [HBM] * 2 + [VMEM],
        out_specs=(VMEM,) * 3,
        scratch_shapes=[
            pltpu.VMEM((local, slots, features), jnp.bfloat16),
            pltpu.SemaphoreType.DMA((2,)),
        ],
        input_output_aliases={len(tokens) + 6: 0},
        compiler_params=GRANT,
        cost_estimate=pl.CostEstimate(
            flops=4 * pairs * local * slots * features * units,
            bytes_accessed=6 * local * features * units,
            transcendentals=pairs * local * slots * units,
        ),
        name="far_hidden",
    )(*tokens, hots, coefs, gates, ups, in_hbm(w_down), in_hbm(start_state), hidden)


def down_kernel(core, start, hidden_ref, down_ref, _, out_ref):
    pairs, count, width = out_ref.shape
    local, units, _ = down_ref.shape
    columns = pl.ds(start, width)
    total = None
    for j in range(local):
        inner = pl.ds(j * units, units)
        parts = [hidden_ref[pl.ds((2 * p + core) * count, count), inner] for p in range(pairs)]
        term = jnp.dot(
            jnp.concatenate(parts, axis=0), down_ref[j, :, columns], preferred_element_type=jnp.float32
        )
        total = term if total is None else total + term
    for p in range(pairs):
        out_ref[p] = total[p * count : (p + 1) * count].astype(out_ref.dtype)


def down_rows(hidden, downs, order, send, count, start, width):
    pairs = hidden.shape[0] // (2 * count)
    return pl.pallas_call(
        functools.partial(down_kernel, int(send), start),
        out_shape=pltpu.VMEM((pairs, count, width), jnp.bfloat16 if send else jnp.float32),
        in_specs=[VMEM, VMEM, ANY],
        out_specs=VMEM,
        compiler_params=GRANT,
        cost_estimate=BRIEF,
        name="down_rows",
    )(hidden, downs, order)


def core_sum_kernel(widths, keep, got, factor, _, *outs):
    step = factor[0:1, 0:1]
    first = 0
    for n, width in enumerate(widths):
        columns = pl.ds(first, width)
        first += width
        for p in range(keep.shape[0]):
            total = step * (keep[p, :, columns] + got[p, :, columns].astype(jnp.float32))
            if p == 0:
                outs[2 * n][...] = total
            else:
                outs[2 * n + 1][p - 1] = total.astype(jnp.bfloat16)


def core_sum(keep, got, factor, order, widths):
    pairs, count, _ = keep.shape
    shapes = []
    for width in widths:
        shapes.append(pltpu.VMEM((count, width), jnp.float32))
        shapes.append(pltpu.VMEM((pairs - 1, count, width), jnp.bfloat16))
    return pl.pallas_call(
        functools.partial(core_sum_kernel, widths),
        out_shape=tuple(shapes),
        in_specs=[VMEM, VMEM, VMEM, ANY],
        out_specs=(VMEM,) * len(shapes),
        compiler_params=SMALL,
        cost_estimate=BRIEF,
        name="core_sum",
    )(keep, got, factor, order)


def chain_kernel(hop, backs, first, send, start, _, own, *refs):
    outs = refs[len(refs) - 1 - send :]
    result, width = outs[-1], own.shape[1]

    @pl.when(lax.axis_index("tm") == hop)
    def _():
        total = own[...]
        for ref in refs[: backs + (hop > 0)]:
            total = total + ref[...].astype(jnp.float32)
        if send:
            outs[0][...] = total.astype(jnp.bfloat16)
        columns = pl.ds(first, width)
        result[:, columns] = start[:, columns] + total


def chain_step(hop, own, backs, got, first, send, start, result, order):
    inputs = [start, order, own, *backs] + ([] if got is None else [got]) + ([] if result is None else [result])
    return pl.pallas_call(
        functools.partial(chain_kernel, hop, len(backs), first, int(send)),
        out_shape=((pltpu.VMEM(own.shape, jnp.bfloat16),) if send else ())
        + (pltpu.VMEM(start.shape, jnp.float32),),
        in_specs=[VMEM, ANY] + [VMEM] * (len(inputs) - 2),
        out_specs=(VMEM,) * (1 + send),
        input_output_aliases={} if result is None else {len(inputs) - 1: int(send)},
        compiler_params=SMALL,
        cost_estimate=BRIEF,
        name="chain_step",
    )(*inputs)


def write_kernel(first, result, _, out, mark, sems):
    mark[...] = jnp.zeros_like(mark)
    last = lax.axis_index("tm") == lax.axis_size("tm") - 1
    head, tail = pl.ds(0, first), pl.ds(first, result.shape[1] - first)
    copies = [pltpu.make_async_copy(result.at[:, part], out.at[:, part], sems.at[i]) for i, part in enumerate((head, tail))]
    copies[0].start()

    @pl.when(jnp.logical_not(last))
    def _():
        copies[1].start()
        copies[1].wait()

    copies[0].wait()


def write_most(result, first, order):
    return pl.pallas_call(
        functools.partial(write_kernel, first),
        out_shape=(pltpu.HBM(result.shape, result.dtype), pltpu.VMEM((8, 128), jnp.float32)),
        in_specs=[VMEM, ANY],
        out_specs=(HBM, VMEM),
        scratch_shapes=[pltpu.SemaphoreType.DMA((2,))],
        compiler_params=SMALL,
        cost_estimate=BRIEF,
        name="write_most",
    )(result, order)


def last_kernel(first, backs, start, _, own, *refs):
    out, block, sem = refs[-3:]

    @pl.when(lax.axis_index("tm") == lax.axis_size("tm") - 1)
    def _():
        columns = pl.ds(first, own.shape[1])
        total = start[:, columns] + own[...]
        for ref in refs[: backs + 1]:
            total = total + ref[...].astype(jnp.float32)
        block[...] = total
        copy = pltpu.make_async_copy(block, out.at[:, columns], sem)
        copy.start()
        copy.wait()


def last_step(own, backs, got, first, start, out, order):
    inputs = [start, order, own, *backs, got, out]
    return pl.pallas_call(
        functools.partial(last_kernel, first, len(backs)),
        out_shape=pltpu.HBM(out.shape, out.dtype),
        in_specs=[VMEM, ANY] + [VMEM] * (len(inputs) - 3) + [HBM],
        out_specs=HBM,
        scratch_shapes=[pltpu.VMEM(own.shape, jnp.float32), pltpu.SemaphoreType.DMA],
        input_output_aliases={len(inputs) - 1: 0},
        compiler_params=SMALL,
        cost_estimate=BRIEF,
        name="last_step",
    )(*inputs)


def tie_kernel(value_ref, order_ref, out_ref):
    pass


def tie(value, order):
    return pl.pallas_call(
        tie_kernel,
        out_shape=jax.ShapeDtypeStruct(value.shape, value.dtype),
        in_specs=[ANY, ANY],
        out_specs=ANY,
        input_output_aliases={0: 0},
        compiler_params=SMALL,
        cost_estimate=BRIEF,
        name="tie",
    )(value, order)


def exchange(value, low, members, steps):
    pairs = []
    for e in range(members):
        for z in range(steps):
            if z in (low, low + 1):
                pairs.append((e * steps + z, e * steps + 2 * low + 1 - z))
            else:
                pairs.append((e * steps + z, (e ^ 1) * steps + z))
    return lax.ppermute(value, ("expert", "tm"), pairs)


def shards(tokens, route_ids, route_probs, step_size, start_state, w_gate, w_up, w_down):
    members = lax.axis_size("expert")
    steps = lax.axis_size("tm")
    tok_count, feature_count = tokens.shape[1:]
    topk_count = route_ids.shape[2]
    expert_total = w_gate.shape[0] * members
    capacity = 3 * tok_count * topk_count // (2 * expert_total)
    chips = members // 2

    def swapped(value):
        return lax.ppermute(value, "expert", [(i, i ^ 1) for i in range(members)])

    def shifted(value, by):
        return lax.ppermute(value, "expert", [(i, (i + 2 * by) % members) for i in range(members)])

    own = tokens[0]
    far_same = [shifted(own, by) for by in range(1, chips)]
    partner = swapped(own)
    table, own = make_table(route_ids, route_probs, tokens, expert_total)
    far_table = [shifted(table, by) for by in range(1, chips)]
    hidden, gates, ups = near_hidden([table, swapped(table)], [own, partner], w_gate, w_up, capacity, members)
    far_tables, far_tokens = [], []
    for value, piece in zip(far_table, far_same):
        value = tie(value, hidden)
        piece = tie(piece, value)
        far_tables += [value, swapped(value)]
        far_tokens += [piece, swapped(piece)]
    hots, coefs, factor = far_plan(far_tables, step_size, hidden, capacity, w_gate.shape[0])
    hidden, downs, start = far_hidden(far_tokens, hots, coefs, gates, ups, w_down, start_state, hidden)

    widths = [feature_count * share // 16 for share in SHARES]
    parts = len(widths)
    firsts = [sum(widths[:c]) for c in range(parts)]
    events = []
    for g, times in enumerate(DOWN_TIMES):
        for kind, ready in zip(("send", "keep", "core"), times):
            events.append((ready, kind, g, 0))
    for c, times in enumerate(CHAIN_TIMES):
        for hop in range(steps):
            events.append((times[0] + (times[1] + times[2] * (hop - 1) if hop else 0.0), "chain", c, hop))
    order, result = hidden, None
    gots, keeps, owns, backs, arrived = {}, {}, {}, {}, {}
    for _, kind, c, hop in sorted(events):
        if kind in ("send", "keep"):
            group = GROUPS[c]
            width = sum(widths[i] for i in group)
            part = down_rows(hidden, downs, order, kind == "send", tok_count, firsts[group[0]], width)
            if kind == "send":
                gots[c] = swapped(part)
            else:
                keeps[c] = part
            order = part
        elif kind == "core":
            group = GROUPS[c]
            sums = core_sum(keeps[c], gots[c], factor, order, [widths[i] for i in group])
            for n, i in enumerate(group):
                owns[i] = sums[2 * n]
                backs[i] = [shifted(sums[2 * n + 1][by - 1], -by) for by in range(1, chips)]
            order = sums[0]
        else:
            if c == parts - 1 and hop == steps - 1:
                out, order = write_most(result, firsts[c], order)
                out = last_step(owns[c], backs[c], arrived[c], firsts[c], start, out, order)
                continue
            send = hop < steps - 1
            *sent, result = chain_step(
                hop, owns[c], backs[c], arrived.get(c), firsts[c], send, start, result, order
            )
            if send:
                order = sent[0]
                arrived[c] = exchange(sent[0], hop, members, steps)
    return out[None]


def solution(mesh):
    return jax.shard_map(
        shards,
        mesh=mesh,
        in_specs=(
            P("tm", ("copies", "expert"), None),
            P("tm", ("copies", "expert"), None),
            P("tm", ("copies", "expert"), None),
            P(("copies", "tm")),
            P(("copies", "expert"), None),
            P("expert", None, None),
            P("expert", None, None),
            P("expert", None, None),
        ),
        out_specs=P("tm", ("copies", "expert"), None),
        check_vma=False,
    )
```

```python
import functools

import jax
import jax.numpy as jnp
from jax import lax
from jax.experimental import pallas as pl
from jax.experimental.pallas import tpu as pltpu
from jax.sharding import PartitionSpec as P

ANY = pl.BlockSpec(memory_space=pl.ANY)
HBM = pl.BlockSpec(memory_space=pltpu.HBM)
VMEM = pl.BlockSpec(memory_space=pltpu.VMEM)
GRANT = pltpu.CompilerParams(vmem_limit_bytes=7 * 1024 * 1024)
BRIEF = pl.CostEstimate(flops=0, bytes_accessed=0, transcendentals=0)
SMALL = pltpu.CompilerParams(vmem_limit_bytes=2 * 1024 * 1024)


def in_hbm(value):
    return pltpu.with_memory_space_constraint(value, pltpu.HBM)


def slots_of(capacity, blocks):
    return -(-capacity * blocks // 16) * 16


def table_kernel(experts, ids_hbm, probs_hbm, tokens_hbm, table, tokens, ids, probs, sems):
    copy = pltpu.make_async_copy(tokens_hbm.at[0], tokens, sems.at[0])
    smalls = [
        pltpu.make_async_copy(ids_hbm, ids, sems.at[1]),
        pltpu.make_async_copy(probs_hbm, probs, sems.at[2]),
    ]
    copy.start()
    for small in smalls:
        small.start()
    for small in smalls:
        small.wait()
    choices, _, count = ids.shape
    total = probs[0]
    for k in range(1, choices):
        total = total + probs[k]
    names = lax.broadcasted_iota(jnp.int32, table.shape, 0)
    value = jnp.zeros(table.shape, jnp.float32)
    for k in range(choices):
        value = value + jnp.where(ids[k] == names, probs[k] / total, 0.0)
    copy.wait()
    rows = tokens[...].astype(jnp.float32)
    scale = lax.rsqrt(jnp.mean(rows * rows, axis=1, keepdims=True) + 1e-06)
    scale = jnp.broadcast_to(scale, (count, 128)).T[:1]
    table[...] = jnp.where(names == experts, scale, value)


def make_table(ids, probs, tokens, experts):
    count, features = tokens.shape[1:]
    height = -(-(experts + 1) // 8) * 8
    ids, probs = jnp.transpose(ids, (2, 0, 1)), jnp.transpose(probs, (2, 0, 1))
    return pl.pallas_call(
        functools.partial(table_kernel, experts),
        out_shape=(
            pltpu.VMEM((height, count), jnp.float32),
            pltpu.VMEM((count, features), tokens.dtype),
        ),
        in_specs=[HBM] * 3,
        out_specs=(VMEM, VMEM),
        scratch_shapes=[
            pltpu.VMEM(ids.shape, ids.dtype),
            pltpu.VMEM(probs.shape, probs.dtype),
            pltpu.SemaphoreType.DMA((3,)),
        ],
        compiler_params=SMALL,
        name="make_table",
    )(in_hbm(ids), in_hbm(probs), in_hbm(tokens))


def plan(tables, capacity, hots, coefs):
    local, slots, width = hots.shape
    blocks = len(tables)
    count = width // blocks
    experts = local * lax.axis_size("expert")
    first = lax.axis_index("expert") * local
    before = lax.broadcasted_iota(jnp.int32, (count, count), 0)
    after = lax.broadcasted_iota(jnp.int32, (count, count), 1)
    upto = jnp.where(before <= after, 1.0, 0.0).astype(jnp.bfloat16)
    slot_ids = lax.broadcasted_iota(jnp.int32, (slots, width), 0).astype(jnp.float32)
    weights, scales, places = [], [], []
    for b in range(blocks):
        weight = tables[b][pl.ds(first, local), :]
        ones = jnp.where(weight > 0.0, 1.0, 0.0)
        padded = jnp.concatenate([ones, jnp.zeros((-local % 16, count), jnp.float32)], axis=0)
        rank = jnp.dot(padded.astype(jnp.bfloat16), upto, preferred_element_type=jnp.float32)[:local]
        places.append(jnp.where(weight > 0.0, rank + float(b * capacity - 1), -1.0))
        weights.append(weight)
        scales.append(tables[b][pl.ds(experts, 1), :])
    weight = jnp.concatenate(weights, axis=1) if blocks > 1 else weights[0]
    scale = jnp.concatenate(scales, axis=1) if blocks > 1 else scales[0]
    place = jnp.concatenate(places, axis=1) if blocks > 1 else places[0]
    for j in range(local):
        hit = slot_ids == place[j : j + 1, :]
        hots[j] = jnp.where(hit, 1.0, 0.0).astype(jnp.bfloat16)
        coefs[j, :, 0:1] = jnp.sum(jnp.where(hit, scale, 0.0), axis=1, keepdims=True)
        coefs[j, :, 1:2] = jnp.sum(jnp.where(hit, weight[j : j + 1, :], 0.0), axis=1, keepdims=True)


def pack(hots, tokens, rows):
    for j in range(hots.shape[0]):
        rows[j] = jnp.dot(hots[j], tokens, preferred_element_type=jnp.float32).astype(jnp.bfloat16)


def expert_hidden(j, rows, hots, coefs, gates, ups, out_ref, base):
    units = gates.shape[2]
    size = hots.shape[2]
    gate = jnp.dot(rows[j], gates[j], preferred_element_type=jnp.float32)
    up = jnp.dot(rows[j], ups[j], preferred_element_type=jnp.float32)
    scale = coefs[j, :, 0:1]
    weight = coefs[j, :, 1:2]
    g = gate * scale
    h = (g / (1.0 + jnp.exp(-g))) * (up * (scale * weight))
    placed = lax.dot_general(
        hots[j], h.astype(jnp.bfloat16), (((0,), (0,)), ((), ())), preferred_element_type=jnp.float32
    )
    out_ref[pl.ds(base, size), pl.ds(j * units, units)] = placed.astype(jnp.bfloat16)


def near_kernel(capacity, *refs):
    tables, tokens = refs[:2], refs[2:4]
    gate_hbm, up_hbm, hidden, gates, ups = refs[4:9]
    hots, coefs, rows, gate_sem, up_sem = refs[9:]
    local = gates.shape[0]
    copies = []
    for j in range(local):
        copies.append(pltpu.make_async_copy(gate_hbm.at[j], gates.at[j], gate_sem.at[j]))
        copies.append(pltpu.make_async_copy(up_hbm.at[j], ups.at[j], up_sem.at[j]))
    for copy in copies:
        copy.start()
    plan(tables, capacity, hots, coefs)
    pack(hots, jnp.concatenate([t[...] for t in tokens], axis=0), rows)
    for j in range(local):
        copies[2 * j].wait()
        copies[2 * j + 1].wait()
        expert_hidden(j, rows, hots, coefs, gates, ups, hidden, 0)


def near_hidden(tables, tokens, w_gate, w_up, capacity, blocks):
    count, features = tokens[0].shape
    local, _, units = w_gate.shape
    slots = slots_of(capacity, 2)
    return pl.pallas_call(
        functools.partial(near_kernel, capacity),
        out_shape=(
            pltpu.VMEM((blocks * count, local * units), jnp.bfloat16),
            pltpu.VMEM(w_gate.shape, w_gate.dtype),
            pltpu.VMEM(w_up.shape, w_up.dtype),
        ),
        in_specs=[VMEM] * 4 + [HBM] * 2,
        out_specs=(VMEM,) * 3,
        scratch_shapes=[
            pltpu.VMEM((local, slots, 2 * count), jnp.bfloat16),
            pltpu.VMEM((local, slots, 128), jnp.float32),
            pltpu.VMEM((local, slots, features), jnp.bfloat16),
            pltpu.SemaphoreType.DMA((local,)),
            pltpu.SemaphoreType.DMA((local,)),
        ],
        compiler_params=GRANT,
        cost_estimate=pl.CostEstimate(
            flops=4 * local * slots * features * units,
            bytes_accessed=4 * local * features * units,
            transcendentals=local * slots * units,
        ),
        name="near_hidden",
    )(*tables, *tokens, in_hbm(w_gate), in_hbm(w_up))


def far_plan_kernel(capacity, far_count, *refs):
    tables = refs[:far_count]
    step, _, hots, coefs, factor = refs[far_count:]
    factor[...] = jnp.full(factor.shape, step[0])
    for p in range(far_count // 2):
        plan(tables[2 * p : 2 * p + 2], capacity, hots.at[p], coefs.at[p])


def far_plan(tables, step_size, order, capacity, local):
    pairs = len(tables) // 2
    count = tables[0].shape[1]
    slots = slots_of(capacity, 2)
    return pl.pallas_call(
        functools.partial(far_plan_kernel, capacity, len(tables)),
        out_shape=(
            pltpu.VMEM((pairs, local, slots, 2 * count), jnp.bfloat16),
            pltpu.VMEM((pairs, local, slots, 128), jnp.float32),
            pltpu.VMEM((8, 128), jnp.float32),
        ),
        in_specs=[VMEM] * len(tables) + [pl.BlockSpec(memory_space=pltpu.SMEM), ANY],
        out_specs=(VMEM,) * 3,
        compiler_params=SMALL,
        cost_estimate=BRIEF,
        name="far_plan",
    )(*tables, step_size, order)


def far_kernel(far_count, *refs):
    tokens = refs[:far_count]
    hots, coefs, gates, ups, down_hbm, start_hbm, _, hidden, downs, start, rows, sems = refs[far_count:]
    copies = [
        pltpu.make_async_copy(down_hbm, downs, sems.at[0]),
        pltpu.make_async_copy(start_hbm, start, sems.at[1]),
    ]
    for copy in copies:
        copy.start()
    for p in range(far_count // 2):
        both = jnp.concatenate([tokens[2 * p][...], tokens[2 * p + 1][...]], axis=0)
        pack(hots.at[p], both, rows)
        for j in range(gates.shape[0]):
            expert_hidden(j, rows, hots.at[p], coefs.at[p], gates, ups, hidden, (p + 1) * hots.shape[3])
    for copy in copies:
        copy.wait()


def far_hidden(tokens, hots, coefs, gates, ups, w_down, start_state, hidden):
    pairs, local, slots, size = hots.shape
    features, units = gates.shape[1:]
    return pl.pallas_call(
        functools.partial(far_kernel, len(tokens)),
        out_shape=(
            pltpu.VMEM(hidden.shape, hidden.dtype),
            pltpu.VMEM(w_down.shape, w_down.dtype),
            pltpu.VMEM(start_state.shape, start_state.dtype),
        ),
        in_specs=[VMEM] * (len(tokens) + 4) + [HBM] * 2 + [VMEM],
        out_specs=(VMEM,) * 3,
        scratch_shapes=[
            pltpu.VMEM((local, slots, features), jnp.bfloat16),
            pltpu.SemaphoreType.DMA((2,)),
        ],
        input_output_aliases={len(tokens) + 6: 0},
        compiler_params=GRANT,
        cost_estimate=pl.CostEstimate(
            flops=4 * pairs * local * slots * features * units,
            bytes_accessed=6 * local * features * units,
            transcendentals=pairs * local * slots * units,
        ),
        name="far_hidden",
    )(*tokens, hots, coefs, gates, ups, in_hbm(w_down), in_hbm(start_state), hidden)


def down_kernel(core, start, hidden_ref, down_ref, _, out_ref):
    pairs, count, width = out_ref.shape
    local, units, _ = down_ref.shape
    columns = pl.ds(start, width)
    total = None
    for j in range(local):
        inner = pl.ds(j * units, units)
        parts = [hidden_ref[pl.ds((2 * p + core) * count, count), inner] for p in range(pairs)]
        term = jnp.dot(
            jnp.concatenate(parts, axis=0), down_ref[j, :, columns], preferred_element_type=jnp.float32
        )
        total = term if total is None else total + term
    for p in range(pairs):
        out_ref[p] = total[p * count : (p + 1) * count].astype(out_ref.dtype)


def down_rows(hidden, downs, order, send, count, start, width):
    pairs = hidden.shape[0] // (2 * count)
    return pl.pallas_call(
        functools.partial(down_kernel, int(send), start),
        out_shape=pltpu.VMEM((pairs, count, width), jnp.bfloat16 if send else jnp.float32),
        in_specs=[VMEM, VMEM, ANY],
        out_specs=VMEM,
        compiler_params=GRANT,
        cost_estimate=BRIEF,
        name="down_rows",
    )(hidden, downs, order)


def core_sum_kernel(chunks, keep, got, factor, _, *outs):
    pairs, _, width = keep.shape
    width = width // chunks
    step = factor[0:1, 0:1]
    for i in range(chunks):
        columns = pl.ds(i * width, width)
        for p in range(pairs):
            total = step * (keep[p, :, columns] + got[p, :, columns].astype(jnp.float32))
            if p == 0:
                outs[2 * i][...] = total
            else:
                outs[2 * i + 1][p - 1] = total.astype(jnp.bfloat16)


def core_sum(keep, got, factor, order, chunks):
    pairs, count, width = keep.shape
    shapes = []
    for _ in range(chunks):
        shapes.append(pltpu.VMEM((count, width // chunks), jnp.float32))
        shapes.append(pltpu.VMEM((pairs - 1, count, width // chunks), jnp.bfloat16))
    return pl.pallas_call(
        functools.partial(core_sum_kernel, chunks),
        out_shape=tuple(shapes),
        in_specs=[VMEM, VMEM, VMEM, ANY],
        out_specs=(VMEM,) * len(shapes),
        compiler_params=SMALL,
        cost_estimate=BRIEF,
        name="core_sum",
    )(keep, got, factor, order)


def chain_kernel(hop, backs, first, send, start, _, own, *refs):
    outs = refs[len(refs) - 1 - send :]
    result, width = outs[-1], own.shape[1]

    @pl.when(lax.axis_index("tm") == hop)
    def _():
        total = own[...]
        for ref in refs[: backs + (hop > 0)]:
            total = total + ref[...].astype(jnp.float32)
        if send:
            outs[0][...] = total.astype(jnp.bfloat16)
        columns = pl.ds(first, width)
        result[:, columns] = start[:, columns] + total


def chain_step(hop, own, backs, got, first, send, start, result, order):
    inputs = [start, order, own, *backs] + ([] if got is None else [got]) + ([] if result is None else [result])
    return pl.pallas_call(
        functools.partial(chain_kernel, hop, len(backs), first, int(send)),
        out_shape=((pltpu.VMEM(own.shape, jnp.bfloat16),) if send else ())
        + (pltpu.VMEM(start.shape, jnp.float32),),
        in_specs=[VMEM, ANY] + [VMEM] * (len(inputs) - 2),
        out_specs=(VMEM,) * (1 + send),
        input_output_aliases={} if result is None else {len(inputs) - 1: int(send)},
        compiler_params=SMALL,
        cost_estimate=BRIEF,
        name="chain_step",
    )(*inputs)


def write_kernel(first, result, _, out, mark, sems):
    mark[...] = jnp.zeros_like(mark)
    last = lax.axis_index("tm") == lax.axis_size("tm") - 1
    head, tail = pl.ds(0, first), pl.ds(first, result.shape[1] - first)
    copies = [pltpu.make_async_copy(result.at[:, part], out.at[:, part], sems.at[i]) for i, part in enumerate((head, tail))]
    copies[0].start()

    @pl.when(jnp.logical_not(last))
    def _():
        copies[1].start()
        copies[1].wait()

    copies[0].wait()


def write_most(result, first, order):
    return pl.pallas_call(
        functools.partial(write_kernel, first),
        out_shape=(pltpu.HBM(result.shape, result.dtype), pltpu.VMEM((8, 128), jnp.float32)),
        in_specs=[VMEM, ANY],
        out_specs=(HBM, VMEM),
        scratch_shapes=[pltpu.SemaphoreType.DMA((2,))],
        compiler_params=SMALL,
        cost_estimate=BRIEF,
        name="write_most",
    )(result, order)


def last_kernel(first, backs, start, _, own, *refs):
    out, block, sem = refs[-3:]

    @pl.when(lax.axis_index("tm") == lax.axis_size("tm") - 1)
    def _():
        columns = pl.ds(first, own.shape[1])
        total = start[:, columns] + own[...]
        for ref in refs[: backs + 1]:
            total = total + ref[...].astype(jnp.float32)
        block[...] = total
        copy = pltpu.make_async_copy(block, out.at[:, columns], sem)
        copy.start()
        copy.wait()


def last_step(own, backs, got, first, start, out, order):
    inputs = [start, order, own, *backs, got, out]
    return pl.pallas_call(
        functools.partial(last_kernel, first, len(backs)),
        out_shape=pltpu.HBM(out.shape, out.dtype),
        in_specs=[VMEM, ANY] + [VMEM] * (len(inputs) - 3) + [HBM],
        out_specs=HBM,
        scratch_shapes=[pltpu.VMEM(own.shape, jnp.float32), pltpu.SemaphoreType.DMA],
        input_output_aliases={len(inputs) - 1: 0},
        compiler_params=SMALL,
        cost_estimate=BRIEF,
        name="last_step",
    )(*inputs)


def tie_kernel(value_ref, order_ref, out_ref):
    pass


def tie(value, order):
    return pl.pallas_call(
        tie_kernel,
        out_shape=jax.ShapeDtypeStruct(value.shape, value.dtype),
        in_specs=[ANY, ANY],
        out_specs=ANY,
        input_output_aliases={0: 0},
        compiler_params=SMALL,
        cost_estimate=BRIEF,
        name="tie",
    )(value, order)


def exchange(value, low, members, steps):
    pairs = []
    for e in range(members):
        for z in range(steps):
            if z in (low, low + 1):
                pairs.append((e * steps + z, e * steps + 2 * low + 1 - z))
            else:
                pairs.append((e * steps + z, (e ^ 1) * steps + z))
    return lax.ppermute(value, ("expert", "tm"), pairs)


def shards(tokens, route_ids, route_probs, step_size, start_state, w_gate, w_up, w_down):
    members = lax.axis_size("expert")
    steps = lax.axis_size("tm")
    tok_count, feature_count = tokens.shape[1:]
    topk_count = route_ids.shape[2]
    expert_total = w_gate.shape[0] * members
    capacity = 3 * tok_count * topk_count // (2 * expert_total)
    chips = members // 2

    def swapped(value):
        return lax.ppermute(value, "expert", [(i, i ^ 1) for i in range(members)])

    def shifted(value, by):
        return lax.ppermute(value, "expert", [(i, (i + 2 * by) % members) for i in range(members)])

    own = tokens[0]
    far_same = [shifted(own, by) for by in range(1, chips)]
    partner = swapped(own)
    table, own = make_table(route_ids, route_probs, tokens, expert_total)
    far_table = [shifted(table, by) for by in range(1, chips)]
    hidden, gates, ups = near_hidden([table, swapped(table)], [own, partner], w_gate, w_up, capacity, members)
    far_tables, far_tokens = [], []
    for value, piece in zip(far_table, far_same):
        value = tie(value, hidden)
        piece = tie(piece, value)
        far_tables += [value, swapped(value)]
        far_tokens += [piece, swapped(piece)]
    hots, coefs, factor = far_plan(far_tables, step_size, hidden, capacity, w_gate.shape[0])
    hidden, downs, start = far_hidden(far_tokens, hots, coefs, gates, ups, w_down, start_state, hidden)

    parts = 4
    width = feature_count // parts
    groups = [(0, 1), (1, parts - 1)]
    events, ready = [], 0.0
    for g, (_, count) in enumerate(groups):
        events.append((ready, "send", g, 0))
        events.append((ready + 0.9 * count, "keep", g, 0))
        ready += max(2.5, 1.8 * count)
        events.append((ready, "core", g, 0))
    for c in range(parts):
        for hop in range(steps):
            late = 1.7 if c == 0 and hop == steps - 1 else 0.0
            events.append((12.0 + 3.3 * c + 5.0 * hop + late, "chain", c, hop))
    order, result = hidden, None
    gots, keeps, owns, backs, arrived = {}, {}, {}, {}, {}
    for _, kind, c, hop in sorted(events):
        if kind in ("send", "keep"):
            first, count = groups[c]
            part = down_rows(hidden, downs, order, kind == "send", tok_count, first * width, count * width)
            if kind == "send":
                gots[c] = swapped(part)
            else:
                keeps[c] = part
            order = part
        elif kind == "core":
            first, count = groups[c]
            sums = core_sum(keeps[c], gots[c], factor, order, count)
            for i in range(count):
                owns[first + i] = sums[2 * i]
                backs[first + i] = [shifted(sums[2 * i + 1][by - 1], -by) for by in range(1, chips)]
            order = sums[0]
        else:
            if c == parts - 1 and hop == steps - 1:
                out, order = write_most(result, c * width, order)
                out = last_step(owns[c], backs[c], arrived[c], c * width, start, out, order)
                continue
            send = hop < steps - 1
            *sent, result = chain_step(
                hop, owns[c], backs[c], arrived.get(c), c * width, send, start, result, order
            )
            if send:
                order = sent[0]
                arrived[c] = exchange(sent[0], hop, members, steps)
    return out[None]


def solution(mesh):
    return jax.shard_map(
        shards,
        mesh=mesh,
        in_specs=(
            P("tm", ("copies", "expert"), None),
            P("tm", ("copies", "expert"), None),
            P("tm", ("copies", "expert"), None),
            P(("copies", "tm")),
            P(("copies", "expert"), None),
            P("expert", None, None),
            P("expert", None, None),
            P("expert", None, None),
        ),
        out_specs=P("tm", ("copies", "expert"), None),
        check_vma=False,
    )
```
